32 devices in a mesh: dp: 4 (over y, core), fsdp: 8 (over z, x).
Axes of the slice: x: 2, y: 2, z: 4, core: 2. Of those that a mesh axis runs over, the one named last changes fastest.
Arguments:
- frames: bfloat16 [81920, 512], P(('dp', 'fsdp')), may hold values from -6 to 6
- memory: bfloat16 [16384, 512], P(('dp', 'fsdp')), may hold values from -6 to 6
- left_keys: bfloat16 [122880, 512], P(('dp', 'fsdp')), may hold values from -6 to 6
- left_values: bfloat16 [122880, 512], P(('dp', 'fsdp')), may hold values from -6 to 6
- lengths: int32 [4096], P(('dp', 'fsdp')), may hold values from 4 to 16
- cotangent: bfloat16 [81920, 512], P(('dp', 'fsdp')), may hold values from -6 to 6
- attn_w: float32 [4, 512, 512], P(None, 'fsdp'), as said below
- ffn_in: float32 [512, 2048], P('fsdp'), may hold values from -0.25 to 0.25
- ffn_out: float32 [2048, 512], P('fsdp'), may hold values from -0.125 to 0.125
- norm_params: float32 [4, 512], P(None, 'fsdp'), as said below
- attn_m: float32 [4, 512, 512], P(None, 'fsdp'), as said below
- attn_v: float32 [4, 512, 512], P(None, 'fsdp'), as said below
- ffn_in_m: float32 [512, 2048], P('fsdp'), as said below
- ffn_in_v: float32 [512, 2048], P('fsdp'), as said below
- ffn_out_m: float32 [2048, 512], P('fsdp'), as said below
- ffn_out_v: float32 [2048, 512], P('fsdp'), as said below
- norm_m: float32 [4, 512], P(None, 'fsdp'), as said below
- norm_v: float32 [4, 512], P(None, 'fsdp'), as said below
Outputs:
- output: bfloat16 [81920, 512], P(('dp', 'fsdp'))
- input_grad: float32 [81920, 512], P(('dp', 'fsdp'))
- attn_grad: float32 [4, 512, 512], P(None, 'fsdp')
- attn_first: float32 [4, 512, 512], P(None, 'fsdp')
- attn_second: float32 [4, 512, 512], P(None, 'fsdp')
- attn_new: float32 [4, 512, 512], P(None, 'fsdp')
- attn_copy: bfloat16 [4, 512, 512], P(None, 'fsdp')
- in_grad: float32 [512, 2048], P('fsdp')
- in_first: float32 [512, 2048], P('fsdp')
- in_second: float32 [512, 2048], P('fsdp')
- in_new: float32 [512, 2048], P('fsdp')
- in_copy: bfloat16 [512, 2048], P('fsdp')
- out_grad: float32 [2048, 512], P('fsdp')
- out_first: float32 [2048, 512], P('fsdp')
- out_second: float32 [2048, 512], P('fsdp')
- out_new: float32 [2048, 512], P('fsdp')
- out_copy: bfloat16 [2048, 512], P('fsdp')
- norm_grad: float32 [4, 512], P(None, 'fsdp')
- norm_first: float32 [4, 512], P(None, 'fsdp')
- norm_second: float32 [4, 512], P(None, 'fsdp')
- norm_new: float32 [4, 512], P(None, 'fsdp')
- norm_copy: bfloat16 [4, 512], P(None, 'fsdp')
The draws below stay inside these ranges and needn't reach their ends.
Inputs may be any that keep to these rules, and one draw needn't show every extreme that they name: attn_w holds four independent 512 x 512 matrices of entries. `norm_params`: gains near 1, shifts near 0. `attn_v`: positive entries. `ffn_in_v`: positive entries. `ffn_out_v`: positive entries. `norm_v`: positive entries. `attn_m`: entries of both signs. `ffn_in_m`: entries of both signs. `ffn_out_m`: entries of both signs. `norm_m`: entries of both signs.
All inputs are finite; a program needn't handle non-finite values.
Results may differ from the reference program's by a relative error of at most 0.024.
Values may be sent and summed in bfloat16 or wider, within the bound.
No kernel may reach another device: no remote copies, remote signals or barrier semaphores. Data moves between devices by JAX's collectives and lax.ppermute only.
A program may use at most 320 MiB of HBM per device.

```python
import math
import jax
import jax.numpy as jnp
from jax import lax

D = 512
HEADS = 8
FF = 2048
SEG = 16
LEFT = 30
MEM = 4
STEP = 5
ROWS_SPAN = 20
KEYS = 54
SPANS = 4096
ROWS = 81920


def typical_size(factor):
    return factor * math.sqrt(ROWS)


def first_moment(key, array_shape, factor):
    return typical_size(factor) * jax.random.normal(key, array_shape, jnp.float32)


def second_moment(key, array_shape, factor):
    spread = jax.random.uniform(key, array_shape, jnp.float32, math.log(0.5), math.log(8.0))
    return typical_size(factor) ** 2 * jnp.exp(spread)


def attention_factor():
    return jnp.array([0.1, 0.1, 0.5, 0.3], jnp.float32).reshape(4, 1, 1)


def norm_factor():
    return jnp.array([1.0, 1.0, 0.5, 0.5], jnp.float32).reshape(4, 1)


def draw_attn_w(key, part):
    key = jax.random.fold_in(key, 3)
    scales = jnp.array([1.0, 1.0, 1.0, math.sqrt(40.0)], jnp.float32).reshape(4, 1, 1)
    return jax.random.normal(key, (4, D, D), jnp.float32) * scales / math.sqrt(D)


def draw_norm_params(key, part):
    key = jax.random.fold_in(key, 5)
    centre = jnp.array([1.0, 0.0, 1.0, 0.0], jnp.float32).reshape(4, 1)
    spread = jnp.array([0.15, 0.3, 0.15, 0.3], jnp.float32).reshape(4, 1)
    return centre + spread * jax.random.normal(key, (4, D), jnp.float32)


def draw_attn_m(key, part):
    key = jax.random.fold_in(key, 11)
    return first_moment(key, (4, D, D), attention_factor())


def draw_attn_v(key, part):
    key = jax.random.fold_in(key, 12)
    return second_moment(key, (4, D, D), attention_factor())


def draw_ffn_in_m(key, part):
    key = jax.random.fold_in(key, 13)
    return first_moment(key, (D, FF), 0.35)


def draw_ffn_in_v(key, part):
    key = jax.random.fold_in(key, 14)
    return second_moment(key, (D, FF), 0.35)


def draw_ffn_out_m(key, part):
    key = jax.random.fold_in(key, 15)
    return first_moment(key, (FF, D), 0.65)


def draw_ffn_out_v(key, part):
    key = jax.random.fold_in(key, 16)
    return second_moment(key, (FF, D), 0.65)


def draw_norm_m(key, part):
    key = jax.random.fold_in(key, 17)
    return first_moment(key, (4, D), norm_factor())


def draw_norm_v(key, part):
    key = jax.random.fold_in(key, 18)
    return second_moment(key, (4, D), norm_factor())


def touch_ends(values, stream_key, low, top_value):
    longest = values.shape.index(max(values.shape))
    spots = []
    for shift in (0, 1):
        where = [jax.random.randint(jax.random.fold_in(stream_key, axis), (), 0, length) for axis, length in enumerate(values.shape)]
        where[longest] = (where[longest] + shift) % values.shape[longest]
        spots.append(tuple(where))
    return values.at[spots[0]].set(low).at[spots[1]].set(top_value)


def shard_levels(own_key, shape, pieces, smallest, top_value):
    def one(dim, parts):
        draws = jax.random.uniform(jax.random.fold_in(jax.random.fold_in(own_key, 6), dim), (parts,), jnp.float32, smallest / len(pieces), top_value / len(pieces))
        return jnp.repeat(jnp.exp(draws), shape[dim] // parts).reshape((-1,) + (1,) * (len(shape) - dim - 1))

    factor_of = one(*pieces[0])
    for cut in pieces[1:]:
        factor_of = factor_of * one(*cut)
    return factor_of


def normal_values(key, dims, width, most, pieces=(), kind=jnp.bfloat16):
    values = jax.random.normal(key, dims, jnp.float32) * width
    if len(pieces) > 0:
        values = shard_levels(key, dims, pieces, -0.22, 0.18) * values
    return jnp.clip(values, min=-most, max=most).astype(kind)


def setup_inputs(seed: int = 0) -> dict:
    seeds = jax.random.split(jax.random.key(seed), 19)
    frames = normal_values(seeds[0], (ROWS, D), 1.0, 6.0, ((0, 32),))
    memory = normal_values(seeds[1], (SPANS * MEM, D), 1.0, 6.0, ((0, 32),))
    left_keys = normal_values(seeds[2], (SPANS * LEFT, D), 1.0, 6.0, ((0, 32),))
    left_values = normal_values(seeds[3], (SPANS * LEFT, D), 1.0, 6.0, ((0, 32),))
    lengths = touch_ends(jax.random.randint(seeds[4], (SPANS,), 4, SEG + 1), jax.random.fold_in(seeds[4], 1), 4, SEG).astype(jnp.int32)
    cotangent = normal_values(seeds[5], (ROWS, D), 1.0, 6.0, ((0, 32),))
    attn_w = draw_attn_w(jax.random.fold_in(seeds[18], 71), 0)
    ffn_in = normal_values(seeds[7], (D, FF), D ** -0.5, 0.25, ((0, 8),), jnp.float32)
    ffn_out = normal_values(seeds[8], (FF, D), FF ** -0.5, 0.125, ((0, 8),), jnp.float32)
    norm_params = draw_norm_params(jax.random.fold_in(seeds[18], 71), 0)
    attn_m = draw_attn_m(jax.random.fold_in(seeds[18], 71), 0)
    attn_v = draw_attn_v(jax.random.fold_in(seeds[18], 71), 0)
    ffn_in_m = draw_ffn_in_m(jax.random.fold_in(seeds[18], 71), 0)
    ffn_in_v = draw_ffn_in_v(jax.random.fold_in(seeds[18], 71), 0)
    ffn_out_m = draw_ffn_out_m(jax.random.fold_in(seeds[18], 71), 0)
    ffn_out_v = draw_ffn_out_v(jax.random.fold_in(seeds[18], 71), 0)
    norm_m = draw_norm_m(jax.random.fold_in(seeds[18], 71), 0)
    norm_v = draw_norm_v(jax.random.fold_in(seeds[18], 71), 0)
    return {"frames": frames, "memory": memory, "left_keys": left_keys, "left_values": left_values, "lengths": lengths, "cotangent": cotangent, "attn_w": attn_w, "ffn_in": ffn_in, "ffn_out": ffn_out, "norm_params": norm_params, "attn_m": attn_m, "attn_v": attn_v, "ffn_in_m": ffn_in_m, "ffn_in_v": ffn_in_v, "ffn_out_m": ffn_out_m, "ffn_out_v": ffn_out_v, "norm_m": norm_m, "norm_v": norm_v}


@jax.custom_vjp
def low(v):
    return lax.optimization_barrier(v.astype(jnp.bfloat16)).astype(jnp.float32)

@jax.custom_vjp
def low_back(v):
    return v

def low_keep(v):
    return (low(v), None)

def low_pass(kept, grad):
    return (grad,)

def back_keep(v):
    return (v, None)

def back_low(kept, grad):
    return (low(grad),)
low.defvjp(low_keep, low_pass)
low_back.defvjp(back_keep, back_low)
eps_norm = 1e-05
beta_first = 0.5
beta_second = 0.5
weight_decay = 0.01
eps_adam = 1e-08
rates_attention = (0.04, 0.04, 0.04, 0.25)
rate_ffn_in = 0.04
rate_ffn_out = 0.02
rate_norm = 0.2
masked_score = -1000000000.0

def round_both(values):
    return low_back(low(values))

def layer_norm(values, gain, shift):
    row_mean = lax.optimization_barrier(jnp.mean(values, axis=-1, keepdims=True))
    centred = values - row_mean
    variance = lax.optimization_barrier(jnp.mean(centred * centred, axis=-1, keepdims=True))
    return centred * lax.rsqrt(variance + eps_norm) * gain + shift

def dot_high(left, right):
    return jnp.dot(left, right, precision=lax.Precision.HIGHEST, preferred_element_type=jnp.float32)

def key_mask(lengths):
    position = jnp.arange(KEYS, dtype=jnp.int32)[None, :]
    fixed_part = (position < MEM + LEFT) | (position >= MEM + LEFT + SEG)
    return fixed_part | (position - (MEM + LEFT) < lengths[:, None])

def block_apply(weights_low, frames, memory, left_keys, left_values, lengths):
    attn_w, ffn_in, ffn_out, norm_params = weights_low
    span_count = lengths.shape[0]
    head_size = D // HEADS
    hidden = low(layer_norm(frames, norm_params[0], norm_params[1]))
    query = round_both(dot_high(hidden, attn_w[0]))
    key_all = round_both(jnp.concatenate([dot_high(memory, attn_w[1]).reshape(span_count, MEM, D), left_keys.reshape(span_count, LEFT, D), dot_high(hidden, attn_w[1]).reshape(span_count, ROWS_SPAN, D)], axis=1))
    value_all = round_both(jnp.concatenate([dot_high(memory, attn_w[2]).reshape(span_count, MEM, D), left_values.reshape(span_count, LEFT, D), dot_high(hidden, attn_w[2]).reshape(span_count, ROWS_SPAN, D)], axis=1))
    query_heads = query.reshape(span_count, ROWS_SPAN, HEADS, head_size)
    key_heads = key_all.reshape(span_count, KEYS, HEADS, head_size)
    value_heads = value_all.reshape(span_count, KEYS, HEADS, head_size)
    score_scale = 1.0 / math.sqrt(head_size)
    scores = low_back(jnp.einsum('cqhe,ckhe->chqk', query_heads, key_heads, precision=lax.Precision.HIGHEST) * score_scale)
    scores = jnp.where(key_mask(lengths)[:, None, None, :], scores, masked_score)
    soft_probs = jax.nn.softmax(scores, axis=-1)
    attended = round_both(jnp.einsum('chqk,ckhe->cqhe', low(soft_probs), value_heads, precision=lax.Precision.HIGHEST)).reshape(span_count * ROWS_SPAN, D)
    residual = frames + low_back(dot_high(attended, attn_w[3]))
    hidden_two = low(layer_norm(residual, norm_params[2], norm_params[3]))
    inner_pre = low_back(dot_high(hidden_two, ffn_in))
    activated = low(jax.nn.gelu(inner_pre))
    return residual + low_back(dot_high(activated, ffn_out))

def adamw_update(weight, grad_sum, first_old, second_old, rate):
    first_new = beta_first * first_old + (1.0 - beta_first) * grad_sum
    second_new = beta_second * second_old + (1.0 - beta_second) * grad_sum * grad_sum
    first_hat = first_new / (1.0 - beta_first ** STEP)
    second_hat = second_new / (1.0 - beta_second ** STEP)
    weight_new = weight - rate * (first_hat / (jnp.sqrt(second_hat) + eps_adam) + weight_decay * weight)
    return (first_new, second_new, weight_new)

def reference(frames, memory, left_keys, left_values, lengths, cotangent, attn_w, ffn_in, ffn_out, norm_params, attn_m, attn_v, ffn_in_m, ffn_in_v, ffn_out_m, ffn_out_v, norm_m, norm_v):
    weights_low = (low(attn_w), low(ffn_in), low(ffn_out), low(norm_params))
    group = math.gcd(SPANS, 128)
    frames_all = frames.astype(jnp.float32)
    memory_all = memory.astype(jnp.float32)
    keys_all = left_keys.astype(jnp.float32)
    values_all = left_values.astype(jnp.float32)
    cotangent_all = cotangent.astype(jnp.float32)

    def group_step(grad_total, group_index):
        span_start = group_index * group

        def piece(array, rows_each):
            return lax.dynamic_slice_in_dim(array, span_start * rows_each, group * rows_each, 0)
        memory_part = piece(memory_all, MEM)
        keys_part = piece(keys_all, LEFT)
        values_part = piece(values_all, LEFT)
        lengths_part = lax.dynamic_slice_in_dim(lengths, span_start, group, 0)

        def apply_part(weights_in, frames_in):
            return block_apply(weights_in, frames_in, memory_part, keys_part, values_part, lengths_part)
        result, pull_back = jax.vjp(apply_part, weights_low, piece(frames_all, ROWS_SPAN))
        weight_grads, frames_grad = pull_back(piece(cotangent_all, ROWS_SPAN))
        grad_total = jax.tree.map(jnp.add, grad_total, weight_grads)
        return (grad_total, (result.astype(jnp.bfloat16), frames_grad))
    grad_zero = tuple((jnp.zeros_like(weight) for weight in weights_low))
    grad_total, (outputs, input_grads) = lax.scan(group_step, grad_zero, jnp.arange(SPANS // group, dtype=jnp.int32))
    output = outputs.reshape(ROWS, D)
    input_grad = input_grads.reshape(ROWS, D)
    attn_grad, in_grad, out_grad, norm_grad = grad_total
    attn_rate = jnp.array(rates_attention, jnp.float32).reshape(4, 1, 1)
    attn_first, attn_second, attn_new = adamw_update(attn_w, attn_grad, attn_m, attn_v, attn_rate)
    in_first, in_second, in_new = adamw_update(ffn_in, in_grad, ffn_in_m, ffn_in_v, rate_ffn_in)
    out_first, out_second, out_new = adamw_update(ffn_out, out_grad, ffn_out_m, ffn_out_v, rate_ffn_out)
    norm_first, norm_second, norm_new = adamw_update(norm_params, norm_grad, norm_m, norm_v, rate_norm)
    return (output, input_grad, attn_grad, attn_first, attn_second, attn_new, attn_new.astype(jnp.bfloat16), in_grad, in_first, in_second, in_new, in_new.astype(jnp.bfloat16), out_grad, out_first, out_second, out_new, out_new.astype(jnp.bfloat16), norm_grad, norm_first, norm_second, norm_new, norm_new.astype(jnp.bfloat16))
```

```python
import functools
import math

import jax
import jax.numpy as jnp
import numpy as np
from jax import lax
from jax.experimental import pallas as pl
from jax.experimental.pallas import tpu as pltpu
from jax.sharding import PartitionSpec as P

D = 512
FF = 2048
HEADS = 8
SEG = 16
LEFT = 30
MEM = 4
STEP = 5
ROWS_SPAN = 20
GROUP = 4
QROWS = GROUP * ROWS_SPAN
MROWS = GROUP * MEM
LROWS = GROUP * LEFT
LWIN = 128
KPAD = 256
HALF = 256
PAIR = 128
NORM_ROWS = 16

F32 = jnp.float32
BF16 = jnp.bfloat16
BLOCKED = -1e9
EPS_NORM = 1e-05
BETA_FIRST = 0.5
BETA_SECOND = 0.5
WEIGHT_DECAY = 0.01
EPS_ADAM = 1e-08
RATES_ATTENTION = (0.04, 0.04, 0.04, 0.25)
RATE_FFN_IN = 0.04
RATE_FFN_OUT = 0.02
RATE_NORM = 0.2
VMEM_LIMIT = 56 * 2**20


def dot(a, b):
    return lax.dot_general(a, b, (((1,), (0,)), ((), ())), preferred_element_type=F32)


def dot_last(a, b):
    return lax.dot_general(a, b, (((1,), (1,)), ((), ())), preferred_element_type=F32)


def dot_rows(a, b):
    return lax.dot_general(a, b, (((0,), (0,)), ((), ())), preferred_element_type=F32)


def normalize(x):
    mean = jnp.mean(x, axis=1, keepdims=True)
    centred = x - mean
    variance = jnp.mean(centred * centred, axis=1, keepdims=True)
    scale = lax.rsqrt(variance + EPS_NORM)
    return centred * scale, scale


def norm_back(grad, normed, scale, gain):
    grad = grad * gain
    first = jnp.mean(grad, axis=1, keepdims=True)
    second = jnp.mean(grad * normed, axis=1, keepdims=True)
    return scale * (grad - first - normed * second)


def gelu_parts(x):
    c = math.sqrt(2.0 / math.pi)
    square = x * x
    t = jnp.tanh(x * (c + (c * 0.044715) * square))
    half = 0.5 * x
    value = half + half * t
    slope = 0.5 + 0.5 * t + half * (1.0 - t * t) * (c + (3.0 * c * 0.044715) * square)
    return value, slope


def spread_pair(x):
    lane = lax.broadcasted_iota(jnp.int32, x.shape, 1)
    zero = jnp.zeros_like(x)
    return jnp.concatenate([jnp.where(lane < 64, x, zero), jnp.where(lane < 64, zero, x)], axis=0)


def join_pair(x):
    rows = x.shape[0] // 2
    lane = lax.broadcasted_iota(jnp.int32, (rows, PAIR), 1)
    return jnp.where(lane < 64, x[:rows], x[rows:])


def left_start(g):
    return LROWS * g - (8 if g % 2 else 0)


def span_masks():
    query_span = np.arange(2 * QROWS) % QROWS // ROWS_SPAN
    masks = np.full((2, 2 * QROWS, KPAD), BLOCKED, np.float32)
    for odd in range(2):
        span = np.full(KPAD, -1)
        span[:MROWS] = np.arange(MROWS) // MEM
        span[MROWS : MROWS + QROWS] = np.arange(QROWS) // ROWS_SPAN
        start = MROWS + QROWS + (8 if odd else 0)
        span[start : start + LROWS] = np.arange(LROWS) // LEFT
        masks[odd][query_span[:, None] == span[None, :]] = 0.0
    return masks


def length_bias(lengths):
    groups = lengths.shape[0] // GROUP
    key = np.arange(KPAD)
    is_frame = (key >= MROWS) & (key < MROWS + QROWS)
    place = np.where(is_frame, (key - MROWS) % ROWS_SPAN, 0)
    span = np.where(is_frame, (key - MROWS) // ROWS_SPAN, 0)
    own = lengths.reshape(groups, GROUP)
    length = jnp.zeros((groups, KPAD), jnp.int32)
    for s in range(GROUP):
        length = jnp.where(jnp.asarray(span == s)[None, :], own[:, s : s + 1], length)
    dead = jnp.asarray(is_frame & (place < SEG))[None, :] & (jnp.asarray(place)[None, :] >= length)
    return jnp.where(dead, BLOCKED, 0.0).astype(F32).reshape(groups, 1, KPAD)


def adamw(weight, grad, first_old, second_old, rate):
    first = BETA_FIRST * first_old + (1.0 - BETA_FIRST) * grad
    second = BETA_SECOND * second_old + (1.0 - BETA_SECOND) * grad * grad
    first_hat = first / (1.0 - BETA_FIRST**STEP)
    second_hat = second / (1.0 - BETA_SECOND**STEP)
    new = weight - rate * (first_hat / (jnp.sqrt(second_hat) + EPS_ADAM) + WEIGHT_DECAY * weight)
    return first, second, new


class Places:
    def __init__(self, mesh):
        self.n = mesh.shape["fsdp"]
        self.dp = mesh.shape["dp"]
        power = max(int(math.log2(self.n)) - 1, 0) // 2
        self.X = 2**power
        self.Z = self.n // self.X
        self.C = 2
        self.Y = self.dp // self.C

    def me(self):
        f = lax.axis_index("fsdp")
        d = lax.axis_index("dp")
        return jnp.stack([f // self.X, f % self.X, d % self.C]).astype(jnp.int32)

    def slot_to(self, me_ref, f):
        dz = lax.rem(f // self.X + self.Z - me_ref[0], self.Z)
        dx = lax.rem(f % self.X + self.X - me_ref[1], self.X)
        return dx * self.Z + dz

    def slot_from(self, me_ref, f):
        dz = lax.rem(me_ref[0] + self.Z - f // self.X, self.Z)
        dx = lax.rem(me_ref[1] + self.X - f % self.X, self.X)
        return dx * self.Z + dz

    def shift(self, value, dz, dx):
        X, Z = self.X, self.Z
        perm = [
            (z * X + x, (z + dz) % Z * X + (x + dx) % X) for z in range(Z) for x in range(X)
        ]
        return lax.ppermute(value, "fsdp", perm)

    def other_core(self, value):
        return lax.ppermute(value, "dp", [(d, d ^ 1) for d in range(self.dp)])

    def sum_over_y(self, value):
        step = 1
        while step < self.Y:
            got = lax.ppermute(value, "dp", [(d, d ^ (2 * step)) for d in range(self.dp)])
            value = (value.astype(F32) + got.astype(F32)).astype(BF16)
            step *= 2
        return value


def call(kernel, me, grid, ins, outs, scratch, name, flops=0, moved=0, aliases=None):
    def spec(block, index):
        if block is None:
            return pl.BlockSpec(memory_space=pl.ANY)
        return pl.BlockSpec(block, lambda *a: index(*a[:-1]))

    return pl.pallas_call(
        kernel,
        grid_spec=pltpu.PrefetchScalarGridSpec(
            num_scalar_prefetch=1,
            grid=grid,
            in_specs=[spec(b, f) for _, b, f in ins],
            out_specs=[spec(b, f) for _, _, b, f in outs],
            scratch_shapes=scratch,
        ),
        out_shape=[jax.ShapeDtypeStruct(s, d) for s, d, _, _ in outs],
        compiler_params=pltpu.CompilerParams(vmem_limit_bytes=VMEM_LIMIT),
        cost_estimate=pl.CostEstimate(flops=flops, bytes_accessed=moved, transcendentals=0),
        input_output_aliases=aliases or {},
        name=name,
    )(me, *[a for a, _, _ in ins])


def whole(shape):
    return shape, lambda i: (0,) * len(shape)


def rows_of(shape, column=0):
    return shape, lambda i: (i, column)


def pack_first(me, attn_w, norm_params, places):
    r = D // places.n
    h = r // 2

    def kernel(me_ref, w_ref, n_ref, out_ref, scratch):
        lower = me_ref[2] == 0
        for k in range(3):
            w = w_ref[k]
            out_ref[k * h : (k + 1) * h, :] = jnp.where(lower, w[:h], w[h:]).astype(BF16)
        scratch[...] = jnp.zeros_like(scratch)
        scratch[0:4, 0:r] = n_ref[...]
        out_ref[3 * h :, :] = scratch[...].astype(BF16)

    (out,) = call(
        kernel,
        me,
        (1,),
        [
            (attn_w, (3, r, HALF), lambda i: (0, 0, 0)),
            (norm_params, *whole((4, r))),
        ],
        [((3 * h + NORM_ROWS, HALF), BF16, *whole((3 * h + NORM_ROWS, HALF)))],
        [pltpu.VMEM((NORM_ROWS, HALF), F32)],
        "pack_first",
        moved=4 * 3 * r * HALF,
    )
    return out


def pack_rest(me, attn_w, ffn_in, ffn_out, places):
    r, r2 = D // places.n, FF // places.n
    h = r // 2

    def kernel(me_ref, w_ref, in_ref, out_w_ref, second_ref, up_ref, down_ref):
        lower = me_ref[2] == 0
        for k in range(3):
            w = w_ref[k, :, HALF:]
            second_ref[k * h : (k + 1) * h, :] = jnp.where(lower, w[:h], w[h:]).astype(BF16)
        half = FF // 2
        for k in range(4):
            up_ref[k * r : (k + 1) * r, :] = jnp.where(
                lower,
                in_ref[:, k * HALF : (k + 1) * HALF],
                in_ref[:, half + k * HALF : half + (k + 1) * HALF],
            ).astype(BF16)
        down_ref[:r2, :] = jnp.where(lower, out_w_ref[:, :HALF], out_w_ref[:, HALF:]).astype(BF16)
        w = w_ref[3]
        down_ref[r2:, :] = jnp.where(lower, w[:, :HALF], w[:, HALF:]).astype(BF16)

    return call(
        kernel,
        me,
        (1,),
        [
            (attn_w, *whole((4, r, D))),
            (ffn_in, *whole((r, FF))),
            (ffn_out, *whole((r2, D))),
        ],
        [
            ((3 * h, HALF), BF16, *whole((3 * h, HALF))),
            ((4 * r, HALF), BF16, *whole((4 * r, HALF))),
            ((r2 + r, HALF), BF16, *whole((r2 + r, HALF))),
        ],
        [],
        "pack_rest",
        moved=4 * (4 * r * D + r * FF + r2 * D),
    )


def attention_forward(me, pair, x, memory, left_keys, left_values, bias, masks, weights, places):
    first = pair == 0
    fresh = pair % 2 == 0
    spans = memory.shape[0] // MEM
    step_spans = 32 if spans % 32 == 0 else 16
    groups = step_spans // GROUP
    rows = step_spans * ROWS_SPAN
    n, r = places.n, D // places.n
    h = r // 2

    def kernel(me_ref, x_ref, mem_ref, lk_ref, lv_ref, bias_ref, mask_ref, *rest):
        if fresh:
            own_ref, other_ref, *rest = rest
        else:
            w_ref, *rest = rest
        qkv_ref, kvm_ref, att_ref, p_ref, *rest = rest
        if fresh:
            w_ref, *rest = rest
        if first:
            hid_ref, xhat_ref, memt_ref, norm_ref, *rest = rest
        ks, vs = rest

        @pl.when(pl.program_id(0) == 0)
        def _():
            ks[...] = jnp.zeros_like(ks)
            vs[...] = jnp.zeros_like(vs)
            lower = me_ref[2] == 0
            if first:
                norm_ref[...] = jnp.zeros_like(norm_ref)
            if fresh:
                for f in range(n):
                    slot = places.slot_from(me_ref, f)
                    mine, sib = own_ref[slot], other_ref[slot]
                    for at, part in (
                        (slice(f * r, f * r + h), jnp.where(lower, mine, sib)),
                        (slice(f * r + h, (f + 1) * r), jnp.where(lower, sib, mine)),
                    ):
                        for k in range(3):
                            for side in range(2):
                                w_ref[side, at, k * PAIR : (k + 1) * PAIR] = part[
                                    k * h : (k + 1) * h, side * PAIR : (side + 1) * PAIR
                                ]
                    if first:
                        tail = mine[3 * h :, :].astype(F32)
                        norm_ref[:, f * r : (f + 1) * r] = tail[0:8, 0:r]

        w = w_ref[0]
        if first:
            xhat, _ = normalize(x_ref[...].astype(F32))
            xhat_ref[...] = xhat.astype(BF16).T
            memt_ref[...] = mem_ref[...].T
            hidden = (xhat * norm_ref[0:1, :] + norm_ref[1:2, :]).astype(BF16)
            hid_ref[...] = hidden
        else:
            hidden = x_ref[...]
        qkv = dot(hidden, w).astype(BF16)
        query = qkv[:, :PAIR] * jnp.asarray(0.125, BF16)
        qkv_ref[:, :PAIR] = query
        qkv_ref[:, PAIR:] = qkv[:, PAIR:]
        kvm = dot(mem_ref[...], w[:, PAIR:]).astype(BF16)
        kvm_ref[...] = kvm
        for g in range(groups):
            ls = left_start(g)
            for dest, low, src in ((ks, 0, lk_ref), (vs, PAIR, lv_ref)):
                dest[g, 0:MROWS, :] = kvm[MROWS * g : MROWS * (g + 1), low : low + PAIR]
                dest[g, MROWS : MROWS + QROWS, :] = qkv[
                    QROWS * g : QROWS * (g + 1), PAIR + low : 2 * PAIR + low
                ]
                dest[g, MROWS + QROWS : MROWS + QROWS + LWIN, :] = src[ls : ls + LWIN, :]
        for g in range(groups):
            dead = mask_ref[g % 2] + bias_ref[g]
            scores = dot_last(spread_pair(query[QROWS * g : QROWS * (g + 1)]), ks[g]) + dead
            e = jnp.exp(scores - jnp.max(scores, axis=1, keepdims=True))
            probs = (e * (1.0 / jnp.sum(e, axis=1, keepdims=True))).astype(BF16)
            p_ref[2 * QROWS * g : 2 * QROWS * (g + 1), :] = probs
            att_ref[QROWS * g : QROWS * (g + 1), :] = join_pair(dot(probs, vs[g])).astype(BF16)

    count = x.shape[0]
    ins = [
        (x, *rows_of((rows, D))),
        (memory, *rows_of((step_spans * MEM, D))),
        (left_keys, *rows_of((step_spans * LEFT, PAIR), pair)),
        (left_values, *rows_of((step_spans * LEFT, PAIR), pair)),
        (bias, (groups, 1, KPAD), lambda i: (i, 0, 0)),
        (masks, *whole((2, 2 * QROWS, KPAD))),
    ]
    outs = [
        ((count, 3 * PAIR), BF16, *rows_of((rows, 3 * PAIR))),
        ((spans * MEM, 2 * PAIR), BF16, *rows_of((step_spans * MEM, 2 * PAIR))),
        ((count, PAIR), BF16, *rows_of((rows, PAIR))),
        ((2 * spans * ROWS_SPAN, KPAD), BF16, *rows_of((2 * rows, KPAD))),
    ]
    if fresh:
        ins += [(a, *whole(a.shape)) for a in weights]
        outs += [((2, D, 3 * PAIR), BF16, *whole((2, D, 3 * PAIR)))]
    else:
        ins += [(weights, (1, D, 3 * PAIR), lambda i: (1, 0, 0))]
    if first:
        columns = lambda i: (0, i)
        outs += [
            ((count, D), BF16, *rows_of((rows, D))),
            ((D, count), BF16, (D, rows), columns),
            ((D, spans * MEM), BF16, (D, step_spans * MEM), columns),
            ((8, D), F32, *whole((8, D))),
        ]
    return call(
        kernel,
        me,
        (spans // step_spans,),
        ins,
        outs,
        [pltpu.VMEM((groups, KPAD, PAIR), BF16)] * 2,
        f"attention_forward_{pair}",
        flops=2 * count * D * 3 * PAIR * 4,
        moved=2 * (count * D * 2 + spans * LEFT * PAIR * 2 + spans * 2 * ROWS_SPAN * KPAD),
    )


def feed_forward(me, attended_pairs, frames, cotangent, norm, up, down, places):
    count = frames.shape[0]
    rows = 512
    steps = count // rows
    chunk = 1024
    n, r, r2 = places.n, D // places.n, FF // places.n
    X, Z = places.X, places.Z

    def kernel(me_ref, a0, a1, a2, a3, fr_ref, cot_ref, norm_ref, *rest):
        up_refs, other_up_refs = rest[:X], rest[X : 2 * X]
        down_refs, other_down_refs = rest[2 * X : 3 * X], rest[3 * X : 4 * X]
        out_ref, res_ref, gatt_ref, gn_ref, keep_up, send_up, keep_down, send_down = rest[4 * X : 4 * X + 8]
        w1, w2, wo, acc1, acc2, acco = rest[4 * X + 8 :]
        i = pl.program_id(0)
        lower = me_ref[2] == 0

        @pl.when(i == 0)
        def _():
            acc1[...] = jnp.zeros_like(acc1)
            acc2[...] = jnp.zeros_like(acc2)
            acco[...] = jnp.zeros_like(acco)
            gn_ref[...] = jnp.zeros_like(gn_ref)
            for dx in range(X):
                xx = lax.rem(me_ref[1] + X - dx, X)
                for dz in range(Z):
                    zz = lax.rem(me_ref[0] + Z - dz, Z)
                    f = zz * X + xx

                    def halves(mine, sib):
                        return jnp.where(lower, mine, sib), jnp.where(lower, sib, mine)

                    low, high = halves(up_refs[dx][dz], other_up_refs[dx][dz])
                    at = pl.ds(pl.multiple_of(f * r, r), r)
                    at2 = pl.ds(pl.multiple_of(f * r2, r2), r2)
                    for k in range(4):
                        w1[at, k * HALF : (k + 1) * HALF] = low[k * r : (k + 1) * r]
                        w1[at, FF // 2 + k * HALF : FF // 2 + (k + 1) * HALF] = high[k * r : (k + 1) * r]
                    low, high = halves(down_refs[dx][dz], other_down_refs[dx][dz])
                    w2[at2, :HALF] = low[:r2]
                    w2[at2, HALF:] = high[:r2]
                    wo[at, :HALF] = low[r2:]
                    wo[at, HALF:] = high[r2:]

        attended = jnp.concatenate([a0[...], a1[...], a2[...], a3[...]], axis=1)
        residual = fr_ref[...].astype(F32) + dot(attended, wo[...])
        normed, scale = normalize(residual)
        gain = norm_ref[2:3, :]
        hidden = (normed * gain + norm_ref[3:4, :]).astype(BF16)
        cot = cot_ref[...]
        output = residual
        grad = None
        for j in range(FF // chunk):
            s = slice(j * chunk, (j + 1) * chunk)
            inner = dot(hidden, w1[:, s])
            grad_act = dot_last(cot, w2[s, :])
            value, slope = gelu_parts(inner)
            active = value.astype(BF16)
            grad_inner = (grad_act * slope).astype(BF16)
            output = output + dot(active, w2[s, :])
            part = dot_last(grad_inner, w1[:, s])
            grad = part if grad is None else grad + part
            acc1[:, s] += dot_rows(hidden, grad_inner)
            acc2[:, s] += dot_rows(cot, active)
        out_ref[...] = output.astype(BF16)
        gn_ref[0:1, :] += jnp.sum(grad * normed, axis=0, keepdims=True)
        gn_ref[1:2, :] += jnp.sum(grad, axis=0, keepdims=True)
        grad_residual = cot.astype(F32) + norm_back(grad, normed, scale, gain)
        res_ref[...] = grad_residual
        grad_low = grad_residual.astype(BF16)
        gatt_ref[...] = dot_last(grad_low, wo[...]).astype(BF16)
        acco[...] += dot_rows(attended, grad_low)

        @pl.when(i == steps - 1)
        def _():
            for f in range(n):
                slot = places.slot_to(me_ref, f)

                def put(keep_ref, send_ref, at, low, high):
                    low, high = low.astype(BF16), high.astype(BF16)
                    keep_ref[slot, at, :] = jnp.where(lower, low, high)
                    send_ref[slot, at, :] = jnp.where(lower, high, low)

                here = slice(f * r, (f + 1) * r)
                for k in range(4):
                    put(
                        keep_up,
                        send_up,
                        slice(k * r, (k + 1) * r),
                        acc1[here, k * HALF : (k + 1) * HALF],
                        acc1[here, FF // 2 + k * HALF : FF // 2 + (k + 1) * HALF],
                    )
                turned = acc2[:, f * r2 : (f + 1) * r2].T
                put(keep_down, send_down, slice(0, r2), turned[:, :HALF], turned[:, HALF:])
                put(keep_down, send_down, slice(r2, r2 + r), acco[here, :HALF], acco[here, HALF:])

    wires = [(n, 4 * r, HALF)] * 2 + [(n, r2 + r, HALF)] * 2
    return call(
        kernel,
        me,
        (steps,),
        [(a, *rows_of((rows, PAIR))) for a in attended_pairs]
        + [
            (frames, *rows_of((rows, D))),
            (cotangent, *rows_of((rows, D))),
            (norm, *whole((8, D))),
        ]
        + [(a, *whole(a.shape)) for a in (*up[0], *up[1], *down[0], *down[1])],
        [
            ((count, D), BF16, *rows_of((rows, D))),
            ((count, D), F32, *rows_of((rows, D))),
            ((count, D), BF16, *rows_of((rows, D))),
            ((8, D), F32, *whole((8, D))),
        ]
        + [(wire, BF16, *whole(wire)) for wire in wires],
        [
            pltpu.VMEM((D, FF), BF16),
            pltpu.VMEM((FF, D), BF16),
            pltpu.VMEM((D, D), BF16),
            pltpu.VMEM((D, FF), F32),
            pltpu.VMEM((D, FF), F32),
            pltpu.VMEM((D, D), F32),
        ],
        "feed_forward",
        flops=2 * count * D * (6 * FF + 3 * D) * 2,
        moved=2 * count * D * 8,
    )


def attention_backward(me, pair, xhat, memory_t, left_keys, left_values, saved, grad_att, norm, norm_parts, places):
    last = norm_parts is not None
    qkv, kvm, probs, weights = saved
    spans = memory_t.shape[1] // MEM
    step_spans = 32 if spans % 32 == 0 else 16
    steps = spans // step_spans
    groups = step_spans // GROUP
    rows = step_spans * ROWS_SPAN
    n, r = places.n, D // places.n
    h = r // 2
    m = 3 * h + (NORM_ROWS if last else 0)
    side = pair % 2
    parts = norm_parts if last else []

    def kernel(me_ref, xhat_ref, mem_ref, lk_ref, lv_ref, qkv_ref, kvm_ref, p_ref, da_ref, w_ref, norm_ref, *rest):
        part_refs = rest[: len(parts)]
        d_ref, keep_ref, send_ref, gn_ref, ks, vs, dm, acc, accm, sums = rest[len(parts) :]
        i = pl.program_id(0)

        @pl.when(i == 0)
        def _():
            ks[...] = jnp.zeros_like(ks)
            vs[...] = jnp.zeros_like(vs)
            acc[...] = jnp.zeros_like(acc)
            accm[...] = jnp.zeros_like(accm)
            sums[...] = jnp.zeros_like(sums)

        for g in range(groups):
            ls = left_start(g)
            for dest, low, src in ((ks, 0, lk_ref), (vs, PAIR, lv_ref)):
                dest[g, 0:MROWS, :] = kvm_ref[MROWS * g : MROWS * (g + 1), low : low + PAIR]
                dest[g, MROWS : MROWS + QROWS, :] = qkv_ref[
                    QROWS * g : QROWS * (g + 1), PAIR + low : 2 * PAIR + low
                ]
                dest[g, MROWS + QROWS : MROWS + QROWS + LWIN, :] = src[ls : ls + LWIN, :]
        for g in range(groups):
            here = slice(QROWS * g, QROWS * (g + 1))
            there = slice(MROWS * g, MROWS * (g + 1))
            q = spread_pair(qkv_ref[here, :PAIR])
            da = spread_pair(da_ref[here, :])
            p = p_ref[2 * QROWS * g : 2 * QROWS * (g + 1), :]
            wide = p.astype(F32)
            dp = dot_last(da, vs[g])
            ds = (wide * (dp - jnp.sum(wide * dp, axis=1, keepdims=True))).astype(BF16)
            d_ref[here, 0:PAIR] = (join_pair(dot(ds, ks[g])) * 0.125).astype(BF16)
            dk = dot_rows(ds[:, :PAIR], q).astype(BF16)
            dv = dot_rows(p[:, :PAIR], da).astype(BF16)
            d_ref[here, PAIR : 2 * PAIR] = dk[MROWS : MROWS + QROWS]
            d_ref[here, 2 * PAIR :] = dv[MROWS : MROWS + QROWS]
            dm[there, :PAIR] = dk[:MROWS]
            dm[there, PAIR:] = dv[:MROWS]
        d = d_ref[...]
        acc[...] += dot(xhat_ref[...], d)
        accm[...] += dot(mem_ref[...], dm[...])
        sums[0:1, :] += jnp.sum(d.astype(F32), axis=0, keepdims=True)

        @pl.when(i == steps - 1)
        def _():
            lower = me_ref[2] == 0
            w = w_ref[0].astype(F32)
            total = acc[...]
            row_sum = sums[0:1, :]
            lane = lax.broadcasted_iota(jnp.int32, (D, PAIR), 1)
            gain_grad = jnp.sum(total * w, axis=1, keepdims=True)
            shift_grad = jnp.sum(row_sum * w, axis=1, keepdims=True)
            turned = jnp.where(lane == 0, gain_grad, jnp.where(lane == 1, shift_grad, 0.0)).T[0:8, :]
            gn_ref[...] = turned
            columns = jnp.where(
                lax.broadcasted_iota(jnp.int32, (PAIR, D), 0) == 0,
                norm_ref[0:1, :],
                jnp.where(lax.broadcasted_iota(jnp.int32, (PAIR, D), 0) == 1, norm_ref[1:2, :], 0.0),
            ).T
            grads = total * columns[:, 0:1] + columns[:, 1:2] * row_sum
            gq = grads[:, :PAIR]
            gk = grads[:, PAIR : 2 * PAIR] + accm[:, :PAIR]
            gv = grads[:, 2 * PAIR :] + accm[:, PAIR:]
            if last:
                first_norm = turned
                for ref in part_refs[1:]:
                    first_norm = first_norm + ref[...]
                norm_grad = jnp.concatenate([first_norm[0:2], part_refs[0][0:2, :], jnp.zeros((12, D), F32)], axis=0)
                gn_ref[...] = norm_grad[0:8]
            for f in range(n):
                slot = places.slot_to(me_ref, f)
                for k, grad in enumerate((gq, gk, gv)):
                    low = grad[f * r : f * r + h].astype(BF16)
                    high = grad[f * r + h : (f + 1) * r].astype(BF16)
                    keep_ref[slot, k * h : (k + 1) * h, :] = jnp.where(lower, low, high)
                    send_ref[slot, k * h : (k + 1) * h, :] = jnp.where(lower, high, low)
                if last:
                    piece = norm_grad[:, f * r : (f + 1) * r].astype(BF16)
                    keep_ref[slot, 3 * h :, :] = jnp.zeros((NORM_ROWS, PAIR), BF16)
                    send_ref[slot, 3 * h :, :] = jnp.zeros((NORM_ROWS, PAIR), BF16)
                    keep_ref[slot, 3 * h :, 0:r] = piece
                    send_ref[slot, 3 * h :, 0:r] = piece

    count = xhat.shape[1]
    wire = (n, m, PAIR)
    return call(
        kernel,
        me,
        (steps,),
        [
            (xhat, (D, rows), lambda i: (0, i)),
            (memory_t, (D, step_spans * MEM), lambda i: (0, i)),
            (left_keys, *rows_of((step_spans * LEFT, PAIR), pair)),
            (left_values, *rows_of((step_spans * LEFT, PAIR), pair)),
            (qkv, *rows_of((rows, 3 * PAIR))),
            (kvm, *rows_of((step_spans * MEM, 2 * PAIR))),
            (probs, *rows_of((2 * rows, KPAD))),
            (grad_att, *rows_of((rows, PAIR), pair)),
            (weights, (1, D, 3 * PAIR), lambda i: (side, 0, 0)),
            (norm, *whole((8, D))),
        ]
        + [(a, *whole((8, D))) for a in parts],
        [
            ((count, 3 * PAIR), BF16, *rows_of((rows, 3 * PAIR))),
            (wire, BF16, *whole(wire)),
            (wire, BF16, *whole(wire)),
            ((8, D), F32, *whole((8, D))),
        ],
        [pltpu.VMEM((groups, KPAD, PAIR), BF16)] * 2
        + [
            pltpu.VMEM((step_spans * MEM, 2 * PAIR), BF16),
            pltpu.VMEM((D, 3 * PAIR), F32),
            pltpu.VMEM((D, 2 * PAIR), F32),
            pltpu.VMEM((8, 3 * PAIR), F32),
        ],
        f"attention_backward_{pair}",
        flops=2 * count * D * 3 * PAIR * 8,
        moved=2 * (count * D * 2 + spans * LEFT * PAIR * 2 + spans * QROWS // 2 * KPAD),
    )


def frames_gradient(me, frames, grad_residual, grads, weights, norm, part, before):
    count = frames.shape[0]
    rows = 256
    steps = count // rows // 2
    start = part * steps

    def kernel(me_ref, fr_ref, res_ref, d0, d1, d2, d3, w0_ref, w1_ref, norm_ref, *rest):
        out_ref = rest[-1]
        d = jnp.concatenate([d0[...], d1[...], d2[...], d3[...]], axis=1)
        w = jnp.concatenate([w0_ref[0], w0_ref[1], w1_ref[0], w1_ref[1]], axis=1)
        grad = dot_last(d, w)
        xhat, scale = normalize(fr_ref[...].astype(F32))
        out_ref[...] = res_ref[...] + norm_back(grad, xhat, scale, norm_ref[0:1, :])

    def block(shape):
        return shape, lambda i: (start + i, 0)

    ins = [(frames, *block((rows, D))), (grad_residual, *block((rows, D)))]
    ins += [(d, *block((rows, 3 * PAIR))) for d in grads]
    ins += [(w, *whole((2, D, 3 * PAIR))) for w in weights]
    ins += [(norm, *whole((8, D)))]
    if part:
        ins += [(before, None, None)]
    (out,) = call(
        kernel,
        me,
        (steps,),
        ins,
        [((count, D), F32, *block((rows, D)))],
        [],
        f"frames_gradient_{part}",
        flops=count * D * 3 * D,
        moved=count * D * 8,
        aliases={len(ins): 0} if part else None,
    )
    return out


def after(value, *others):
    return lax.optimization_barrier((value, *others))[0]


def add(a, b):
    return a.astype(F32) + b.astype(F32)


def update_ffn(me, up, down, ffn_in, ffn_in_m, ffn_in_v, ffn_out, ffn_out_m, ffn_out_v, places):
    r, r2 = D // places.n, FF // places.n
    half = FF // 2

    def kernel(me_ref, up_ref, other_up_ref, down_ref, other_down_ref, wi, mi, vi, wo, mo, vo, *outs):
        lower = me_ref[2] == 0

        def halves(mine, sib):
            return jnp.where(lower, mine, sib).astype(F32), jnp.where(lower, sib, mine).astype(F32)

        def put(refs, at, grad, w, m, v, rate):
            g_ref, f_ref, s_ref, n_ref, c_ref = refs
            first, second, new = adamw(w[:, at], grad, m[:, at], v[:, at], rate)
            g_ref[:, at] = grad
            f_ref[:, at] = first
            s_ref[:, at] = second
            n_ref[:, at] = new
            c_ref[:, at] = new.astype(BF16)

        low, high = halves(up_ref[...], other_up_ref[...])
        for k in range(4):
            for base, part in ((0, low), (half, high)):
                at = slice(base + k * HALF, base + (k + 1) * HALF)
                put(outs[:5], at, part[k * r : (k + 1) * r], wi, mi, vi, RATE_FFN_IN)
        low, high = halves(down_ref[:r2, :], other_down_ref[:r2, :])
        for at, part in ((slice(0, HALF), low), (slice(HALF, D), high)):
            put(outs[5:], at, part, wo, mo, vo, RATE_FFN_OUT)

    si, so = (r, FF), (r2, D)
    return call(
        kernel,
        me,
        (1,),
        [(a, *whole(a.shape)) for a in (*up, *down, ffn_in, ffn_in_m, ffn_in_v, ffn_out, ffn_out_m, ffn_out_v)],
        [(s, t, *whole(s)) for s in (si, so) for t in (F32, F32, F32, F32, BF16)],
        [],
        "update_ffn",
        moved=4 * 8 * (r * FF + r2 * D),
    )


def update_attention(me, down, halves_sums, attn_w, attn_m, attn_v, norm_params, norm_m, norm_v, places):
    r, r2 = D // places.n, FF // places.n
    h = r // 2
    sums = [*down, *halves_sums[0], *halves_sums[1]]

    def kernel(me_ref, *refs):
        sum_refs = refs[: len(sums)]
        w, m, v, nw, nm, nv = refs[len(sums) : len(sums) + 6]
        outs = refs[len(sums) + 6 : len(sums) + 11]
        norm_outs = refs[len(sums) + 11 :]
        lower = me_ref[2] == 0

        def put(k, at, columns, grad):
            rate = RATES_ATTENTION[k]
            first, second, new = adamw(w[k, at, columns], grad, m[k, at, columns], v[k, at, columns], rate)
            for ref, value in zip(outs, (grad, first, second, new, new.astype(BF16))):
                ref[k, at, columns] = value

        def halves(index, at):
            mine, sib = sum_refs[index][at, :], sum_refs[index + 1][at, :]
            low = jnp.where(lower, mine, sib).astype(F32)
            return low, jnp.where(lower, sib, mine).astype(F32)

        low, high = halves(0, slice(r2, r2 + r))
        put(3, slice(0, r), slice(0, HALF), low)
        put(3, slice(0, r), slice(HALF, D), high)
        for p in range(4):
            columns = slice(p * PAIR, (p + 1) * PAIR)
            for k in range(3):
                at = (p % 2) * 3 * h + k * h
                low, high = halves(2 + 2 * (p // 2), slice(at, at + h))
                put(k, slice(0, h), columns, low)
                put(k, slice(h, r), columns, high)
        grad = sum_refs[4][6 * h :, :].astype(F32)[0:4, 0:r]
        first, second, new = adamw(nw[...], grad, nm[...], nv[...], RATE_NORM)
        for ref, value in zip(norm_outs, (grad, first, second, new, new.astype(BF16))):
            ref[...] = value

    shape, small = (4, r, D), (4, r)
    ins = (*sums, attn_w, attn_m, attn_v, norm_params, norm_m, norm_v)
    return call(
        kernel,
        me,
        (1,),
        [(a, *whole(a.shape)) for a in ins],
        [(s, t, *whole(s)) for s in (shape, small) for t in (F32, F32, F32, F32, BF16)],
        [],
        "update_attention",
        moved=4 * 8 * 4 * r * D,
    )


def shards(
    places,
    frames,
    memory,
    left_keys,
    left_values,
    lengths,
    cotangent,
    attn_w,
    ffn_in,
    ffn_out,
    norm_params,
    attn_m,
    attn_v,
    ffn_in_m,
    ffn_in_v,
    ffn_out_m,
    ffn_out_v,
    norm_m,
    norm_v,
):
    X, Z = places.X, places.Z
    tie = lax.optimization_barrier
    me = places.me()
    bias = length_bias(lengths)
    masks = jnp.asarray(span_masks())

    def direct(value):
        return [
            value if dx == dz == 0 else places.shift(value, dz, dx)
            for dx in range(X)
            for dz in range(Z)
        ]

    def along_z(value):
        return [value if dz == 0 else places.shift(value, dz, 0) for dz in range(Z)]

    def along_x(value):
        return [value if dx == 0 else places.shift(value, 0, dx) for dx in range(X)]

    first_wire = pack_first(me, attn_w, norm_params, places)
    second_wire, up_wire, down_wire = pack_rest(me, attn_w, ffn_in, ffn_out, places)
    first = direct(first_wire)
    second_wire, *first = tie((second_wire, *first))
    second = direct(second_wire)
    first = jnp.stack(first)
    weights = first, places.other_core(first)

    def forward(token, pair, x, weights):
        return attention_forward(
            token, pair, x, memory, left_keys, left_values, bias, masks, weights, places
        )

    qkv0, kvm0, att0, p0, w_low, hidden, xhat, memory_t, norm = forward(me, 0, frames, weights)
    me, up_wire, att0, *second = tie((me, up_wire, att0, *second))
    second = jnp.stack(second)
    weights = second, places.other_core(second)
    up = along_z(up_wire)
    qkv1, kvm1, att1, p1 = forward(me, 1, hidden, w_low)
    me, down_wire, att1, *up = tie((me, down_wire, att1, *up))
    up = along_x(jnp.stack(up))
    down = along_z(down_wire)
    qkv2, kvm2, att2, p2, w_high = forward(me, 2, hidden, weights)
    me, att2, up, down = tie((me, att2, up, down))
    up = up, [places.other_core(part) for part in up]
    down = along_x(jnp.stack(down))
    qkv3, kvm3, att3, p3 = forward(me, 3, hidden, w_high)
    down = down, [places.other_core(part) for part in down]
    output, grad_residual, grad_att, norm_two, keep_up, send_up, keep_down, send_down = feed_forward(
        me, (att0, att1, att2, att3), frames, cotangent, norm, up, down, places
    )

    def backward(token, pair, saved, norm_parts=None):
        return attention_backward(
            token, pair, xhat, memory_t, left_keys, left_values, saved, grad_att, norm, norm_parts, places
        )

    def split(total):
        return total.reshape((X, Z) + total.shape[1:])

    def send_x(total):
        return [places.shift(total[dx].astype(BF16), 0, dx) for dx in range(1, X)]

    def send_z(column):
        return [places.shift(column[dz].astype(BF16), dz, 0) for dz in range(1, Z)]

    def collect(mine, got):
        for part in got:
            mine = add(mine, part)
        return mine

    got_up, got_down = places.other_core(send_up), places.other_core(send_down)
    d0, keep0, send0, n0 = backward(me, 0, (qkv0, kvm0, p0, w_low))
    me, got_up, got_down, d0 = tie((me, got_up, got_down, d0))
    up, down = split(add(keep_up, got_up)), split(add(keep_down, got_down))
    got_up = send_x(up)
    d1, keep1, send1, n1 = backward(me, 1, (qkv1, kvm1, p1, w_low))
    me, down, d1, *got_up = tie((me, down, d1, *got_up))
    up = collect(up[0], got_up)
    got_up, got_down = send_z(up), send_x(down)
    keep01, send01 = jnp.concatenate([keep0, keep1], axis=1), jnp.concatenate([send0, send1], axis=1)
    got01 = places.other_core(send01)
    d2, keep2, send2, n2 = backward(me, 2, (qkv2, kvm2, p2, w_high))
    me, d2, got01, got_up, got_down = tie((me, d2, got01, got_up, got_down))
    up, down = collect(up[0], got_up).astype(BF16), collect(down[0], got_down)
    got_down = send_z(down)
    sum01 = split(add(keep01, got01))
    got01 = send_x(sum01)
    up = places.sum_over_y(up)
    got2 = places.other_core(send2)
    d3, keep3, send3, n3 = backward(me, 3, (qkv3, kvm3, p3, w_high), [norm_two, n0, n1, n2])
    me, d3, got2, got01, got_down, up = tie((me, d3, got2, got01, got_down, up))
    got3 = places.other_core(send3)
    down = collect(down[0], got_down).astype(BF16)
    down = places.sum_over_y(down)
    up = up, places.other_core(up)
    sum01 = collect(sum01[0], got01)
    got01 = send_z(sum01)
    sum23 = split(jnp.concatenate([add(keep2, got2), add(keep3, got3)], axis=1))
    got23 = send_x(sum23)
    frames_part = functools.partial(
        frames_gradient, frames=frames, grad_residual=grad_residual, grads=(d0, d1, d2, d3),
        weights=(w_low, w_high), norm=norm,
    )
    input_grad = frames_part(me, part=0, before=None)
    me, input_grad, down, up, got01, got23 = tie((me, input_grad, down, up, got01, got23))
    down = down, places.other_core(down)
    sum23 = collect(sum23[0], got23)
    got23 = send_z(sum23)
    sum01 = places.sum_over_y(collect(sum01[0], got01).astype(BF16))
    input_grad = frames_part(me, part=1, before=input_grad)
    me, input_grad, sum01, got23, down = tie((me, input_grad, sum01, got23, down))
    sum23 = places.sum_over_y(collect(sum23[0], got23).astype(BF16))
    sum01 = sum01, places.other_core(sum01)
    ffn = update_ffn(me, up, down, ffn_in, ffn_in_m, ffn_in_v, ffn_out, ffn_out_m, ffn_out_v, places)
    sum23 = sum23, places.other_core(sum23)
    attention = update_attention(
        me, down, (sum01, sum23), attn_w, attn_m, attn_v, norm_params, norm_m, norm_v, places
    )
    return (output, input_grad, *attention[:5], *ffn, *attention[5:])


def solution(mesh):
    rows = P(("dp", "fsdp"), None)
    attn, ffn, norm = P(None, "fsdp", None), P("fsdp", None), P(None, "fsdp")
    return jax.shard_map(
        functools.partial(shards, Places(mesh)),
        mesh=mesh,
        in_specs=(rows,) * 4
        + (P(("dp", "fsdp")), rows, attn, ffn, ffn, norm)
        + (attn, attn, ffn, ffn, ffn, ffn, norm, norm),
        out_specs=(rows, rows) + (attn,) * 5 + (ffn,) * 10 + (norm,) * 5,
        check_vma=False,
    )
```

```python
import functools
import math

import jax
import jax.numpy as jnp
import numpy as np
from jax import lax
from jax.experimental import pallas as pl
from jax.experimental.pallas import tpu as pltpu
from jax.sharding import PartitionSpec as P

D = 512
FF = 2048
HEADS = 8
SEG = 16
LEFT = 30
MEM = 4
STEP = 5
ROWS_SPAN = 20
GROUP = 4
QROWS = GROUP * ROWS_SPAN
MROWS = GROUP * MEM
LROWS = GROUP * LEFT
LWIN = 128
KPAD = 256
HALF = 256
PAIR = 128
NORM_ROWS = 16

F32 = jnp.float32
BF16 = jnp.bfloat16
BLOCKED = -1e9
EPS_NORM = 1e-05
BETA_FIRST = 0.5
BETA_SECOND = 0.5
WEIGHT_DECAY = 0.01
EPS_ADAM = 1e-08
RATES_ATTENTION = (0.04, 0.04, 0.04, 0.25)
RATE_FFN_IN = 0.04
RATE_FFN_OUT = 0.02
RATE_NORM = 0.2
VMEM_LIMIT = 56 * 2**20


def dot(a, b):
    return lax.dot_general(a, b, (((1,), (0,)), ((), ())), preferred_element_type=F32)


def dot_last(a, b):
    return lax.dot_general(a, b, (((1,), (1,)), ((), ())), preferred_element_type=F32)


def dot_rows(a, b):
    return lax.dot_general(a, b, (((0,), (0,)), ((), ())), preferred_element_type=F32)


def normalize(x):
    mean = jnp.mean(x, axis=1, keepdims=True)
    centred = x - mean
    variance = jnp.mean(centred * centred, axis=1, keepdims=True)
    scale = lax.rsqrt(variance + EPS_NORM)
    return centred * scale, scale


def norm_back(grad, normed, scale, gain):
    grad = grad * gain
    first = jnp.mean(grad, axis=1, keepdims=True)
    second = jnp.mean(grad * normed, axis=1, keepdims=True)
    return scale * (grad - first - normed * second)


def gelu_parts(x):
    c = math.sqrt(2.0 / math.pi)
    square = x * x
    t = jnp.tanh(x * (c + (c * 0.044715) * square))
    half = 0.5 * x
    value = half + half * t
    slope = 0.5 + 0.5 * t + half * (1.0 - t * t) * (c + (3.0 * c * 0.044715) * square)
    return value, slope


def spread_pair(x):
    lane = lax.broadcasted_iota(jnp.int32, x.shape, 1)
    zero = jnp.zeros_like(x)
    return jnp.concatenate([jnp.where(lane < 64, x, zero), jnp.where(lane < 64, zero, x)], axis=0)


def join_pair(x):
    rows = x.shape[0] // 2
    lane = lax.broadcasted_iota(jnp.int32, (rows, PAIR), 1)
    return jnp.where(lane < 64, x[:rows], x[rows:])


def left_start(g):
    return LROWS * g - (8 if g % 2 else 0)


def span_masks():
    query_span = np.arange(2 * QROWS) % QROWS // ROWS_SPAN
    masks = np.full((2, 2 * QROWS, KPAD), BLOCKED, np.float32)
    for odd in range(2):
        span = np.full(KPAD, -1)
        span[:MROWS] = np.arange(MROWS) // MEM
        span[MROWS : MROWS + QROWS] = np.arange(QROWS) // ROWS_SPAN
        start = MROWS + QROWS + (8 if odd else 0)
        span[start : start + LROWS] = np.arange(LROWS) // LEFT
        masks[odd][query_span[:, None] == span[None, :]] = 0.0
    return masks


def length_bias(lengths):
    groups = lengths.shape[0] // GROUP
    key = np.arange(KPAD)
    is_frame = (key >= MROWS) & (key < MROWS + QROWS)
    place = np.where(is_frame, (key - MROWS) % ROWS_SPAN, 0)
    span = np.where(is_frame, (key - MROWS) // ROWS_SPAN, 0)
    own = lengths.reshape(groups, GROUP)
    length = jnp.zeros((groups, KPAD), jnp.int32)
    for s in range(GROUP):
        length = jnp.where(jnp.asarray(span == s)[None, :], own[:, s : s + 1], length)
    dead = jnp.asarray(is_frame & (place < SEG))[None, :] & (jnp.asarray(place)[None, :] >= length)
    return jnp.where(dead, BLOCKED, 0.0).astype(F32).reshape(groups, 1, KPAD)


def adamw(weight, grad, first_old, second_old, rate):
    first = BETA_FIRST * first_old + (1.0 - BETA_FIRST) * grad
    second = BETA_SECOND * second_old + (1.0 - BETA_SECOND) * grad * grad
    first_hat = first / (1.0 - BETA_FIRST**STEP)
    second_hat = second / (1.0 - BETA_SECOND**STEP)
    new = weight - rate * (first_hat / (jnp.sqrt(second_hat) + EPS_ADAM) + WEIGHT_DECAY * weight)
    return first, second, new


class Places:
    def __init__(self, mesh):
        self.n = mesh.shape["fsdp"]
        self.dp = mesh.shape["dp"]
        power = max(int(math.log2(self.n)) - 1, 0) // 2
        self.X = 2**power
        self.Z = self.n // self.X
        self.C = 2
        self.Y = self.dp // self.C

    def me(self):
        f = lax.axis_index("fsdp")
        d = lax.axis_index("dp")
        return jnp.stack([f // self.X, f % self.X, d % self.C, d // self.C]).astype(jnp.int32)

    def slot_to(self, me_ref, f):
        dz = lax.rem(f // self.X + self.Z - me_ref[0], self.Z)
        dx = lax.rem(f % self.X + self.X - me_ref[1], self.X)
        return dx * self.Z + dz

    def slot_from(self, me_ref, f):
        dz = lax.rem(me_ref[0] + self.Z - f // self.X, self.Z)
        dx = lax.rem(me_ref[1] + self.X - f % self.X, self.X)
        return dx * self.Z + dz

    def shift(self, value, dz, dx):
        X, Z = self.X, self.Z
        perm = [
            (z * X + x, (z + dz) % Z * X + (x + dx) % X) for z in range(Z) for x in range(X)
        ]
        return lax.ppermute(value, "fsdp", perm)

    def y_joined(self, me_ref, ref):
        slots = [lax.rem(me_ref[3] + self.Y - y, self.Y) for y in range(self.Y)]
        return jnp.concatenate([ref[slot] for slot in slots], axis=0)

    def y_slot_to(self, me_ref, y):
        return lax.rem(y + self.Y - me_ref[3], self.Y)

    def shift_y(self, value, dy):
        dp = self.dp
        return lax.ppermute(value, "dp", [(d, (d + 2 * dy) % dp) for d in range(dp)])

    def other_core(self, value):
        return lax.ppermute(value, "dp", [(d, d ^ 1) for d in range(self.dp)])

    def sum_over_y(self, value):
        step = 1
        while step < self.Y:
            got = lax.ppermute(value, "dp", [(d, d ^ (2 * step)) for d in range(self.dp)])
            value = (value.astype(F32) + got.astype(F32)).astype(BF16)
            step *= 2
        return value


def call(kernel, me, grid, ins, outs, scratch, name, flops=0, moved=0, aliases=None):
    def spec(block, index):
        if block is None:
            return pl.BlockSpec(memory_space=pl.ANY)
        return pl.BlockSpec(block, lambda *a: index(*a[:-1]))

    return pl.pallas_call(
        kernel,
        grid_spec=pltpu.PrefetchScalarGridSpec(
            num_scalar_prefetch=1,
            grid=grid,
            in_specs=[spec(b, f) for _, b, f in ins],
            out_specs=[spec(b, f) for _, _, b, f in outs],
            scratch_shapes=scratch,
        ),
        out_shape=[jax.ShapeDtypeStruct(s, d) for s, d, _, _ in outs],
        compiler_params=pltpu.CompilerParams(vmem_limit_bytes=VMEM_LIMIT),
        cost_estimate=pl.CostEstimate(flops=flops, bytes_accessed=moved, transcendentals=0),
        input_output_aliases=aliases or {},
        name=name,
    )(me, *[a for a, _, _ in ins])


def whole(shape):
    return shape, lambda i: (0,) * len(shape)


def rows_of(shape, column=0):
    return shape, lambda i: (i, column)


def pack_first(me, attn_w, norm_params, places):
    r = D // places.n
    h = r // 2

    def kernel(me_ref, w_ref, n_ref, out_ref, scratch):
        lower = me_ref[2] == 0
        for k in range(3):
            w = w_ref[k]
            out_ref[k * h : (k + 1) * h, :] = jnp.where(lower, w[:h], w[h:]).astype(BF16)
        scratch[...] = jnp.zeros_like(scratch)
        scratch[0:4, 0:r] = n_ref[...]
        out_ref[3 * h :, :] = scratch[...].astype(BF16)

    (out,) = call(
        kernel,
        me,
        (1,),
        [
            (attn_w, (3, r, HALF), lambda i: (0, 0, 0)),
            (norm_params, *whole((4, r))),
        ],
        [((3 * h + NORM_ROWS, HALF), BF16, *whole((3 * h + NORM_ROWS, HALF)))],
        [pltpu.VMEM((NORM_ROWS, HALF), F32)],
        "pack_first",
        moved=4 * 3 * r * HALF,
    )
    return out


def pack_rest(me, attn_w, ffn_in, ffn_out, places):
    r, r2 = D // places.n, FF // places.n
    h, q = r // 2, r2 // places.dp

    def kernel(me_ref, w_ref, in_ref, out_w_ref, second_ref, up_ref):
        lower = me_ref[2] == 0
        for k in range(3):
            w = w_ref[k, :, HALF:]
            second_ref[k * h : (k + 1) * h, :] = jnp.where(lower, w[:h], w[h:]).astype(BF16)
        member = me_ref[3] * 2 + me_ref[2]
        w = out_w_ref[pl.ds(pl.multiple_of(member * q, q), q), :].astype(BF16)
        second_ref[3 * h : 3 * h + q, :] = w[:, :HALF]
        second_ref[3 * h + q :, :] = w[:, HALF:]
        half = FF // 2
        for k in range(4):
            up_ref[k * r : (k + 1) * r, :] = jnp.where(
                lower,
                in_ref[:, k * HALF : (k + 1) * HALF],
                in_ref[:, half + k * HALF : half + (k + 1) * HALF],
            ).astype(BF16)
        w = w_ref[3]
        up_ref[4 * r :, :] = jnp.where(lower, w[:, :HALF], w[:, HALF:]).astype(BF16)

    shapes = (3 * h + 2 * q, HALF), (5 * r, HALF)
    return call(
        kernel,
        me,
        (1,),
        [
            (attn_w, *whole((4, r, D))),
            (ffn_in, *whole((r, FF))),
            (ffn_out, *whole((r2, D))),
        ],
        [(shape, BF16, *whole(shape)) for shape in shapes],
        [],
        "pack_rest",
        moved=4 * (4 * r * D + r * FF + r2 * D),
    )


def attention_forward(me, half, x, memory, left_keys, left_values, bias, masks, own, other, places):
    first = half == 0
    spans = memory.shape[0] // MEM
    step_spans = 32 if spans % 32 == 0 else 16
    groups = step_spans // GROUP
    rows = step_spans * ROWS_SPAN
    n, r = places.n, D // places.n
    h = r // 2

    def kernel(me_ref, x_ref, mem_ref, lk_ref, lv_ref, bias_ref, mask_ref, own_ref, other_ref, *rest):
        qkv_ref, kvm_ref, att_ref, p_ref, w_ref, *rest = rest
        if first:
            hid_ref, xhat_ref, memt_ref, norm_ref, *rest = rest
        ks, vs = rest

        @pl.when(pl.program_id(0) == 0)
        def _():
            ks[...] = jnp.zeros_like(ks)
            vs[...] = jnp.zeros_like(vs)
            lower = me_ref[2] == 0
            if first:
                norm_ref[...] = jnp.zeros_like(norm_ref)
            for f in range(n):
                slot = places.slot_from(me_ref, f)
                mine, sib = own_ref[slot], other_ref[slot]
                for at, part in (
                    (slice(f * r, f * r + h), jnp.where(lower, mine, sib)),
                    (slice(f * r + h, (f + 1) * r), jnp.where(lower, sib, mine)),
                ):
                    for k in range(3):
                        w_ref[at, k * HALF : (k + 1) * HALF] = part[k * h : (k + 1) * h]
                if first:
                    tail = mine[3 * h :, :].astype(F32)
                    norm_ref[:, f * r : (f + 1) * r] = tail[0:8, 0:r]

        w = w_ref[...]
        if first:
            xhat, _ = normalize(x_ref[...].astype(F32))
            xhat_ref[...] = xhat.astype(BF16).T
            memt_ref[...] = mem_ref[...].T
            hidden = (xhat * norm_ref[0:1, :] + norm_ref[1:2, :]).astype(BF16)
            hid_ref[...] = hidden
        else:
            hidden = x_ref[...]
        qkv = dot(hidden, w).astype(BF16)
        query = qkv[:, :HALF] * jnp.asarray(0.125, BF16)
        qkv_ref[:, :HALF] = query
        qkv_ref[:, HALF:] = qkv[:, HALF:]
        kvm = dot(mem_ref[...], w[:, HALF:]).astype(BF16)
        kvm_ref[...] = kvm
        for g in range(groups):
            ls = left_start(g)
            for dest, low, src in ((ks, 0, lk_ref), (vs, HALF, lv_ref)):
                dest[g, 0:MROWS, :] = kvm[MROWS * g : MROWS * (g + 1), low : low + HALF]
                dest[g, MROWS : MROWS + QROWS, :] = qkv[
                    QROWS * g : QROWS * (g + 1), HALF + low : 2 * HALF + low
                ]
                dest[g, MROWS + QROWS : MROWS + QROWS + LWIN, :] = src[ls : ls + LWIN, :]
        for g0 in range(0, groups, 4):
            work = {}
            units = [(g, p) for g in range(g0, g0 + 4) for p in range(2)]
            for g, p in units:
                s = slice(p * PAIR, (p + 1) * PAIR)
                work[g, p] = dot_last(spread_pair(query[QROWS * g : QROWS * (g + 1), s]), ks[g, :, s])
            for g, p in units:
                scores = work[g, p] + (mask_ref[g % 2] + bias_ref[g])
                work[g, p] = jnp.exp(scores - jnp.max(scores, axis=1, keepdims=True))
            for g, p in units:
                s = slice(p * PAIR, (p + 1) * PAIR)
                e = work[g, p]
                right = jnp.concatenate([vs[g, :, s], jnp.ones((KPAD, PAIR), BF16)], axis=1)
                work[g, p] = e, dot(e.astype(BF16), right)
            for g, p in units:
                s = slice(p * PAIR, (p + 1) * PAIR)
                e, mixed = work[g, p]
                scale = 1.0 / mixed[:, PAIR:]
                at = slice(2 * QROWS * g, 2 * QROWS * (g + 1))
                p_ref[p, at, :PAIR] = (e[:, :PAIR] * scale).astype(BF16)
                p_ref[p, at, PAIR:] = (e[:, PAIR:] * scale).astype(BF16)
                att_ref[QROWS * g : QROWS * (g + 1), s] = join_pair(mixed[:, :PAIR] * scale).astype(BF16)

    count = x.shape[0]
    wide = 3 * HALF
    ins = [
        (x, *rows_of((rows, D))),
        (memory, *rows_of((step_spans * MEM, D))),
        (left_keys, *rows_of((step_spans * LEFT, HALF), half)),
        (left_values, *rows_of((step_spans * LEFT, HALF), half)),
        (bias, (groups, 1, KPAD), lambda i: (i, 0, 0)),
        (masks, *whole((2, 2 * QROWS, KPAD))),
        (own, *whole(own.shape)),
        (other, *whole(other.shape)),
    ]
    outs = [
        ((count, wide), BF16, *rows_of((rows, wide))),
        ((spans * MEM, 2 * HALF), BF16, *rows_of((step_spans * MEM, 2 * HALF))),
        ((count, HALF), BF16, *rows_of((rows, HALF))),
        ((2, 2 * count, KPAD), BF16, (2, 2 * rows, KPAD), lambda i: (0, i, 0)),
        ((D, wide), BF16, *whole((D, wide))),
    ]
    if first:
        columns = lambda i: (0, i)
        outs += [
            ((count, D), BF16, *rows_of((rows, D))),
            ((D, count), BF16, (D, rows), columns),
            ((D, spans * MEM), BF16, (D, step_spans * MEM), columns),
            ((8, D), F32, *whole((8, D))),
        ]
    return call(
        kernel,
        me,
        (spans // step_spans,),
        ins,
        outs,
        [pltpu.VMEM((groups, KPAD, HALF), BF16)] * 2,
        f"attention_forward_{half}",
        flops=2 * count * D * wide * 4,
        moved=2 * (count * D * 3 + spans * LEFT * D + spans * 4 * ROWS_SPAN * KPAD),
    )


def feed_forward(me, attended_halves, frames, cotangent, norm, up, down, places):
    count = frames.shape[0]
    rows = 512
    steps = count // rows
    chunk = 256
    n, r, r2 = places.n, D // places.n, FF // places.n
    X, Y, Z = places.X, places.Y, places.Z
    q, part_rows = r2 // places.dp, (r + r2) // Y

    def kernel(me_ref, a0, a1, fr_ref, cot_ref, norm_ref, *rest):
        up_refs, other_up_refs, rest = rest[:X], rest[X : 2 * X], rest[2 * X :]
        down_refs, other_down_refs, rest = rest[:Y], rest[Y : 2 * Y], rest[2 * Y :]
        out_ref, res_ref, gatt_ref, gn_ref, keep_up, send_up, keep_down, send_down, *rest = rest
        w1, w2, wo, acc1, acc2, acco = rest
        i = pl.program_id(0)
        lower = me_ref[2] == 0

        @pl.when(i == 0)
        def _():
            acc1[...] = jnp.zeros_like(acc1)
            acc2[...] = jnp.zeros_like(acc2)
            acco[...] = jnp.zeros_like(acco)
            gn_ref[...] = jnp.zeros_like(gn_ref)
            for dx in range(X):
                xx = lax.rem(me_ref[1] + X - dx, X)
                for dz in range(Z):
                    zz = lax.rem(me_ref[0] + Z - dz, Z)
                    f = zz * X + xx

                    def halves(mine, sib):
                        return jnp.where(lower, mine, sib), jnp.where(lower, sib, mine)

                    low, high = halves(up_refs[dx][dz], other_up_refs[dx][dz])
                    at = pl.ds(pl.multiple_of(f * r, r), r)
                    for k in range(4):
                        w1[at, k * HALF : (k + 1) * HALF] = low[k * r : (k + 1) * r]
                        w1[at, FF // 2 + k * HALF : FF // 2 + (k + 1) * HALF] = high[k * r : (k + 1) * r]
                    wo[at, :HALF] = low[4 * r :]
                    wo[at, HALF:] = high[4 * r :]
                    for dy in range(Y):
                        yy = lax.rem(me_ref[3] + Y - dy, Y)
                        for core, part in enumerate(
                            halves(down_refs[dy][dx, dz], other_down_refs[dy][dx, dz])
                        ):
                            at = pl.ds(pl.multiple_of(f * r2 + (yy * 2 + core) * q, q), q)
                            w2[at, :HALF] = part[:q]
                            w2[at, HALF:] = part[q:]

        attended = jnp.concatenate([a0[...], a1[...]], axis=1)
        residual = fr_ref[...].astype(F32) + dot(attended, wo[...])
        normed, scale = normalize(residual)
        gain = norm_ref[2:3, :]
        hidden = (normed * gain + norm_ref[3:4, :]).astype(BF16)
        cot = cot_ref[...]
        output = residual
        grad = None
        slices = [slice(j * chunk, (j + 1) * chunk) for j in range(FF // chunk)]
        late = None
        for j, s in enumerate(slices):
            inner, grad_act = dot(hidden, w1[:, s]), dot_last(cot, w2[s, :])
            if late is not None:
                u, active, grad_inner = late
                output = output + dot(active, w2[u, :])
                part = dot_last(grad_inner, w1[:, u])
                grad = part if grad is None else grad + part
                acc1[:, u] += dot_rows(hidden, grad_inner)
                acc2[:, u] += dot_rows(cot, active)
            value, slope = gelu_parts(inner)
            late = s, value.astype(BF16), (grad_act * slope).astype(BF16)
        u, active, grad_inner = late
        output = output + dot(active, w2[u, :])
        grad = grad + dot_last(grad_inner, w1[:, u])
        acc1[:, u] += dot_rows(hidden, grad_inner)
        acc2[:, u] += dot_rows(cot, active)
        out_ref[...] = output.astype(BF16)
        gn_ref[0:1, :] += jnp.sum(grad * normed, axis=0, keepdims=True)
        gn_ref[1:2, :] += jnp.sum(grad, axis=0, keepdims=True)
        grad_residual = cot.astype(F32) + norm_back(grad, normed, scale, gain)
        res_ref[...] = grad_residual
        grad_low = grad_residual.astype(BF16)
        gatt_ref[...] = dot_last(grad_low, wo[...]).astype(BF16)
        acco[...] += dot_rows(attended, grad_low)

        @pl.when(i == steps - 1)
        def _():
            for f in range(n):
                slot = places.slot_to(me_ref, f)

                def sides(low, high):
                    low, high = low.astype(BF16), high.astype(BF16)
                    return jnp.where(lower, low, high), jnp.where(lower, high, low)

                here = slice(f * r, (f + 1) * r)
                for k in range(4):
                    at = slice(k * r, (k + 1) * r)
                    keep_up[slot, at, :], send_up[slot, at, :] = sides(
                        acc1[here, k * HALF : (k + 1) * HALF],
                        acc1[here, FF // 2 + k * HALF : FF // 2 + (k + 1) * HALF],
                    )
                turned = acc2[:, f * r2 : (f + 1) * r2].T
                low = jnp.concatenate([acco[here, :HALF], turned[:, :HALF]], axis=0)
                high = jnp.concatenate([acco[here, HALF:], turned[:, HALF:]], axis=0)
                for y in range(Y):
                    at = slice(y * part_rows, (y + 1) * part_rows)
                    to = places.y_slot_to(me_ref, y)
                    keep_down[to, slot], send_down[to, slot] = sides(low[at], high[at])

    wires = [(n, 4 * r, HALF)] * 2 + [(Y, n, part_rows, HALF)] * 2
    return call(
        kernel,
        me,
        (steps,),
        [(a, *rows_of((rows, HALF))) for a in attended_halves]
        + [
            (frames, *rows_of((rows, D))),
            (cotangent, *rows_of((rows, D))),
            (norm, *whole((8, D))),
        ]
        + [(a, *whole(a.shape)) for a in (*up[0], *up[1], *down[0], *down[1])],
        [
            ((count, D), BF16, *rows_of((rows, D))),
            ((count, D), F32, *rows_of((rows, D))),
            ((count, D), BF16, *rows_of((rows, D))),
            ((8, D), F32, *whole((8, D))),
        ]
        + [(wire, BF16, *whole(wire)) for wire in wires],
        [
            pltpu.VMEM((D, FF), BF16),
            pltpu.VMEM((FF, D), BF16),
            pltpu.VMEM((D, D), BF16),
            pltpu.VMEM((D, FF), F32),
            pltpu.VMEM((D, FF), F32),
            pltpu.VMEM((D, D), F32),
        ],
        "feed_forward",
        flops=2 * count * D * (6 * FF + 3 * D) * 2,
        moved=2 * count * D * 8,
    )


def attention_backward(me, half, xhat, memory_t, left_keys, left_values, saved, grad_att, norm, norm_parts, places):
    last = norm_parts is not None
    qkv, kvm, probs, weights, attended = saved
    spans = memory_t.shape[1] // MEM
    step_spans = 32 if spans % 32 == 0 else 16
    steps = spans // step_spans
    groups = step_spans // GROUP
    rows = step_spans * ROWS_SPAN
    n, r = places.n, D // places.n
    h = r // 2
    m = 3 * h + (NORM_ROWS if last else 0)
    wide = 3 * HALF
    parts = norm_parts if last else []

    def kernel(me_ref, xhat_ref, mem_ref, lk_ref, lv_ref, qkv_ref, kvm_ref, p_ref, da_ref, att_ref, w_ref, norm_ref, *rest):
        part_refs = rest[: len(parts)]
        d_ref, keep_ref, send_ref, gn_ref, ks, vs, dm, acc, accm, sums = rest[len(parts) :]
        i = pl.program_id(0)

        @pl.when(i == 0)
        def _():
            ks[...] = jnp.zeros_like(ks)
            vs[...] = jnp.zeros_like(vs)
            acc[...] = jnp.zeros_like(acc)
            accm[...] = jnp.zeros_like(accm)
            sums[...] = jnp.zeros_like(sums)

        for g in range(groups):
            ls = left_start(g)
            for dest, low, src in ((ks, 0, lk_ref), (vs, HALF, lv_ref)):
                dest[g, 0:MROWS, :] = kvm_ref[MROWS * g : MROWS * (g + 1), low : low + HALF]
                dest[g, MROWS : MROWS + QROWS, :] = qkv_ref[
                    QROWS * g : QROWS * (g + 1), HALF + low : 2 * HALF + low
                ]
                dest[g, MROWS + QROWS : MROWS + QROWS + LWIN, :] = src[ls : ls + LWIN, :]
        negative = jnp.full((KPAD, PAIR), -1.0, BF16)
        for g0 in range(0, groups, 4):
            work = {}
            units = [(g, k) for g in range(g0, g0 + 4) for k in range(2)]
            for g, k in units:
                here = slice(QROWS * g, QROWS * (g + 1))
                s = slice(k * PAIR, (k + 1) * PAIR)
                grad = da_ref[here, s]
                product = (grad.astype(F32) * att_ref[here, s].astype(F32)).astype(BF16)
                da = spread_pair(grad)
                left = jnp.concatenate([da, spread_pair(product)], axis=1)
                right = jnp.concatenate([vs[g, :, s], negative], axis=1)
                work[g, k] = da, dot_last(left, right)
            for g, k in units:
                da, centred = work[g, k]
                p = p_ref[k, 2 * QROWS * g : 2 * QROWS * (g + 1), :]
                work[g, k] = da, p, (p.astype(F32) * centred).astype(BF16)
            for g, k in units:
                here = slice(QROWS * g, QROWS * (g + 1))
                s = slice(k * PAIR, (k + 1) * PAIR)
                d_ref[here, s] = (join_pair(dot(work[g, k][2], ks[g, :, s])) * 0.125).astype(BF16)
            for g, k in units:
                here = slice(QROWS * g, QROWS * (g + 1))
                there = slice(MROWS * g, MROWS * (g + 1))
                s = slice(k * PAIR, (k + 1) * PAIR)
                at = k * PAIR
                da, p, ds = work[g, k]
                q = spread_pair(qkv_ref[here, s])
                dk = dot_rows(ds[:, :PAIR], q).astype(BF16)
                dv = dot_rows(p[:, :PAIR], da).astype(BF16)
                d_ref[here, HALF + at : HALF + at + PAIR] = dk[MROWS : MROWS + QROWS]
                d_ref[here, 2 * HALF + at : 2 * HALF + at + PAIR] = dv[MROWS : MROWS + QROWS]
                dm[there, at : at + PAIR] = dk[:MROWS]
                dm[there, HALF + at : HALF + at + PAIR] = dv[:MROWS]
        d = d_ref[...]
        acc[...] += dot(xhat_ref[...], d)
        accm[...] += dot(mem_ref[...], dm[...])
        sums[0:1, :] += jnp.sum(d.astype(F32), axis=0, keepdims=True)

        @pl.when(i == steps - 1)
        def _():
            lower = me_ref[2] == 0
            w = w_ref[...].astype(F32)
            total = acc[...]
            row_sum = sums[0:1, :]
            lane = lax.broadcasted_iota(jnp.int32, (D, PAIR), 1)
            gain_grad = jnp.sum(total * w, axis=1, keepdims=True)
            shift_grad = jnp.sum(row_sum * w, axis=1, keepdims=True)
            turned = jnp.where(lane == 0, gain_grad, jnp.where(lane == 1, shift_grad, 0.0)).T[0:8, :]
            gn_ref[...] = turned
            line = lax.broadcasted_iota(jnp.int32, (PAIR, D), 0)
            columns = jnp.where(line == 0, norm_ref[0:1, :], jnp.where(line == 1, norm_ref[1:2, :], 0.0)).T
            grads = total * columns[:, 0:1] + columns[:, 1:2] * row_sum
            gq = grads[:, :HALF]
            gk = grads[:, HALF : 2 * HALF] + accm[:, :HALF]
            gv = grads[:, 2 * HALF :] + accm[:, HALF:]
            if last:
                first_norm = turned
                for ref in part_refs[1:]:
                    first_norm = first_norm + ref[...]
                norm_grad = jnp.concatenate([first_norm[0:2], part_refs[0][0:2, :], jnp.zeros((12, D), F32)], axis=0)
                gn_ref[...] = norm_grad[0:8]
            for f in range(n):
                slot = places.slot_to(me_ref, f)
                for k, grad in enumerate((gq, gk, gv)):
                    low = grad[f * r : f * r + h].astype(BF16)
                    high = grad[f * r + h : (f + 1) * r].astype(BF16)
                    keep_ref[slot, k * h : (k + 1) * h, :] = jnp.where(lower, low, high)
                    send_ref[slot, k * h : (k + 1) * h, :] = jnp.where(lower, high, low)
                if last:
                    piece = norm_grad[:, f * r : (f + 1) * r].astype(BF16)
                    for ref in (keep_ref, send_ref):
                        ref[slot, 3 * h :, :] = jnp.zeros((NORM_ROWS, HALF), BF16)
                        ref[slot, 3 * h :, 0:r] = piece

    count = xhat.shape[1]
    wire = (n, m, HALF)
    return call(
        kernel,
        me,
        (steps,),
        [
            (xhat, (D, rows), lambda i: (0, i)),
            (memory_t, (D, step_spans * MEM), lambda i: (0, i)),
            (left_keys, *rows_of((step_spans * LEFT, HALF), half)),
            (left_values, *rows_of((step_spans * LEFT, HALF), half)),
            (qkv, *rows_of((rows, wide))),
            (kvm, *rows_of((step_spans * MEM, 2 * HALF))),
            (probs, (2, 2 * rows, KPAD), lambda i: (0, i, 0)),
            (grad_att, *rows_of((rows, HALF), half)),
            (attended, *rows_of((rows, HALF))),
            (weights, *whole((D, wide))),
            (norm, *whole((8, D))),
        ]
        + [(a, *whole((8, D))) for a in parts],
        [
            ((count, wide), BF16, *rows_of((rows, wide))),
            (wire, BF16, *whole(wire)),
            (wire, BF16, *whole(wire)),
            ((8, D), F32, *whole((8, D))),
        ],
        [pltpu.VMEM((groups, KPAD, HALF), BF16)] * 2
        + [
            pltpu.VMEM((step_spans * MEM, 2 * HALF), BF16),
            pltpu.VMEM((D, wide), F32),
            pltpu.VMEM((D, 2 * HALF), F32),
            pltpu.VMEM((8, wide), F32),
        ],
        f"attention_backward_{half}",
        flops=2 * count * D * wide * 8,
        moved=2 * (count * D * 5 + spans * LEFT * D + spans * 4 * ROWS_SPAN * KPAD),
    )


def frames_gradient(me, frames, grad_residual, grads, weights, norm, part, before):
    count = frames.shape[0]
    rows = 256
    steps = count // rows // 2
    start = part * steps

    def kernel(me_ref, fr_ref, res_ref, d0, d1, w0_ref, w1_ref, norm_ref, *rest):
        out_ref = rest[-1]
        grad = dot_last(d0[...], w0_ref[...]) + dot_last(d1[...], w1_ref[...])
        xhat, scale = normalize(fr_ref[...].astype(F32))
        out_ref[...] = res_ref[...] + norm_back(grad, xhat, scale, norm_ref[0:1, :])

    def block(shape):
        return shape, lambda i: (start + i, 0)

    ins = [(frames, *block((rows, D))), (grad_residual, *block((rows, D)))]
    ins += [(d, *block((rows, 3 * HALF))) for d in grads]
    ins += [(w, *whole((D, 3 * HALF))) for w in weights]
    ins += [(norm, *whole((8, D)))]
    if part:
        ins += [(before, None, None)]
    (out,) = call(
        kernel,
        me,
        (steps,),
        ins,
        [((count, D), F32, *block((rows, D)))],
        [],
        f"frames_gradient_{part}",
        flops=count * D * 3 * D,
        moved=count * D * 8,
        aliases={len(ins): 0} if part else None,
    )
    return out


def after(value, *others):
    return lax.optimization_barrier((value, *others))[0]


def add(a, b):
    return a.astype(F32) + b.astype(F32)


def update_ffn(me, up, down, ffn_in, ffn_in_m, ffn_in_v, ffn_out, ffn_out_m, ffn_out_v, places):
    r, r2 = D // places.n, FF // places.n
    half = FF // 2

    def kernel(me_ref, own_ref, other_ref, own_down, other_down, wi, mi, vi, wo, mo, vo, *outs):
        lower = me_ref[2] == 0

        def halves(mine, sib):
            return jnp.where(lower, mine, sib).astype(F32), jnp.where(lower, sib, mine).astype(F32)

        def put(refs, at, grad, w, m, v, rate):
            g_ref, f_ref, s_ref, n_ref, c_ref = refs
            first, second, new = adamw(w[:, at], grad, m[:, at], v[:, at], rate)
            g_ref[:, at] = grad
            f_ref[:, at] = first
            s_ref[:, at] = second
            n_ref[:, at] = new
            c_ref[:, at] = new.astype(BF16)

        low, high = halves(own_ref[...], other_ref[...])
        for k in range(4):
            for base, part in ((0, low), (half, high)):
                at = slice(base + k * HALF, base + (k + 1) * HALF)
                put(outs[:5], at, part[k * r : (k + 1) * r], wi, mi, vi, RATE_FFN_IN)
        low, high = halves(places.y_joined(me_ref, own_down), places.y_joined(me_ref, other_down))
        for at, part in ((slice(0, HALF), low), (slice(HALF, D), high)):
            put(outs[5:], at, part[r:], wo, mo, vo, RATE_FFN_OUT)

    si, so = (r, FF), (r2, D)
    return call(
        kernel,
        me,
        (1,),
        [(a, *whole(a.shape)) for a in (*up, *down, ffn_in, ffn_in_m, ffn_in_v, ffn_out, ffn_out_m, ffn_out_v)],
        [(s, t, *whole(s)) for s in (si, so) for t in (F32, F32, F32, F32, BF16)],
        [],
        "update_ffn",
        moved=4 * 8 * (r * FF + r2 * D),
    )


def update_attention(me, rest, sums, attn_w, attn_m, attn_v, norm_params, norm_m, norm_v, places):
    r, r2 = D // places.n, FF // places.n
    h = r // 2
    sums = [*rest, *sums]

    def kernel(me_ref, *refs):
        sum_refs = refs[: len(sums)]
        w, m, v, nw, nm, nv = refs[len(sums) : len(sums) + 6]
        outs = refs[len(sums) + 6 : len(sums) + 11]
        norm_outs = refs[len(sums) + 11 :]
        lower = me_ref[2] == 0

        def put(k, at, columns, grad):
            rate = RATES_ATTENTION[k]
            first, second, new = adamw(w[k, at, columns], grad, m[k, at, columns], v[k, at, columns], rate)
            for ref, value in zip(outs, (grad, first, second, new, new.astype(BF16))):
                ref[k, at, columns] = value

        def halves(mine, sib):
            return jnp.where(lower, mine, sib).astype(F32), jnp.where(lower, sib, mine).astype(F32)

        low, high = halves(*[places.y_joined(me_ref, ref)[:r] for ref in sum_refs[:2]])
        put(3, slice(0, r), slice(0, HALF), low)
        put(3, slice(0, r), slice(HALF, D), high)
        for p in range(2):
            columns = slice(p * HALF, (p + 1) * HALF)
            for k in range(3):
                at = p * 3 * h + k * h
                low, high = halves(*[ref[at : at + h, :] for ref in sum_refs[2:]])
                put(k, slice(0, h), columns, low)
                put(k, slice(h, r), columns, high)
        grad = sum_refs[2][6 * h :, :].astype(F32)[0:4, 0:r]
        first, second, new = adamw(nw[...], grad, nm[...], nv[...], RATE_NORM)
        for ref, value in zip(norm_outs, (grad, first, second, new, new.astype(BF16))):
            ref[...] = value

    shape, small = (4, r, D), (4, r)
    ins = (*sums, attn_w, attn_m, attn_v, norm_params, norm_m, norm_v)
    return call(
        kernel,
        me,
        (1,),
        [(a, *whole(a.shape)) for a in ins],
        [(s, t, *whole(s)) for s in (shape, small) for t in (F32, F32, F32, F32, BF16)],
        [],
        "update_attention",
        moved=4 * 8 * 4 * r * D,
    )


def shards(
    places,
    frames,
    memory,
    left_keys,
    left_values,
    lengths,
    cotangent,
    attn_w,
    ffn_in,
    ffn_out,
    norm_params,
    attn_m,
    attn_v,
    ffn_in_m,
    ffn_in_v,
    ffn_out_m,
    ffn_out_v,
    norm_m,
    norm_v,
):
    X, Z = places.X, places.Z
    tie = lax.optimization_barrier
    me = places.me()
    bias = length_bias(lengths)
    masks = jnp.asarray(span_masks())

    def direct(value):
        return [
            value if dx == dz == 0 else places.shift(value, dz, dx)
            for dx in range(X)
            for dz in range(Z)
        ]

    def along_z(value):
        return [value if dz == 0 else places.shift(value, dz, 0) for dz in range(Z)]

    def along_x(value):
        return [value if dx == 0 else places.shift(value, 0, dx) for dx in range(X)]

    def split(total):
        return total.reshape((X, Z) + total.shape[1:])

    def send_x(total):
        return [places.shift(total[dx].astype(BF16), 0, dx) for dx in range(1, X)]

    def send_z(column):
        return [places.shift(column[dz].astype(BF16), dz, 0) for dz in range(1, Z)]

    def collect(mine, got):
        for part in got:
            mine = add(mine, part)
        return mine

    first_wire = pack_first(me, attn_w, norm_params, places)
    mixed, up_wire = pack_rest(me, attn_w, ffn_in, ffn_out, places)
    first = direct(first_wire)
    mixed = jnp.stack(along_z(mixed))
    up_wire, first = tie((up_wire, first))
    first = jnp.stack(first)
    mixed = along_x(mixed)
    up = along_z(up_wire)
    me, first = tie((me, first))

    def forward(token, half, x, own, other):
        return attention_forward(
            token, half, x, memory, left_keys, left_values, bias, masks, own, other, places
        )

    qkv0, kvm0, att0, p0, w_low, hidden, xhat, memory_t, norm = forward(
        me, 0, frames, first, places.other_core(first)
    )
    me, att0, mixed, up = tie((me, att0, mixed, up))
    h3 = 3 * (D // places.n) // 2
    second = jnp.concatenate([part[:, :h3] for part in mixed], axis=0)
    down = jnp.stack([part[:, h3:] for part in mixed])
    down = [down if dy == 0 else places.shift_y(down, dy) for dy in range(places.Y)]
    up = along_x(jnp.stack(up))
    qkv1, kvm1, att1, p1, w_high = forward(me, 1, hidden, second, places.other_core(second))
    me, att1, up, down = tie((me, att1, up, down))
    up = up, [places.other_core(part) for part in up]
    down = down, [places.other_core(part) for part in down]
    output, grad_residual, grad_att, norm_two, keep_up, send_up, keep_down, send_down = feed_forward(
        me, (att0, att1), frames, cotangent, norm, up, down, places
    )

    def backward(token, half, saved, norm_parts=None):
        return attention_backward(
            token, half, xhat, memory_t, left_keys, left_values, saved, grad_att, norm, norm_parts, places
        )

    def send_y(total):
        return [places.shift_y(total[dy].astype(BF16), dy) for dy in range(1, places.Y)]

    up = split(add(keep_up, places.other_core(send_up)))
    down = add(keep_down, places.other_core(send_down))
    got_up, got_down = send_x(up), send_y(down)
    me, up, down = tie((me, up, down))
    d0, keep0, send0, n0 = backward(me, 0, (qkv0, kvm0, p0, w_low, att0))
    me, d0, got_up, got_down = tie((me, d0, got_up, got_down))
    up, down = collect(up[0], got_up), split(collect(down[0], got_down))
    got_up, got_down = send_z(up), send_x(down)
    got0 = places.other_core(send0)
    d1, keep1, send1, n1 = backward(me, 1, (qkv1, kvm1, p1, w_high, att1), [norm_two, n0])
    me, d1, got0, got_up, got_down = tie((me, d1, got0, got_up, got_down))
    got1 = places.other_core(send1)
    up, down = collect(up[0], got_up).astype(BF16), collect(down[0], got_down)
    attn = split(jnp.concatenate([add(keep0, got0), add(keep1, got1)], axis=1))
    got = send_x(attn)
    got_down = send_z(down)
    up = places.sum_over_y(up)
    frames_part = functools.partial(
        frames_gradient, frames=frames, grad_residual=grad_residual, grads=(d0, d1),
        weights=(w_low, w_high), norm=norm,
    )
    me, attn = tie((me, attn))
    input_grad = frames_part(me, part=0, before=None)
    me, input_grad, up, got, got_down = tie((me, input_grad, up, got, got_down))
    attn = collect(attn[0], got)
    got = send_z(attn)
    up = up, places.other_core(up)
    down = collect(down[0], got_down).astype(BF16)
    down = jnp.stack([down if dy == 0 else places.shift_y(down, dy) for dy in range(places.Y)])
    input_grad = frames_part(me, part=1, before=input_grad)
    me, input_grad, up, down, got = tie((me, input_grad, up, down, got))
    down = down, places.other_core(down)
    attn = places.sum_over_y(collect(attn[0], got).astype(BF16))
    ffn = update_ffn(me, up, down, ffn_in, ffn_in_m, ffn_in_v, ffn_out, ffn_out_m, ffn_out_v, places)
    attn = attn, places.other_core(attn)
    attention = update_attention(
        me, down, attn, attn_w, attn_m, attn_v, norm_params, norm_m, norm_v, places
    )
    return (output, input_grad, *attention[:5], *ffn, *attention[5:])


def solution(mesh):
    rows = P(("dp", "fsdp"), None)
    attn, ffn, norm = P(None, "fsdp", None), P("fsdp", None), P(None, "fsdp")
    return jax.shard_map(
        functools.partial(shards, Places(mesh)),
        mesh=mesh,
        in_specs=(rows,) * 4
        + (P(("dp", "fsdp")), rows, attn, ffn, ffn, norm)
        + (attn, attn, ffn, ffn, ffn, ffn, norm, norm),
        out_specs=(rows, rows) + (attn,) * 5 + (ffn,) * 10 + (norm,) * 5,
        check_vma=False,
    )
```

```python
import functools
import math

import jax
import jax.numpy as jnp
import numpy as np
from jax import lax
from jax.experimental import pallas as pl
from jax.experimental.pallas import tpu as pltpu
from jax.sharding import PartitionSpec as P

D = 512
FF = 2048
HEADS = 8
SEG = 16
LEFT = 30
MEM = 4
STEP = 5
ROWS_SPAN = 20
GROUP = 4
QROWS = GROUP * ROWS_SPAN
MROWS = GROUP * MEM
LROWS = GROUP * LEFT
LWIN = 128
KPAD = 256
HALF = 256
PAIR = 128
NORM_ROWS = 16

F32 = jnp.float32
BF16 = jnp.bfloat16
BLOCKED = -1e9
EPS_NORM = 1e-05
BETA_FIRST = 0.5
BETA_SECOND = 0.5
WEIGHT_DECAY = 0.01
EPS_ADAM = 1e-08
RATES_ATTENTION = (0.04, 0.04, 0.04, 0.25)
RATE_FFN_IN = 0.04
RATE_FFN_OUT = 0.02
RATE_NORM = 0.2


def dot(a, b):
    return lax.dot_general(a, b, (((1,), (0,)), ((), ())), preferred_element_type=F32)


def dot_last(a, b):
    return lax.dot_general(a, b, (((1,), (1,)), ((), ())), preferred_element_type=F32)


def dot_rows(a, b):
    return lax.dot_general(a, b, (((0,), (0,)), ((), ())), preferred_element_type=F32)


def normalize(x):
    mean = jnp.mean(x, axis=1, keepdims=True)
    centred = x - mean
    variance = jnp.mean(centred * centred, axis=1, keepdims=True)
    scale = lax.rsqrt(variance + EPS_NORM)
    return centred * scale, scale


def norm_back(grad, normed, scale, gain):
    grad = grad * gain
    first = jnp.mean(grad, axis=1, keepdims=True)
    second = jnp.mean(grad * normed, axis=1, keepdims=True)
    return scale * (grad - first - normed * second)


def gelu_parts(x):
    c = math.sqrt(2.0 / math.pi)
    square = x * x
    t = jnp.tanh(x * (c + (c * 0.044715) * square))
    half = 0.5 * x
    value = half + half * t
    slope = 0.5 + 0.5 * t + half * (1.0 - t * t) * (c + (3.0 * c * 0.044715) * square)
    return value, slope


def spread_pair(x):
    lane = lax.broadcasted_iota(jnp.int32, x.shape, 1)
    zero = jnp.zeros_like(x)
    return jnp.concatenate([jnp.where(lane < 64, x, zero), jnp.where(lane < 64, zero, x)], axis=0)


def join_pair(x):
    rows = x.shape[0] // 2
    lane = lax.broadcasted_iota(jnp.int32, (rows, PAIR), 1)
    return jnp.where(lane < 64, x[:rows], x[rows:])


def left_start(g):
    return LROWS * g - (8 if g % 2 else 0)


def span_masks():
    query_span = np.arange(2 * QROWS) % QROWS // ROWS_SPAN
    masks = np.full((2, 2 * QROWS, KPAD), BLOCKED, np.float32)
    for odd in range(2):
        span = np.full(KPAD, -1)
        span[:MROWS] = np.arange(MROWS) // MEM
        span[MROWS : MROWS + QROWS] = np.arange(QROWS) // ROWS_SPAN
        start = MROWS + QROWS + (8 if odd else 0)
        span[start : start + LROWS] = np.arange(LROWS) // LEFT
        masks[odd][query_span[:, None] == span[None, :]] = 0.0
    return masks


def dead_keys(lengths_ref, group):
    key = lax.broadcasted_iota(jnp.int32, (1, KPAD), 1) - MROWS
    length = jnp.full((1, KPAD), ROWS_SPAN, jnp.int32)
    place = jnp.zeros((1, KPAD), jnp.int32)
    for s in range(GROUP):
        inside = (key >= s * ROWS_SPAN) & (key < s * ROWS_SPAN + SEG)
        length = jnp.where(inside, lengths_ref[group * GROUP + s], length)
        place = jnp.where(inside, key - s * ROWS_SPAN, place)
    return jnp.where(place >= length, BLOCKED, 0.0)


def adamw(weight, grad, first_old, second_old, rate):
    first = BETA_FIRST * first_old + (1.0 - BETA_FIRST) * grad
    second = BETA_SECOND * second_old + (1.0 - BETA_SECOND) * grad * grad
    first_hat = first / (1.0 - BETA_FIRST**STEP)
    second_hat = second / (1.0 - BETA_SECOND**STEP)
    new = weight - rate * (first_hat / (jnp.sqrt(second_hat) + EPS_ADAM) + WEIGHT_DECAY * weight)
    return first, second, new


class Places:
    def __init__(self, mesh):
        self.n = mesh.shape["fsdp"]
        self.dp = mesh.shape["dp"]
        power = max(int(math.log2(self.n)) - 1, 0) // 2
        self.X = 2**power
        self.Z = self.n // self.X
        self.C = 2
        self.Y = self.dp // self.C

    def me(self):
        f = lax.axis_index("fsdp")
        d = lax.axis_index("dp")
        return jnp.stack([f // self.X, f % self.X, d % self.C, d // self.C]).astype(jnp.int32)

    def slot_to(self, me_ref, f):
        dz = lax.rem(f // self.X + self.Z - me_ref[0], self.Z)
        dx = lax.rem(f % self.X + self.X - me_ref[1], self.X)
        return dx * self.Z + dz

    def slot_from(self, me_ref, f):
        dz = lax.rem(me_ref[0] + self.Z - f // self.X, self.Z)
        dx = lax.rem(me_ref[1] + self.X - f % self.X, self.X)
        return dx * self.Z + dz

    def shift(self, value, dz, dx):
        X, Z = self.X, self.Z
        perm = [
            (z * X + x, (z + dz) % Z * X + (x + dx) % X) for z in range(Z) for x in range(X)
        ]
        return lax.ppermute(value, "fsdp", perm)

    def y_joined(self, me_ref, ref):
        slots = [lax.rem(me_ref[3] + self.Y - y, self.Y) for y in range(self.Y)]
        return jnp.concatenate([ref[slot] for slot in slots], axis=0)

    def y_slot_to(self, me_ref, y):
        return lax.rem(y + self.Y - me_ref[3], self.Y)

    def shift_y(self, value, dy):
        dp = self.dp
        return lax.ppermute(value, "dp", [(d, (d + 2 * dy) % dp) for d in range(dp)])

    def other_core(self, value):
        return lax.ppermute(value, "dp", [(d, d ^ 1) for d in range(self.dp)])

    def sum_over_y(self, value):
        step = 1
        while step < self.Y:
            got = lax.ppermute(value, "dp", [(d, d ^ (2 * step)) for d in range(self.dp)])
            value = (value.astype(F32) + got.astype(F32)).astype(BF16)
            step *= 2
        return value


def call(kernel, me, grid, ins, outs, scratch, name, flops=0, moved=0, aliases=None, limit=32):
    def spec(block, index):
        if block is None:
            return pl.BlockSpec(memory_space=pltpu.VMEM if index is None else pl.ANY)
        return pl.BlockSpec(block, lambda *a: index(*a[:-1]))

    return pl.pallas_call(
        kernel,
        grid_spec=pltpu.PrefetchScalarGridSpec(
            num_scalar_prefetch=1,
            grid=grid,
            in_specs=[spec(b, f) for _, b, f in ins],
            out_specs=[spec(b, f) for _, _, b, f in outs],
            scratch_shapes=scratch,
        ),
        out_shape=[jax.ShapeDtypeStruct(s, d) for s, d, _, _ in outs],
        compiler_params=pltpu.CompilerParams(vmem_limit_bytes=limit * 2**20),
        cost_estimate=pl.CostEstimate(flops=flops, bytes_accessed=moved, transcendentals=0),
        input_output_aliases=aliases or {},
        name=name,
    )(me, *[a for a, _, _ in ins])


def resident(array):
    return array, None, None


def whole(shape):
    return shape, lambda i: (0,) * len(shape)


def rows_of(shape, column=0):
    return shape, lambda i: (i, column)


def pack_first(attn_w, norm_params, places):
    r = D // places.n
    h = r // 2
    start = lax.axis_index("dp") % 2 * h
    rows = lax.dynamic_slice(attn_w[:3, :, :HALF], (0, start, 0), (3, h, HALF)).reshape(3 * h, HALF)
    norms = jnp.pad(norm_params, ((0, NORM_ROWS - 4), (0, HALF - r)))
    return jnp.concatenate([rows, norms], axis=0).astype(BF16)


def pack_rest(me, attn_w, ffn_in, ffn_out, places):
    r, r2 = D // places.n, FF // places.n
    h, q = r // 2, r2 // places.dp

    def kernel(me_ref, w_ref, in_ref, out_w_ref, second_ref, up_ref):
        lower = me_ref[2] == 0
        for k in range(3):
            w = w_ref[k, :, HALF:]
            second_ref[k * h : (k + 1) * h, :] = jnp.where(lower, w[:h], w[h:]).astype(BF16)
        member = me_ref[3] * 2 + me_ref[2]
        w = out_w_ref[pl.ds(pl.multiple_of(member * q, q), q), :].astype(BF16)
        second_ref[3 * h : 3 * h + q, :] = w[:, :HALF]
        second_ref[3 * h + q :, :] = w[:, HALF:]
        half = FF // 2
        for k in range(4):
            up_ref[k * r : (k + 1) * r, :] = jnp.where(
                lower,
                in_ref[:, k * HALF : (k + 1) * HALF],
                in_ref[:, half + k * HALF : half + (k + 1) * HALF],
            ).astype(BF16)
        w = w_ref[3]
        up_ref[4 * r :, :] = jnp.where(lower, w[:, :HALF], w[:, HALF:]).astype(BF16)

    shapes = (3 * h + 2 * q, HALF), (5 * r, HALF)
    return call(
        kernel,
        me,
        (1,),
        [
            (attn_w, *whole((4, r, D))),
            (ffn_in, *whole((r, FF))),
            (ffn_out, *whole((r2, D))),
        ],
        [(shape, BF16, *whole(shape)) for shape in shapes],
        [],
        "pack_rest",
        limit=58,
        moved=4 * (4 * r * D + r * FF + r2 * D),
    )


def attention_forward(me, half, x, memory, left_keys, left_values, masks, weights, places, part=0, parts=1, before=None):
    first = half == 0
    fresh = before is None
    spans = memory.shape[0] // MEM
    step_spans = 32 if spans % 32 == 0 else 16
    groups = step_spans // GROUP
    rows = step_spans * ROWS_SPAN
    n, r = places.n, D // places.n
    h = r // 2

    steps = spans // step_spans // parts
    start = part * steps

    def kernel(me_ref, x_ref, mem_ref, lk_ref, lv_ref, mask_ref, *rest):
        if fresh:
            own_ref, other_ref, *rest = rest
        else:
            w_ref, *rest = rest
            if first:
                norm_ref, *rest = rest
            rest = rest[len(aliased) :]
        qkv_ref, kvm_ref, att_ref, p_ref, *rest = rest
        if first:
            hid_ref, xhat_ref, memt_ref, *rest = rest
        if fresh:
            w_ref, *rest = rest
            if first:
                norm_ref, *rest = rest
        ks, vs = rest

        @pl.when(pl.program_id(0) == 0)
        def _():
            ks[...] = jnp.zeros_like(ks)
            vs[...] = jnp.zeros_like(vs)
            lower = me_ref[2] == 0
            if first and fresh:
                norm_ref[...] = jnp.zeros_like(norm_ref)
            for f in range(n) if fresh else ():
                slot = places.slot_from(me_ref, f)
                mine, sib = own_ref[slot], other_ref[slot]
                for at, part in (
                    (slice(f * r, f * r + h), jnp.where(lower, mine, sib)),
                    (slice(f * r + h, (f + 1) * r), jnp.where(lower, sib, mine)),
                ):
                    for k in range(3):
                        w_ref[at, k * HALF : (k + 1) * HALF] = part[k * h : (k + 1) * h]
                if first:
                    tail = mine[3 * h :, :].astype(F32)
                    norm_ref[:, f * r : (f + 1) * r] = tail[0:8, 0:r]

        w = w_ref[...]
        if first:
            xhat, _ = normalize(x_ref[...].astype(F32))
            xhat_ref[...] = xhat.astype(BF16).T
            memt_ref[...] = mem_ref[...].T
            hidden = (xhat * norm_ref[0:1, :] + norm_ref[1:2, :]).astype(BF16)
            hid_ref[...] = hidden
        else:
            hidden = x_ref[...]
        qkv = dot(hidden, w).astype(BF16)
        query = qkv[:, :HALF] * jnp.asarray(0.125, BF16)
        qkv_ref[:, :HALF] = query
        qkv_ref[:, HALF:] = qkv[:, HALF:]
        kvm = dot(mem_ref[...], w[:, HALF:]).astype(BF16)
        kvm_ref[...] = kvm
        for g in range(groups):
            ls = left_start(g)
            for dest, low, src in ((ks, 0, lk_ref), (vs, HALF, lv_ref)):
                dest[g, 0:MROWS, :] = kvm[MROWS * g : MROWS * (g + 1), low : low + HALF]
                dest[g, MROWS : MROWS + QROWS, :] = qkv[
                    QROWS * g : QROWS * (g + 1), HALF + low : 2 * HALF + low
                ]
                dest[g, MROWS + QROWS : MROWS + QROWS + LWIN, :] = src[ls : ls + LWIN, :]
        for g0 in range(0, groups, 4):
            work = {}
            units = [(g, p) for g in range(g0, g0 + 4) for p in range(2)]
            dead = {
                g: mask_ref[g % 2] + dead_keys(me_ref, (start + pl.program_id(0)) * groups + g + 1)
                for g in range(g0, g0 + 4)
            }
            for g, p in units:
                s = slice(p * PAIR, (p + 1) * PAIR)
                work[g, p] = dot_last(spread_pair(query[QROWS * g : QROWS * (g + 1), s]), ks[g, :, s])
            for g, p in units:
                scores = work[g, p] + dead[g]
                work[g, p] = jnp.exp(scores - jnp.max(scores, axis=1, keepdims=True))
            for g, p in units:
                s = slice(p * PAIR, (p + 1) * PAIR)
                e = work[g, p]
                right = jnp.concatenate([vs[g, :, s], jnp.ones((KPAD, PAIR), BF16)], axis=1)
                work[g, p] = e, dot(e.astype(BF16), right)
            for g, p in units:
                s = slice(p * PAIR, (p + 1) * PAIR)
                e, mixed = work[g, p]
                scale = 1.0 / mixed[:, PAIR:]
                at = slice(2 * QROWS * g, 2 * QROWS * (g + 1))
                p_ref[p, at, :PAIR] = (e[:, :PAIR] * scale).astype(BF16)
                p_ref[p, at, PAIR:] = (e[:, PAIR:] * scale).astype(BF16)
                att_ref[QROWS * g : QROWS * (g + 1), s] = join_pair(mixed[:, :PAIR] * scale).astype(BF16)

    count = x.shape[0]
    wide = 3 * HALF

    def some(shape, column=0):
        return shape, lambda i: (start + i, column)

    ins = [
        (x, *some((rows, D))),
        (memory, *some((step_spans * MEM, D))),
        (left_keys, *some((step_spans * LEFT, HALF), half)),
        (left_values, *some((step_spans * LEFT, HALF), half)),
        (masks, *whole((2, 2 * QROWS, KPAD))),
    ]
    outs = [
        ((count, wide), BF16, *some((rows, wide))),
        ((spans * MEM, 2 * HALF), BF16, *some((step_spans * MEM, 2 * HALF))),
        ((count, HALF), BF16, *some((rows, HALF))),
        ((2, 2 * count, KPAD), BF16, (2, 2 * rows, KPAD), lambda i: (0, start + i, 0)),
    ]
    if first:
        columns = lambda i: (0, start + i)
        outs += [
            ((count, D), BF16, *some((rows, D))),
            ((D, count), BF16, (D, rows), columns),
            ((D, spans * MEM), BF16, (D, step_spans * MEM), columns),
        ]
    shared = 2 if first else 1
    if fresh:
        aliased = []
        ins += [resident(a) for a in weights]
        outs += [((D, wide), BF16, *whole((D, wide))), ((8, D), F32, *whole((8, D)))][:shared]
    else:
        aliased, kept = before[:-shared], before[-shared:]
        ins += [(a, *whole(a.shape)) for a in kept] + [(a, None, 0) for a in aliased]
    result = call(
        kernel,
        me,
        (steps,),
        ins,
        outs,
        [pltpu.VMEM((groups, KPAD, HALF), BF16)] * 2,
        f"attention_forward_{half}_{part}",
        limit=58,
        flops=2 * count * D * wide * 4 // parts,
        moved=2 * (count * D * 3 + spans * LEFT * D + spans * 4 * ROWS_SPAN * KPAD) // parts,
        aliases={1 + len(ins) - len(aliased) + k: k for k in range(len(aliased))},
    )
    return list(result) if fresh else [*result, *kept]


def feed_forward(me, attended_halves, frames, cotangent, norm, up, down, places):
    count = frames.shape[0]
    rows = 512
    steps = count // rows
    chunk = 256
    n, r, r2 = places.n, D // places.n, FF // places.n
    X, Y, Z = places.X, places.Y, places.Z
    q, part_rows = r2 // places.dp, (r + r2) // Y

    def kernel(me_ref, a0, a1, fr_ref, cot_ref, norm_ref, *rest):
        up_refs, other_up_refs, rest = rest[:X], rest[X : 2 * X], rest[2 * X :]
        down_refs, other_down_refs, rest = rest[:Y], rest[Y : 2 * Y], rest[2 * Y :]
        out_ref, res_ref, gatt_ref, gn_ref, keep_up, send_up, keep_down, send_down, *rest = rest
        w1, w2, wo, acc1, acc2, acco = rest
        i = pl.program_id(0)
        lower = me_ref[2] == 0

        @pl.when(i == 0)
        def _():
            acc1[...] = jnp.zeros_like(acc1)
            acc2[...] = jnp.zeros_like(acc2)
            acco[...] = jnp.zeros_like(acco)
            gn_ref[...] = jnp.zeros_like(gn_ref)
            for dx in range(X):
                xx = lax.rem(me_ref[1] + X - dx, X)
                for dz in range(Z):
                    zz = lax.rem(me_ref[0] + Z - dz, Z)
                    f = zz * X + xx

                    def halves(mine, sib):
                        return jnp.where(lower, mine, sib), jnp.where(lower, sib, mine)

                    low, high = halves(up_refs[dx][dz], other_up_refs[dx][dz])
                    at = pl.ds(pl.multiple_of(f * r, r), r)
                    for k in range(4):
                        w1[at, k * HALF : (k + 1) * HALF] = low[k * r : (k + 1) * r]
                        w1[at, FF // 2 + k * HALF : FF // 2 + (k + 1) * HALF] = high[k * r : (k + 1) * r]
                    wo[at, :HALF] = low[4 * r :]
                    wo[at, HALF:] = high[4 * r :]
                    for dy in range(Y):
                        yy = lax.rem(me_ref[3] + Y - dy, Y)
                        for core, part in enumerate(
                            halves(down_refs[dy][dx, dz], other_down_refs[dy][dx, dz])
                        ):
                            at = pl.ds(pl.multiple_of(f * r2 + (yy * 2 + core) * q, q), q)
                            w2[at, :HALF] = part[:q]
                            w2[at, HALF:] = part[q:]

        attended = jnp.concatenate([a0[...], a1[...]], axis=1)
        residual = fr_ref[...].astype(F32) + dot(attended, wo[...])
        normed, scale = normalize(residual)
        gain = norm_ref[2:3, :]
        hidden = (normed * gain + norm_ref[3:4, :]).astype(BF16)
        cot = cot_ref[...]
        output = residual
        grad = None
        slices = [slice(j * chunk, (j + 1) * chunk) for j in range(FF // chunk)]
        late = None
        for j, s in enumerate(slices):
            inner, grad_act = dot(hidden, w1[:, s]), dot_last(cot, w2[s, :])
            if late is not None:
                u, active, grad_inner = late
                output = output + dot(active, w2[u, :])
                part = dot_last(grad_inner, w1[:, u])
                grad = part if grad is None else grad + part
                acc1[:, u] += dot_rows(hidden, grad_inner)
                acc2[:, u] += dot_rows(cot, active)
            value, slope = gelu_parts(inner)
            late = s, value.astype(BF16), (grad_act * slope).astype(BF16)
        u, active, grad_inner = late
        output = output + dot(active, w2[u, :])
        grad = grad + dot_last(grad_inner, w1[:, u])
        acc1[:, u] += dot_rows(hidden, grad_inner)
        acc2[:, u] += dot_rows(cot, active)
        out_ref[...] = output.astype(BF16)
        gn_ref[0:1, :] += jnp.sum(grad * normed, axis=0, keepdims=True)
        gn_ref[1:2, :] += jnp.sum(grad, axis=0, keepdims=True)
        grad_residual = cot.astype(F32) + norm_back(grad, normed, scale, gain)
        res_ref[...] = grad_residual
        grad_low = grad_residual.astype(BF16)
        gatt_ref[...] = dot_last(grad_low, wo[...]).astype(BF16)
        acco[...] += dot_rows(attended, grad_low)

        @pl.when(i == steps - 1)
        def _():
            for f in range(n):
                slot = places.slot_to(me_ref, f)

                def sides(low, high):
                    low, high = low.astype(BF16), high.astype(BF16)
                    return jnp.where(lower, low, high), jnp.where(lower, high, low)

                here = slice(f * r, (f + 1) * r)
                for k in range(4):
                    at = slice(k * r, (k + 1) * r)
                    keep_up[slot, at, :], send_up[slot, at, :] = sides(
                        acc1[here, k * HALF : (k + 1) * HALF],
                        acc1[here, FF // 2 + k * HALF : FF // 2 + (k + 1) * HALF],
                    )
                turned = acc2[:, f * r2 : (f + 1) * r2].T
                low = jnp.concatenate([acco[here, :HALF], turned[:, :HALF]], axis=0)
                high = jnp.concatenate([acco[here, HALF:], turned[:, HALF:]], axis=0)
                for y in range(Y):
                    at = slice(y * part_rows, (y + 1) * part_rows)
                    to = places.y_slot_to(me_ref, y)
                    keep_down[to, slot], send_down[to, slot] = sides(low[at], high[at])

    wires = [(n, 4 * r, HALF)] * 2 + [(Y, n, part_rows, HALF)] * 2
    return call(
        kernel,
        me,
        (steps,),
        [(a, *rows_of((rows, HALF))) for a in attended_halves]
        + [
            (frames, *rows_of((rows, D))),
            (cotangent, *rows_of((rows, D))),
            (norm, *whole((8, D))),
        ]
        + [resident(a) for a in (*up[0], *up[1], *down[0], *down[1])],
        [
            ((count, D), BF16, *rows_of((rows, D))),
            ((count, D), F32, *rows_of((rows, D))),
            ((count, D), BF16, *rows_of((rows, D))),
            ((8, D), F32, *whole((8, D))),
        ]
        + [(wire, BF16, *whole(wire)) for wire in wires],
        [
            pltpu.VMEM((D, FF), BF16),
            pltpu.VMEM((FF, D), BF16),
            pltpu.VMEM((D, D), BF16),
            pltpu.VMEM((D, FF), F32),
            pltpu.VMEM((D, FF), F32),
            pltpu.VMEM((D, D), F32),
        ],
        "feed_forward",
        limit=46,
        flops=2 * count * D * (6 * FF + 3 * D) * 2,
        moved=2 * count * D * 8,
    )


def attention_backward(me, half, xhat, memory_t, left_keys, left_values, saved, grad_att, norm, norm_parts, places):
    last = norm_parts is not None
    qkv, kvm, probs, weights, attended = saved
    spans = memory_t.shape[1] // MEM
    step_spans = 32 if spans % 32 == 0 else 16
    steps = spans // step_spans
    groups = step_spans // GROUP
    rows = step_spans * ROWS_SPAN
    n, r = places.n, D // places.n
    h = r // 2
    m = 3 * h + (NORM_ROWS if last else 0)
    wide = 3 * HALF
    parts = norm_parts if last else []

    def kernel(me_ref, xhat_ref, mem_ref, lk_ref, lv_ref, qkv_ref, kvm_ref, p_ref, da_ref, att_ref, w_ref, norm_ref, *rest):
        part_refs = rest[: len(parts)]
        d_ref, keep_ref, send_ref, gn_ref, ks, vs, dm, acc, accm, sums = rest[len(parts) :]
        i = pl.program_id(0)

        @pl.when(i == 0)
        def _():
            ks[...] = jnp.zeros_like(ks)
            vs[...] = jnp.zeros_like(vs)
            acc[...] = jnp.zeros_like(acc)
            accm[...] = jnp.zeros_like(accm)
            sums[...] = jnp.zeros_like(sums)

        for g in range(groups):
            ls = left_start(g)
            for dest, low, src in ((ks, 0, lk_ref), (vs, HALF, lv_ref)):
                dest[g, 0:MROWS, :] = kvm_ref[MROWS * g : MROWS * (g + 1), low : low + HALF]
                dest[g, MROWS : MROWS + QROWS, :] = qkv_ref[
                    QROWS * g : QROWS * (g + 1), HALF + low : 2 * HALF + low
                ]
                dest[g, MROWS + QROWS : MROWS + QROWS + LWIN, :] = src[ls : ls + LWIN, :]
        negative = jnp.full((KPAD, PAIR), -1.0, BF16)
        for g0 in range(0, groups, 4):
            work = {}
            units = [(g, k) for g in range(g0, g0 + 4) for k in range(2)]
            for g, k in units:
                here = slice(QROWS * g, QROWS * (g + 1))
                s = slice(k * PAIR, (k + 1) * PAIR)
                grad = da_ref[here, s]
                product = (grad.astype(F32) * att_ref[here, s].astype(F32)).astype(BF16)
                da = spread_pair(grad)
                left = jnp.concatenate([da, spread_pair(product)], axis=1)
                right = jnp.concatenate([vs[g, :, s], negative], axis=1)
                work[g, k] = da, dot_last(left, right)
            for g, k in units:
                da, centred = work[g, k]
                p = p_ref[k, 2 * QROWS * g : 2 * QROWS * (g + 1), :]
                work[g, k] = da, p, (p.astype(F32) * centred).astype(BF16)
            for g, k in units:
                here = slice(QROWS * g, QROWS * (g + 1))
                s = slice(k * PAIR, (k + 1) * PAIR)
                d_ref[here, s] = (join_pair(dot(work[g, k][2], ks[g, :, s])) * 0.125).astype(BF16)
            for g, k in units:
                here = slice(QROWS * g, QROWS * (g + 1))
                there = slice(MROWS * g, MROWS * (g + 1))
                s = slice(k * PAIR, (k + 1) * PAIR)
                at = k * PAIR
                da, p, ds = work[g, k]
                q = spread_pair(qkv_ref[here, s])
                dk = dot_rows(ds[:, :PAIR], q).astype(BF16)
                dv = dot_rows(p[:, :PAIR], da).astype(BF16)
                d_ref[here, HALF + at : HALF + at + PAIR] = dk[MROWS : MROWS + QROWS]
                d_ref[here, 2 * HALF + at : 2 * HALF + at + PAIR] = dv[MROWS : MROWS + QROWS]
                dm[there, at : at + PAIR] = dk[:MROWS]
                dm[there, HALF + at : HALF + at + PAIR] = dv[:MROWS]
        d = d_ref[...]
        acc[...] += dot(xhat_ref[...], d)
        accm[...] += dot(mem_ref[...], dm[...])
        sums[0:1, :] += jnp.sum(d.astype(F32), axis=0, keepdims=True)

        @pl.when(i == steps - 1)
        def _():
            lower = me_ref[2] == 0
            w = w_ref[...].astype(F32)
            total = acc[...]
            row_sum = sums[0:1, :]
            lane = lax.broadcasted_iota(jnp.int32, (D, PAIR), 1)
            gain_grad = jnp.sum(total * w, axis=1, keepdims=True)
            shift_grad = jnp.sum(row_sum * w, axis=1, keepdims=True)
            turned = jnp.where(lane == 0, gain_grad, jnp.where(lane == 1, shift_grad, 0.0)).T[0:8, :]
            gn_ref[...] = turned
            line = lax.broadcasted_iota(jnp.int32, (PAIR, D), 0)
            columns = jnp.where(line == 0, norm_ref[0:1, :], jnp.where(line == 1, norm_ref[1:2, :], 0.0)).T
            grads = total * columns[:, 0:1] + columns[:, 1:2] * row_sum
            gq = grads[:, :HALF]
            gk = grads[:, HALF : 2 * HALF] + accm[:, :HALF]
            gv = grads[:, 2 * HALF :] + accm[:, HALF:]
            if last:
                first_norm = turned
                for ref in part_refs[1:]:
                    first_norm = first_norm + ref[...]
                norm_grad = jnp.concatenate([first_norm[0:2], part_refs[0][0:2, :], jnp.zeros((12, D), F32)], axis=0)
                gn_ref[...] = norm_grad[0:8]
            for f in range(n):
                slot = places.slot_to(me_ref, f)
                for k, grad in enumerate((gq, gk, gv)):
                    low = grad[f * r : f * r + h].astype(BF16)
                    high = grad[f * r + h : (f + 1) * r].astype(BF16)
                    keep_ref[slot, k * h : (k + 1) * h, :] = jnp.where(lower, low, high)
                    send_ref[slot, k * h : (k + 1) * h, :] = jnp.where(lower, high, low)
                if last:
                    piece = norm_grad[:, f * r : (f + 1) * r].astype(BF16)
                    for ref in (keep_ref, send_ref):
                        ref[slot, 3 * h :, :] = jnp.zeros((NORM_ROWS, HALF), BF16)
                        ref[slot, 3 * h :, 0:r] = piece

    count = xhat.shape[1]
    wire = (n, m, HALF)
    return call(
        kernel,
        me,
        (steps,),
        [
            (xhat, (D, rows), lambda i: (0, i)),
            (memory_t, (D, step_spans * MEM), lambda i: (0, i)),
            (left_keys, *rows_of((step_spans * LEFT, HALF), half)),
            (left_values, *rows_of((step_spans * LEFT, HALF), half)),
            (qkv, *rows_of((rows, wide))),
            (kvm, *rows_of((step_spans * MEM, 2 * HALF))),
            (probs, (2, 2 * rows, KPAD), lambda i: (0, i, 0)),
            (grad_att, *rows_of((rows, HALF), half)),
            (attended, *rows_of((rows, HALF))),
            (weights, *whole((D, wide))),
            (norm, *whole((8, D))),
        ]
        + [(a, *whole((8, D))) for a in parts],
        [
            ((count, wide), BF16, *rows_of((rows, wide))),
            (wire, BF16, *whole(wire)),
            (wire, BF16, *whole(wire)),
            ((8, D), F32, *whole((8, D))),
        ],
        [pltpu.VMEM((groups, KPAD, HALF), BF16)] * 2
        + [
            pltpu.VMEM((step_spans * MEM, 2 * HALF), BF16),
            pltpu.VMEM((D, wide), F32),
            pltpu.VMEM((D, 2 * HALF), F32),
            pltpu.VMEM((8, wide), F32),
        ],
        f"attention_backward_{half}",
        limit=58,
        flops=2 * count * D * wide * 8,
        moved=2 * (count * D * 5 + spans * LEFT * D + spans * 4 * ROWS_SPAN * KPAD),
    )


def frames_gradient(me, frames, grad_residual, grads, weights, norm, part, before):
    count = frames.shape[0]
    rows = 256
    steps = count // rows // 2
    start = part * steps

    def kernel(me_ref, fr_ref, res_ref, d0, d1, w0_ref, w1_ref, norm_ref, *rest):
        out_ref = rest[-1]
        grad = dot_last(d0[...], w0_ref[...]) + dot_last(d1[...], w1_ref[...])
        xhat, scale = normalize(fr_ref[...].astype(F32))
        out_ref[...] = res_ref[...] + norm_back(grad, xhat, scale, norm_ref[0:1, :])

    def block(shape):
        return shape, lambda i: (start + i, 0)

    ins = [(frames, *block((rows, D))), (grad_residual, *block((rows, D)))]
    ins += [(d, *block((rows, 3 * HALF))) for d in grads]
    ins += [(w, *whole((D, 3 * HALF))) for w in weights]
    ins += [(norm, *whole((8, D)))]
    if part:
        ins += [(before, None, 0)]
    (out,) = call(
        kernel,
        me,
        (steps,),
        ins,
        [((count, D), F32, *block((rows, D)))],
        [],
        f"frames_gradient_{part}",
        flops=count * D * 3 * D,
        moved=count * D * 8,
        aliases={len(ins): 0} if part else None,
    )
    return out


def after(value, *others):
    return lax.optimization_barrier((value, *others))[0]


def add(a, b):
    return a.astype(F32) + b.astype(F32)


def update_ffn(me, up, down, ffn_in, ffn_in_m, ffn_in_v, ffn_out, ffn_out_m, ffn_out_v, places):
    r, r2 = D // places.n, FF // places.n
    half = FF // 2

    def kernel(me_ref, own_ref, other_ref, own_down, other_down, wi, mi, vi, wo, mo, vo, *outs):
        lower = me_ref[2] == 0

        def halves(mine, sib):
            return jnp.where(lower, mine, sib).astype(F32), jnp.where(lower, sib, mine).astype(F32)

        def put(refs, at, grad, w, m, v, rate):
            g_ref, f_ref, s_ref, n_ref, c_ref = refs
            first, second, new = adamw(w[:, at], grad, m[:, at], v[:, at], rate)
            g_ref[:, at] = grad
            f_ref[:, at] = first
            s_ref[:, at] = second
            n_ref[:, at] = new
            c_ref[:, at] = new.astype(BF16)

        low, high = halves(own_ref[...], other_ref[...])
        for k in range(4):
            for base, part in ((0, low), (half, high)):
                at = slice(base + k * HALF, base + (k + 1) * HALF)
                put(outs[:5], at, part[k * r : (k + 1) * r], wi, mi, vi, RATE_FFN_IN)
        low, high = halves(places.y_joined(me_ref, own_down), places.y_joined(me_ref, other_down))
        for at, part in ((slice(0, HALF), low), (slice(HALF, D), high)):
            put(outs[5:], at, part[r:], wo, mo, vo, RATE_FFN_OUT)

    si, so = (r, FF), (r2, D)
    return call(
        kernel,
        me,
        (1,),
        [resident(a) for a in (*up, *down)]
        + [(a, *whole(a.shape)) for a in (ffn_in, ffn_in_m, ffn_in_v, ffn_out, ffn_out_m, ffn_out_v)],
        [(s, t, *whole(s)) for s in (si, so) for t in (F32, F32, F32, F32, BF16)],
        [],
        "update_ffn",
        moved=4 * 8 * (r * FF + r2 * D),
    )


def update_attention(me, rest, sums, attn_w, attn_m, attn_v, norm_params, norm_m, norm_v, places):
    r, r2 = D // places.n, FF // places.n
    h = r // 2
    sums = [*rest, *sums]

    def kernel(me_ref, *refs):
        sum_refs = refs[: len(sums)]
        w, m, v, nw, nm, nv = refs[len(sums) : len(sums) + 6]
        outs = refs[len(sums) + 6 : len(sums) + 11]
        norm_outs = refs[len(sums) + 11 :]
        lower = me_ref[2] == 0
        step = pl.program_id(0)

        def put(rate, at, columns, grad):
            first, second, new = adamw(w[0, at, columns], grad, m[0, at, columns], v[0, at, columns], rate)
            for ref, value in zip(outs, (grad, first, second, new, new.astype(BF16))):
                ref[0, at, columns] = value

        def halves(mine, sib):
            return jnp.where(lower, mine, sib).astype(F32), jnp.where(lower, sib, mine).astype(F32)

        for k in range(3):

            @pl.when(step == k)
            def _(k=k):
                for p in range(2):
                    columns = slice(p * HALF, (p + 1) * HALF)
                    at = p * 3 * h + k * h
                    low, high = halves(*[ref[at : at + h, :] for ref in sum_refs[2:]])
                    put(RATES_ATTENTION[k], slice(0, h), columns, low)
                    put(RATES_ATTENTION[k], slice(h, r), columns, high)

        @pl.when(step == 3)
        def _():
            low, high = halves(*[places.y_joined(me_ref, ref)[:r] for ref in sum_refs[:2]])
            put(RATES_ATTENTION[3], slice(0, r), slice(0, HALF), low)
            put(RATES_ATTENTION[3], slice(0, r), slice(HALF, D), high)

        @pl.when(step == 0)
        def _():
            grad = sum_refs[2][6 * h :, :].astype(F32)[0:4, 0:r]
            first, second, new = adamw(nw[...], grad, nm[...], nv[...], RATE_NORM)
            for ref, value in zip(norm_outs, (grad, first, second, new, new.astype(BF16))):
                ref[...] = value

    shape, small = (4, r, D), (4, r)
    block = (1, r, D), lambda i: (i, 0, 0)
    kinds = (F32, F32, F32, F32, BF16)
    return call(
        kernel,
        me,
        (4,),
        [resident(a) for a in sums]
        + [(a, *block) for a in (attn_w, attn_m, attn_v)]
        + [(a, *whole(small)) for a in (norm_params, norm_m, norm_v)],
        [(shape, t, *block) for t in kinds] + [(small, t, *whole(small)) for t in kinds],
        [],
        "update_attention",
        moved=4 * 8 * 4 * r * D,
    )


def shards(
    places,
    frames,
    memory,
    left_keys,
    left_values,
    lengths,
    cotangent,
    attn_w,
    ffn_in,
    ffn_out,
    norm_params,
    attn_m,
    attn_v,
    ffn_in_m,
    ffn_in_v,
    ffn_out_m,
    ffn_out_v,
    norm_m,
    norm_v,
):
    X, Z = places.X, places.Z
    tie = lax.optimization_barrier
    me = jnp.concatenate([places.me(), lengths])
    masks = jnp.asarray(span_masks())

    def direct(value):
        return [
            value if dx == dz == 0 else places.shift(value, dz, dx)
            for dx in range(X)
            for dz in range(Z)
        ]

    def along_z(value):
        return [value if dz == 0 else places.shift(value, dz, 0) for dz in range(Z)]

    def along_x(value):
        return [value if dx == 0 else places.shift(value, 0, dx) for dx in range(X)]

    def split(total):
        return total.reshape((X, Z) + total.shape[1:])

    def send_x(total):
        return [places.shift(total[dx].astype(BF16), 0, dx) for dx in range(1, X)]

    def send_z(column):
        return [places.shift(column[dz].astype(BF16), dz, 0) for dz in range(1, Z)]

    def collect(mine, got):
        for part in got:
            mine = add(mine, part)
        return mine

    first_wire = pack_first(attn_w, norm_params, places)
    mixed, up_wire = pack_rest(me, attn_w, ffn_in, ffn_out, places)
    first = direct(first_wire)
    mixed = along_z(mixed)
    up_wire, first = tie((up_wire, first))
    first = jnp.stack(first)
    up = along_z(up_wire)
    me, first = tie((me, first))

    def forward(token, half, x, weights, **part):
        return attention_forward(
            token, half, x, memory, left_keys, left_values, masks, weights, places, **part
        )

    low = forward(me, 0, frames, (first, places.other_core(first)), parts=2)
    me, low, mixed = tie((me, low, mixed))
    mixed = along_x(jnp.stack(mixed))
    low = forward(me, 0, frames, None, parts=2, part=1, before=low)
    me, low, mixed, up = tie((me, low, mixed, up))
    qkv0, kvm0, att0, p0, hidden, xhat, memory_t, w_low, norm = low
    h3 = 3 * (D // places.n) // 2
    second = jnp.concatenate([part[:, :h3] for part in mixed], axis=0)
    down = jnp.stack([part[:, h3:] for part in mixed])
    down = [down if dy == 0 else places.shift_y(down, dy) for dy in range(places.Y)]
    up = along_x(jnp.stack(up))
    early = places.other_core(up[0]), places.other_core(down[0])
    qkv1, kvm1, att1, p1, w_high = forward(me, 1, hidden, (second, places.other_core(second)))
    me, att1, up, down, early = tie((me, att1, up, down, early))
    up = up, [early[0]] + [places.other_core(part) for part in up[1:]]
    down = down, [early[1]] + [places.other_core(part) for part in down[1:]]
    output, grad_residual, grad_att, norm_two, keep_up, send_up, keep_down, send_down = feed_forward(
        me, (att0, att1), frames, cotangent, norm, up, down, places
    )

    def backward(token, half, saved, norm_parts=None):
        return attention_backward(
            token, half, xhat, memory_t, left_keys, left_values, saved, grad_att, norm, norm_parts, places
        )

    def send_y(total):
        return [places.shift_y(total[dy].astype(BF16), dy) for dy in range(1, places.Y)]

    up = split(add(keep_up, places.other_core(send_up)))
    down = add(keep_down, places.other_core(send_down))
    got_up, got_down = send_x(up), send_y(down)
    me, up, down = tie((me, up, down))
    d0, keep0, send0, n0 = backward(me, 0, (qkv0, kvm0, p0, w_low, att0))
    me, d0, got_up, got_down = tie((me, d0, got_up, got_down))
    up, down = collect(up[0], got_up), split(collect(down[0], got_down))
    got_up, got_down = send_z(up), send_x(down)
    got0 = places.other_core(send0)
    d1, keep1, send1, n1 = backward(me, 1, (qkv1, kvm1, p1, w_high, att1), [norm_two, n0])
    me, d1, got0, got_up, got_down = tie((me, d1, got0, got_up, got_down))
    got1 = places.other_core(send1)
    up, down = collect(up[0], got_up).astype(BF16), collect(down[0], got_down)
    attn = split(jnp.concatenate([add(keep0, got0), add(keep1, got1)], axis=1))
    got = send_x(attn)
    got_down = send_z(down)
    up = places.sum_over_y(up)
    frames_part = functools.partial(
        frames_gradient, frames=frames, grad_residual=grad_residual, grads=(d0, d1),
        weights=(w_low, w_high), norm=norm,
    )
    me, attn = tie((me, attn))
    input_grad = frames_part(me, part=0, before=None)
    me, input_grad, up, got, got_down = tie((me, input_grad, up, got, got_down))
    attn = collect(attn[0], got)
    got = send_z(attn)
    up = up, places.other_core(up)
    down = collect(down[0], got_down).astype(BF16)
    down = jnp.stack([down if dy == 0 else places.shift_y(down, dy) for dy in range(places.Y)])
    input_grad = frames_part(me, part=1, before=input_grad)
    me, input_grad, up, down, got = tie((me, input_grad, up, down, got))
    down = down, places.other_core(down)
    attn = places.sum_over_y(collect(attn[0], got).astype(BF16))
    ffn = update_ffn(me, up, down, ffn_in, ffn_in_m, ffn_in_v, ffn_out, ffn_out_m, ffn_out_v, places)
    attn = attn, places.other_core(attn)
    attention = update_attention(
        me, down, attn, attn_w, attn_m, attn_v, norm_params, norm_m, norm_v, places
    )
    return (output, input_grad, *attention[:5], *ffn, *attention[5:])


def solution(mesh):
    rows = P(("dp", "fsdp"), None)
    attn, ffn, norm = P(None, "fsdp", None), P("fsdp", None), P(None, "fsdp")
    return jax.shard_map(
        functools.partial(shards, Places(mesh)),
        mesh=mesh,
        in_specs=(rows,) * 4
        + (P(("dp", "fsdp")), rows, attn, ffn, ffn, norm)
        + (attn, attn, ffn, ffn, ffn, ffn, norm, norm),
        out_specs=(rows, rows) + (attn,) * 5 + (ffn,) * 10 + (norm,) * 5,
        check_vma=False,
    )
```

```python
import functools
import math

import jax
import jax.numpy as jnp
import numpy as np
from jax import lax
from jax.experimental import pallas as pl
from jax.experimental.pallas import tpu as pltpu
from jax.sharding import PartitionSpec as P

D = 512
FF = 2048
HEADS = 8
SEG = 16
LEFT = 30
MEM = 4
STEP = 5
ROWS_SPAN = 20
GROUP = 4
QROWS = GROUP * ROWS_SPAN
MROWS = GROUP * MEM
LROWS = GROUP * LEFT
LWIN = 128
KPAD = 256
HALF = 256
PAIR = 128
NORM_ROWS = 16

F32 = jnp.float32
BF16 = jnp.bfloat16
BLOCKED = -1e9
EPS_NORM = 1e-05
BETA_FIRST = 0.5
BETA_SECOND = 0.5
WEIGHT_DECAY = 0.01
EPS_ADAM = 1e-08
RATES_ATTENTION = (0.04, 0.04, 0.04, 0.25)
RATE_FFN_IN = 0.04
RATE_FFN_OUT = 0.02
RATE_NORM = 0.2


def dot(a, b):
    return lax.dot_general(a, b, (((1,), (0,)), ((), ())), preferred_element_type=F32)


def dot_last(a, b):
    return lax.dot_general(a, b, (((1,), (1,)), ((), ())), preferred_element_type=F32)


def dot_rows(a, b):
    return lax.dot_general(a, b, (((0,), (0,)), ((), ())), preferred_element_type=F32)


def normalize(x):
    mean = jnp.mean(x, axis=1, keepdims=True)
    centred = x - mean
    variance = jnp.mean(centred * centred, axis=1, keepdims=True)
    scale = lax.rsqrt(variance + EPS_NORM)
    return centred * scale, scale


def norm_back(grad, normed, scale, gain):
    grad = grad * gain
    first = jnp.mean(grad, axis=1, keepdims=True)
    second = jnp.mean(grad * normed, axis=1, keepdims=True)
    return scale * (grad - first - normed * second)


def gelu_parts(x):
    c = math.sqrt(2.0 / math.pi)
    square = x * x
    t = jnp.tanh(x * (c + (c * 0.044715) * square))
    half = 0.5 * x
    value = half + half * t
    slope = 0.5 + 0.5 * t + half * (1.0 - t * t) * (c + (3.0 * c * 0.044715) * square)
    return value, slope


def spread_pair(x):
    lane = lax.broadcasted_iota(jnp.int32, x.shape, 1)
    zero = jnp.zeros_like(x)
    return jnp.concatenate([jnp.where(lane < 64, x, zero), jnp.where(lane < 64, zero, x)], axis=0)


def join_pair(x):
    rows = x.shape[0] // 2
    lane = lax.broadcasted_iota(jnp.int32, (rows, PAIR), 1)
    return jnp.where(lane < 64, x[:rows], x[rows:])


def left_start(g):
    return LROWS * g - (8 if g % 2 else 0)


def span_masks():
    query_span = np.arange(2 * QROWS) % QROWS // ROWS_SPAN
    masks = np.full((2, 2 * QROWS, KPAD), BLOCKED, np.float32)
    for odd in range(2):
        span = np.full(KPAD, -1)
        span[:MROWS] = np.arange(MROWS) // MEM
        span[MROWS : MROWS + QROWS] = np.arange(QROWS) // ROWS_SPAN
        start = MROWS + QROWS + (8 if odd else 0)
        span[start : start + LROWS] = np.arange(LROWS) // LEFT
        masks[odd][query_span[:, None] == span[None, :]] = 0.0
    return masks


def dead_keys(lengths_ref, group):
    key = lax.broadcasted_iota(jnp.int32, (1, KPAD), 1) - MROWS
    length = jnp.full((1, KPAD), ROWS_SPAN, jnp.int32)
    place = jnp.zeros((1, KPAD), jnp.int32)
    for s in range(GROUP):
        inside = (key >= s * ROWS_SPAN) & (key < s * ROWS_SPAN + SEG)
        length = jnp.where(inside, lengths_ref[group * GROUP + s], length)
        place = jnp.where(inside, key - s * ROWS_SPAN, place)
    return jnp.where(place >= length, BLOCKED, 0.0)


def adamw(weight, grad, first_old, second_old, rate):
    first = BETA_FIRST * first_old + (1.0 - BETA_FIRST) * grad
    second = BETA_SECOND * second_old + (1.0 - BETA_SECOND) * grad * grad
    first_hat = first / (1.0 - BETA_FIRST**STEP)
    second_hat = second / (1.0 - BETA_SECOND**STEP)
    new = weight - rate * (first_hat / (jnp.sqrt(second_hat) + EPS_ADAM) + WEIGHT_DECAY * weight)
    return first, second, new


class Places:
    def __init__(self, mesh):
        self.n = mesh.shape["fsdp"]
        self.dp = mesh.shape["dp"]
        power = max(int(math.log2(self.n)) - 1, 0) // 2
        self.X = 2**power
        self.Z = self.n // self.X
        self.C = 2
        self.Y = self.dp // self.C

    def me(self):
        f = lax.axis_index("fsdp")
        d = lax.axis_index("dp")
        return jnp.stack([f // self.X, f % self.X, d % self.C, d // self.C]).astype(jnp.int32)

    def slot_to(self, me_ref, f):
        dz = lax.rem(f // self.X + self.Z - me_ref[0], self.Z)
        dx = lax.rem(f % self.X + self.X - me_ref[1], self.X)
        return dx * self.Z + dz

    def slot_from(self, me_ref, f):
        dz = lax.rem(me_ref[0] + self.Z - f // self.X, self.Z)
        dx = lax.rem(me_ref[1] + self.X - f % self.X, self.X)
        return dx * self.Z + dz

    def shift(self, value, dz, dx):
        X, Z = self.X, self.Z
        perm = [
            (z * X + x, (z + dz) % Z * X + (x + dx) % X) for z in range(Z) for x in range(X)
        ]
        return lax.ppermute(value, "fsdp", perm)

    def y_joined(self, me_ref, ref):
        slots = [lax.rem(me_ref[3] + self.Y - y, self.Y) for y in range(self.Y)]
        return jnp.concatenate([ref[slot] for slot in slots], axis=0)

    def y_slot_to(self, me_ref, y):
        return lax.rem(y + self.Y - me_ref[3], self.Y)

    def shift_y(self, value, dy):
        dp = self.dp
        return lax.ppermute(value, "dp", [(d, (d + 2 * dy) % dp) for d in range(dp)])

    def other_core(self, value):
        return lax.ppermute(value, "dp", [(d, d ^ 1) for d in range(self.dp)])

    def sum_over_y(self, value):
        step = 1
        while step < self.Y:
            got = lax.ppermute(value, "dp", [(d, d ^ (2 * step)) for d in range(self.dp)])
            value = (value.astype(F32) + got.astype(F32)).astype(BF16)
            step *= 2
        return value


def call(kernel, me, grid, ins, outs, scratch, name, flops=0, moved=0, aliases=None, limit=32):
    def spec(block, index):
        if block == "scalar":
            return pl.BlockSpec(memory_space=pltpu.SMEM)
        if block is None:
            return pl.BlockSpec(memory_space=pltpu.VMEM if index is None else pl.ANY)
        return pl.BlockSpec(block, lambda *a: index(*a[:-1]))

    return pl.pallas_call(
        kernel,
        grid_spec=pltpu.PrefetchScalarGridSpec(
            num_scalar_prefetch=1,
            grid=grid,
            in_specs=[spec(b, f) for _, b, f in ins],
            out_specs=[spec(b, f) for _, _, b, f in outs],
            scratch_shapes=scratch,
        ),
        out_shape=[jax.ShapeDtypeStruct(s, d) for s, d, _, _ in outs],
        compiler_params=pltpu.CompilerParams(vmem_limit_bytes=limit * 2**20),
        cost_estimate=pl.CostEstimate(flops=flops // 1000, bytes_accessed=moved // 1000, transcendentals=0),
        input_output_aliases=aliases or {},
        name=name,
    )(me, *[a for a, _, _ in ins])


def resident(array):
    return array, None, None


def whole(shape):
    return shape, lambda i: (0,) * len(shape)


def rows_of(shape, column=0):
    return shape, lambda i: (i, column)


def pack_first(attn_w, norm_params, places):
    r = D // places.n
    h = r // 2
    start = lax.axis_index("dp") % 2 * h
    rows = lax.dynamic_slice(attn_w[:3, :, :HALF], (0, start, 0), (3, h, HALF)).reshape(3 * h, HALF)
    norms = jnp.pad(norm_params, ((0, NORM_ROWS - 4), (0, HALF - r)))
    return jnp.concatenate([rows, norms], axis=0).astype(BF16)


def pack_rest(me, attn_w, ffn_in, ffn_out, places):
    r, r2 = D // places.n, FF // places.n
    h, q = r // 2, r2 // places.dp

    def kernel(me_ref, w_ref, in_ref, out_w_ref, second_ref, up_ref):
        lower = me_ref[2] == 0
        for k in range(3):
            w = w_ref[k, :, HALF:]
            second_ref[k * h : (k + 1) * h, :] = jnp.where(lower, w[:h], w[h:]).astype(BF16)
        member = me_ref[3] * 2 + me_ref[2]
        w = out_w_ref[pl.ds(pl.multiple_of(member * q, q), q), :].astype(BF16)
        second_ref[3 * h : 3 * h + q, :] = w[:, :HALF]
        second_ref[3 * h + q :, :] = w[:, HALF:]
        half = FF // 2
        for k in range(4):
            up_ref[k * r : (k + 1) * r, :] = jnp.where(
                lower,
                in_ref[:, k * HALF : (k + 1) * HALF],
                in_ref[:, half + k * HALF : half + (k + 1) * HALF],
            ).astype(BF16)
        w = w_ref[3]
        up_ref[4 * r :, :] = jnp.where(lower, w[:, :HALF], w[:, HALF:]).astype(BF16)

    shapes = (3 * h + 2 * q, HALF), (5 * r, HALF)
    return call(
        kernel,
        me,
        (1,),
        [
            (attn_w, *whole((4, r, D))),
            (ffn_in, *whole((r, FF))),
            (ffn_out, *whole((r2, D))),
        ],
        [(shape, BF16, *whole(shape)) for shape in shapes],
        [],
        "pack_rest",
        limit=58,
        moved=4 * (4 * r * D + r * FF + r2 * D),
    )


def attention_forward(me, half, x, memory, left_keys, left_values, lengths, masks, weights, places, part=0, parts=1, before=None):
    first = half == 0
    fresh = before is None
    spans = memory.shape[0] // MEM
    step_spans = 32 if spans % 32 == 0 else 16
    groups = step_spans // GROUP
    rows = step_spans * ROWS_SPAN
    n, r = places.n, D // places.n
    h = r // 2

    steps = spans // step_spans // parts
    start = part * steps

    def kernel(me_ref, x_ref, mem_ref, lk_ref, lv_ref, len_ref, mask_ref, *rest):
        if fresh:
            own_ref, other_ref, *rest = rest
        else:
            w_ref, *rest = rest
            if first:
                norm_ref, *rest = rest
            rest = rest[len(aliased) :]
        qkv_ref, kvm_ref, att_ref, p_ref, *rest = rest
        if first:
            hid_ref, xhat_ref, memt_ref, *rest = rest
        if fresh:
            w_ref, *rest = rest
            if first:
                norm_ref, *rest = rest
        ks, vs = rest

        @pl.when(pl.program_id(0) == 0)
        def _():
            ks[...] = jnp.zeros_like(ks)
            vs[...] = jnp.zeros_like(vs)
            lower = me_ref[2] == 0
            if first and fresh:
                norm_ref[...] = jnp.zeros_like(norm_ref)
            for f in range(n) if fresh else ():
                slot = places.slot_from(me_ref, f)
                mine, sib = own_ref[slot], other_ref[slot]
                for at, part in (
                    (slice(f * r, f * r + h), jnp.where(lower, mine, sib)),
                    (slice(f * r + h, (f + 1) * r), jnp.where(lower, sib, mine)),
                ):
                    for k in range(3):
                        w_ref[at, k * HALF : (k + 1) * HALF] = part[k * h : (k + 1) * h]
                if first:
                    tail = mine[3 * h :, :].astype(F32)
                    norm_ref[:, f * r : (f + 1) * r] = tail[0:8, 0:r]

        w = w_ref[...]
        if first:
            xhat, _ = normalize(x_ref[...].astype(F32))
            xhat_ref[...] = xhat.astype(BF16).T
            memt_ref[...] = mem_ref[...].T
            hidden = (xhat * norm_ref[0:1, :] + norm_ref[1:2, :]).astype(BF16)
            hid_ref[...] = hidden
        else:
            hidden = x_ref[...]
        qkv = dot(hidden, w).astype(BF16)
        query = qkv[:, :HALF] * jnp.asarray(0.125, BF16)
        qkv_ref[:, :HALF] = query
        qkv_ref[:, HALF:] = qkv[:, HALF:]
        kvm = dot(mem_ref[...], w[:, HALF:]).astype(BF16)
        kvm_ref[...] = kvm
        for g in range(groups):
            ls = left_start(g)
            for dest, low, src in ((ks, 0, lk_ref), (vs, HALF, lv_ref)):
                dest[g, 0:MROWS, :] = kvm[MROWS * g : MROWS * (g + 1), low : low + HALF]
                dest[g, MROWS : MROWS + QROWS, :] = qkv[
                    QROWS * g : QROWS * (g + 1), HALF + low : 2 * HALF + low
                ]
                dest[g, MROWS + QROWS : MROWS + QROWS + LWIN, :] = src[ls : ls + LWIN, :]
        for g0 in range(0, groups, 4):
            work = {}
            units = [(g, p) for g in range(g0, g0 + 4) for p in range(2)]
            dead = {
                g: mask_ref[g % 2] + dead_keys(len_ref, (start + pl.program_id(0)) * groups + g)
                for g in range(g0, g0 + 4)
            }
            for g, p in units:
                s = slice(p * PAIR, (p + 1) * PAIR)
                work[g, p] = dot_last(spread_pair(query[QROWS * g : QROWS * (g + 1), s]), ks[g, :, s])
            for g, p in units:
                scores = work[g, p] + dead[g]
                work[g, p] = jnp.exp(scores - jnp.max(scores, axis=1, keepdims=True))
            for g, p in units:
                s = slice(p * PAIR, (p + 1) * PAIR)
                e = work[g, p]
                right = jnp.concatenate([vs[g, :, s], jnp.ones((KPAD, PAIR), BF16)], axis=1)
                work[g, p] = e, dot(e.astype(BF16), right)
            for g, p in units:
                s = slice(p * PAIR, (p + 1) * PAIR)
                e, mixed = work[g, p]
                scale = 1.0 / mixed[:, PAIR:]
                at = slice(2 * QROWS * g, 2 * QROWS * (g + 1))
                p_ref[p, at, :PAIR] = (e[:, :PAIR] * scale).astype(BF16)
                p_ref[p, at, PAIR:] = (e[:, PAIR:] * scale).astype(BF16)
                att_ref[QROWS * g : QROWS * (g + 1), s] = join_pair(mixed[:, :PAIR] * scale).astype(BF16)

    count = x.shape[0]
    wide = 3 * HALF

    def some(shape, column=0):
        return shape, lambda i: (start + i, column)

    ins = [
        (x, *some((rows, D))),
        (memory, *some((step_spans * MEM, D))),
        (left_keys, *some((step_spans * LEFT, HALF), half)),
        (left_values, *some((step_spans * LEFT, HALF), half)),
        (lengths, "scalar", None),
        (masks, *whole((2, 2 * QROWS, KPAD))),
    ]
    outs = [
        ((count, wide), BF16, *some((rows, wide))),
        ((spans * MEM, 2 * HALF), BF16, *some((step_spans * MEM, 2 * HALF))),
        ((count, HALF), BF16, *some((rows, HALF))),
        ((2, 2 * count, KPAD), BF16, (2, 2 * rows, KPAD), lambda i: (0, start + i, 0)),
    ]
    if first:
        columns = lambda i: (0, start + i)
        outs += [
            ((count, D), BF16, *some((rows, D))),
            ((D, count), BF16, (D, rows), columns),
            ((D, spans * MEM), BF16, (D, step_spans * MEM), columns),
        ]
    shared = 2 if first else 1
    if fresh:
        aliased = []
        ins += [resident(a) for a in weights]
        outs += [((D, wide), BF16, *whole((D, wide))), ((8, D), F32, *whole((8, D)))][:shared]
    else:
        aliased, kept = before[:-shared], before[-shared:]
        ins += [(a, *whole(a.shape)) for a in kept] + [(a, None, 0) for a in aliased]
    result = call(
        kernel,
        me,
        (steps,),
        ins,
        outs,
        [pltpu.VMEM((groups, KPAD, HALF), BF16)] * 2,
        f"attention_forward_{half}_{part}",
        limit=52,
        flops=2 * count * D * wide * 4 // parts,
        moved=2 * (count * D * 3 + spans * LEFT * D + spans * 4 * ROWS_SPAN * KPAD) // parts,
        aliases={1 + len(ins) - len(aliased) + k: k for k in range(len(aliased))},
    )
    return list(result) if fresh else [*result, *kept]


def feed_forward(me, attended_halves, frames, cotangent, norm, up, down, places):
    count = frames.shape[0]
    rows = 512
    steps = count // rows
    chunk = 256
    n, r, r2 = places.n, D // places.n, FF // places.n
    X, Y, Z = places.X, places.Y, places.Z
    q, part_rows = r2 // places.dp, (r + r2) // Y

    def kernel(me_ref, a0, a1, fr_ref, cot_ref, norm_ref, *rest):
        up_refs, other_up_refs, rest = rest[:X], rest[X : 2 * X], rest[2 * X :]
        down_refs, other_down_refs, rest = rest[:Y], rest[Y : 2 * Y], rest[2 * Y :]
        out_ref, res_ref, gatt_ref, gn_ref, keep_up, send_up, keep_down, send_down, *rest = rest
        w1, w2, wo, acc1, acc2, acco = rest
        i = pl.program_id(0)
        lower = me_ref[2] == 0

        @pl.when(i == 0)
        def _():
            acc1[...] = jnp.zeros_like(acc1)
            acc2[...] = jnp.zeros_like(acc2)
            acco[...] = jnp.zeros_like(acco)
            gn_ref[...] = jnp.zeros_like(gn_ref)
            for dx in range(X):
                xx = lax.rem(me_ref[1] + X - dx, X)
                for dz in range(Z):
                    zz = lax.rem(me_ref[0] + Z - dz, Z)
                    f = zz * X + xx

                    def halves(mine, sib):
                        return jnp.where(lower, mine, sib), jnp.where(lower, sib, mine)

                    low, high = halves(up_refs[dx][dz], other_up_refs[dx][dz])
                    at = pl.ds(pl.multiple_of(f * r, r), r)
                    for k in range(4):
                        w1[at, k * HALF : (k + 1) * HALF] = low[k * r : (k + 1) * r]
                        w1[at, FF // 2 + k * HALF : FF // 2 + (k + 1) * HALF] = high[k * r : (k + 1) * r]
                    wo[at, :HALF] = low[4 * r :]
                    wo[at, HALF:] = high[4 * r :]
                    for dy in range(Y):
                        yy = lax.rem(me_ref[3] + Y - dy, Y)
                        for core, part in enumerate(
                            halves(down_refs[dy][dx, dz], other_down_refs[dy][dx, dz])
                        ):
                            at = pl.ds(pl.multiple_of(f * r2 + (yy * 2 + core) * q, q), q)
                            w2[at, :HALF] = part[:q]
                            w2[at, HALF:] = part[q:]

        attended = jnp.concatenate([a0[...], a1[...]], axis=1)
        residual = fr_ref[...].astype(F32) + dot(attended, wo[...])
        normed, scale = normalize(residual)
        gain = norm_ref[2:3, :]
        hidden = (normed * gain + norm_ref[3:4, :]).astype(BF16)
        cot = cot_ref[...]
        output = residual
        grad = None
        slices = [slice(j * chunk, (j + 1) * chunk) for j in range(FF // chunk)]
        late = None
        for j, s in enumerate(slices):
            inner, grad_act = dot(hidden, w1[:, s]), dot_last(cot, w2[s, :])
            if late is not None:
                u, active, grad_inner = late
                output = output + dot(active, w2[u, :])
                part = dot_last(grad_inner, w1[:, u])
                grad = part if grad is None else grad + part
                acc1[:, u] += dot_rows(hidden, grad_inner)
                acc2[:, u] += dot_rows(cot, active)
            value, slope = gelu_parts(inner)
            late = s, value.astype(BF16), (grad_act * slope).astype(BF16)
        u, active, grad_inner = late
        output = output + dot(active, w2[u, :])
        grad = grad + dot_last(grad_inner, w1[:, u])
        acc1[:, u] += dot_rows(hidden, grad_inner)
        acc2[:, u] += dot_rows(cot, active)
        out_ref[...] = output.astype(BF16)
        gn_ref[0:1, :] += jnp.sum(grad * normed, axis=0, keepdims=True)
        gn_ref[1:2, :] += jnp.sum(grad, axis=0, keepdims=True)
        grad_residual = cot.astype(F32) + norm_back(grad, normed, scale, gain)
        res_ref[...] = grad_residual
        grad_low = grad_residual.astype(BF16)
        gatt_ref[...] = dot_last(grad_low, wo[...]).astype(BF16)
        acco[...] += dot_rows(attended, grad_low)

        @pl.when(i == steps - 1)
        def _():
            for f in range(n):
                slot = places.slot_to(me_ref, f)

                def sides(low, high):
                    low, high = low.astype(BF16), high.astype(BF16)
                    return jnp.where(lower, low, high), jnp.where(lower, high, low)

                here = slice(f * r, (f + 1) * r)
                for k in range(4):
                    at = slice(k * r, (k + 1) * r)
                    keep_up[slot, at, :], send_up[slot, at, :] = sides(
                        acc1[here, k * HALF : (k + 1) * HALF],
                        acc1[here, FF // 2 + k * HALF : FF // 2 + (k + 1) * HALF],
                    )
                turned = acc2[:, f * r2 : (f + 1) * r2].T
                low = jnp.concatenate([acco[here, :HALF], turned[:, :HALF]], axis=0)
                high = jnp.concatenate([acco[here, HALF:], turned[:, HALF:]], axis=0)
                for y in range(Y):
                    at = slice(y * part_rows, (y + 1) * part_rows)
                    to = places.y_slot_to(me_ref, y)
                    keep_down[to, slot], send_down[to, slot] = sides(low[at], high[at])

    wires = [(n, 4 * r, HALF)] * 2 + [(Y, n, part_rows, HALF)] * 2
    return call(
        kernel,
        me,
        (steps,),
        [(a, *rows_of((rows, HALF))) for a in attended_halves]
        + [
            (frames, *rows_of((rows, D))),
            (cotangent, *rows_of((rows, D))),
            (norm, *whole((8, D))),
        ]
        + [resident(a) for a in (*up[0], *up[1], *down[0], *down[1])],
        [
            ((count, D), BF16, *rows_of((rows, D))),
            ((count, D), F32, *rows_of((rows, D))),
            ((count, D), BF16, *rows_of((rows, D))),
            ((8, D), F32, *whole((8, D))),
        ]
        + [(wire, BF16, *whole(wire)) for wire in wires],
        [
            pltpu.VMEM((D, FF), BF16),
            pltpu.VMEM((FF, D), BF16),
            pltpu.VMEM((D, D), BF16),
            pltpu.VMEM((D, FF), F32),
            pltpu.VMEM((D, FF), F32),
            pltpu.VMEM((D, D), F32),
        ],
        "feed_forward",
        limit=46,
        flops=2 * count * D * (6 * FF + 3 * D) * 2,
        moved=2 * count * D * 8,
    )


def attention_backward(me, half, xhat, memory_t, left_keys, left_values, saved, grad_att, norm, norm_parts, places):
    last = norm_parts is not None
    qkv, kvm, probs, weights, attended = saved
    spans = memory_t.shape[1] // MEM
    step_spans = 32 if spans % 32 == 0 else 16
    steps = spans // step_spans
    groups = step_spans // GROUP
    rows = step_spans * ROWS_SPAN
    n, r = places.n, D // places.n
    h = r // 2
    m = 3 * h + (NORM_ROWS if last else 0)
    wide = 3 * HALF
    parts = norm_parts if last else []

    def kernel(me_ref, xhat_ref, mem_ref, lk_ref, lv_ref, qkv_ref, kvm_ref, p_ref, da_ref, att_ref, w_ref, norm_ref, *rest):
        part_refs = rest[: len(parts)]
        d_ref, keep_ref, send_ref, gn_ref, ks, vs, dm, acc, accm, sums = rest[len(parts) :]
        i = pl.program_id(0)

        @pl.when(i == 0)
        def _():
            ks[...] = jnp.zeros_like(ks)
            vs[...] = jnp.zeros_like(vs)
            acc[...] = jnp.zeros_like(acc)
            accm[...] = jnp.zeros_like(accm)
            sums[...] = jnp.zeros_like(sums)

        for g in range(groups):
            ls = left_start(g)
            for dest, low, src in ((ks, 0, lk_ref), (vs, HALF, lv_ref)):
                dest[g, 0:MROWS, :] = kvm_ref[MROWS * g : MROWS * (g + 1), low : low + HALF]
                dest[g, MROWS : MROWS + QROWS, :] = qkv_ref[
                    QROWS * g : QROWS * (g + 1), HALF + low : 2 * HALF + low
                ]
                dest[g, MROWS + QROWS : MROWS + QROWS + LWIN, :] = src[ls : ls + LWIN, :]
        negative = jnp.full((KPAD, PAIR), -1.0, BF16)
        for g0 in range(0, groups, 4):
            work = {}
            units = [(g, k) for g in range(g0, g0 + 4) for k in range(2)]
            for g, k in units:
                here = slice(QROWS * g, QROWS * (g + 1))
                s = slice(k * PAIR, (k + 1) * PAIR)
                grad = da_ref[here, s]
                product = (grad.astype(F32) * att_ref[here, s].astype(F32)).astype(BF16)
                da = spread_pair(grad)
                left = jnp.concatenate([da, spread_pair(product)], axis=1)
                right = jnp.concatenate([vs[g, :, s], negative], axis=1)
                work[g, k] = da, dot_last(left, right)
            for g, k in units:
                da, centred = work[g, k]
                p = p_ref[k, 2 * QROWS * g : 2 * QROWS * (g + 1), :]
                work[g, k] = da, p, (p.astype(F32) * centred).astype(BF16)
            for g, k in units:
                here = slice(QROWS * g, QROWS * (g + 1))
                s = slice(k * PAIR, (k + 1) * PAIR)
                d_ref[here, s] = (join_pair(dot(work[g, k][2], ks[g, :, s])) * 0.125).astype(BF16)
            for g, k in units:
                here = slice(QROWS * g, QROWS * (g + 1))
                there = slice(MROWS * g, MROWS * (g + 1))
                s = slice(k * PAIR, (k + 1) * PAIR)
                at = k * PAIR
                da, p, ds = work[g, k]
                q = spread_pair(qkv_ref[here, s])
                dk = dot_rows(ds[:, :PAIR], q).astype(BF16)
                dv = dot_rows(p[:, :PAIR], da).astype(BF16)
                d_ref[here, HALF + at : HALF + at + PAIR] = dk[MROWS : MROWS + QROWS]
                d_ref[here, 2 * HALF + at : 2 * HALF + at + PAIR] = dv[MROWS : MROWS + QROWS]
                dm[there, at : at + PAIR] = dk[:MROWS]
                dm[there, HALF + at : HALF + at + PAIR] = dv[:MROWS]
        d = d_ref[...]
        acc[...] += dot(xhat_ref[...], d)
        accm[...] += dot(mem_ref[...], dm[...])
        sums[0:1, :] += jnp.sum(d.astype(F32), axis=0, keepdims=True)

        @pl.when(i == steps - 1)
        def _():
            lower = me_ref[2] == 0
            w = w_ref[...].astype(F32)
            total = acc[...]
            row_sum = sums[0:1, :]
            lane = lax.broadcasted_iota(jnp.int32, (D, PAIR), 1)
            gain_grad = jnp.sum(total * w, axis=1, keepdims=True)
            shift_grad = jnp.sum(row_sum * w, axis=1, keepdims=True)
            turned = jnp.where(lane == 0, gain_grad, jnp.where(lane == 1, shift_grad, 0.0)).T[0:8, :]
            gn_ref[...] = turned
            line = lax.broadcasted_iota(jnp.int32, (PAIR, D), 0)
            columns = jnp.where(line == 0, norm_ref[0:1, :], jnp.where(line == 1, norm_ref[1:2, :], 0.0)).T
            grads = total * columns[:, 0:1] + columns[:, 1:2] * row_sum
            gq = grads[:, :HALF]
            gk = grads[:, HALF : 2 * HALF] + accm[:, :HALF]
            gv = grads[:, 2 * HALF :] + accm[:, HALF:]
            if last:
                first_norm = turned
                for ref in part_refs[1:]:
                    first_norm = first_norm + ref[...]
                norm_grad = jnp.concatenate([first_norm[0:2], part_refs[0][0:2, :], jnp.zeros((12, D), F32)], axis=0)
                gn_ref[...] = norm_grad[0:8]
            for f in range(n):
                slot = places.slot_to(me_ref, f)
                for k, grad in enumerate((gq, gk, gv)):
                    low = grad[f * r : f * r + h].astype(BF16)
                    high = grad[f * r + h : (f + 1) * r].astype(BF16)
                    keep_ref[slot, k * h : (k + 1) * h, :] = jnp.where(lower, low, high)
                    send_ref[slot, k * h : (k + 1) * h, :] = jnp.where(lower, high, low)
                if last:
                    piece = norm_grad[:, f * r : (f + 1) * r].astype(BF16)
                    for ref in (keep_ref, send_ref):
                        ref[slot, 3 * h :, :] = jnp.zeros((NORM_ROWS, HALF), BF16)
                        ref[slot, 3 * h :, 0:r] = piece

    count = xhat.shape[1]
    wire = (n, m, HALF)
    return call(
        kernel,
        me,
        (steps,),
        [
            (xhat, (D, rows), lambda i: (0, i)),
            (memory_t, (D, step_spans * MEM), lambda i: (0, i)),
            (left_keys, *rows_of((step_spans * LEFT, HALF), half)),
            (left_values, *rows_of((step_spans * LEFT, HALF), half)),
            (qkv, *rows_of((rows, wide))),
            (kvm, *rows_of((step_spans * MEM, 2 * HALF))),
            (probs, (2, 2 * rows, KPAD), lambda i: (0, i, 0)),
            (grad_att, *rows_of((rows, HALF), half)),
            (attended, *rows_of((rows, HALF))),
            (weights, *whole((D, wide))),
            (norm, *whole((8, D))),
        ]
        + [(a, *whole((8, D))) for a in parts],
        [
            ((count, wide), BF16, *rows_of((rows, wide))),
            (wire, BF16, *whole(wire)),
            (wire, BF16, *whole(wire)),
            ((8, D), F32, *whole((8, D))),
        ],
        [pltpu.VMEM((groups, KPAD, HALF), BF16)] * 2
        + [
            pltpu.VMEM((step_spans * MEM, 2 * HALF), BF16),
            pltpu.VMEM((D, wide), F32),
            pltpu.VMEM((D, 2 * HALF), F32),
            pltpu.VMEM((8, wide), F32),
        ],
        f"attention_backward_{half}",
        limit=50,
        flops=2 * count * D * wide * 8,
        moved=2 * (count * D * 5 + spans * LEFT * D + spans * 4 * ROWS_SPAN * KPAD),
    )


def frames_gradient(me, frames, grad_residual, grads, weights, norm, part, before):
    count = frames.shape[0]
    rows = 256
    steps = count // rows // 2
    start = part * steps

    def kernel(me_ref, fr_ref, res_ref, d0, d1, w0_ref, w1_ref, norm_ref, *rest):
        out_ref = rest[-1]
        grad = dot_last(d0[...], w0_ref[...]) + dot_last(d1[...], w1_ref[...])
        xhat, scale = normalize(fr_ref[...].astype(F32))
        out_ref[...] = res_ref[...] + norm_back(grad, xhat, scale, norm_ref[0:1, :])

    def block(shape):
        return shape, lambda i: (start + i, 0)

    ins = [(frames, *block((rows, D))), (grad_residual, *block((rows, D)))]
    ins += [(d, *block((rows, 3 * HALF))) for d in grads]
    ins += [(w, *whole((D, 3 * HALF))) for w in weights]
    ins += [(norm, *whole((8, D)))]
    if part:
        ins += [(before, None, 0)]
    (out,) = call(
        kernel,
        me,
        (steps,),
        ins,
        [((count, D), F32, *block((rows, D)))],
        [],
        f"frames_gradient_{part}",
        flops=count * D * 3 * D,
        moved=count * D * 8,
        aliases={len(ins): 0} if part else None,
    )
    return out


def after(value, *others):
    return lax.optimization_barrier((value, *others))[0]


def add(a, b):
    return a.astype(F32) + b.astype(F32)


def update_rows(me, sums, rate, weight, first, second, name, joined):
    shape = weight.shape

    def kernel(me_ref, own_ref, other_ref, w, m, v, *outs):
        for at, part in joined(me_ref, own_ref, other_ref):
            part = part.astype(F32)
            new = adamw(w[:, at], part, m[:, at], v[:, at], rate)
            for ref, value in zip(outs, (part, *new, new[2].astype(BF16))):
                ref[:, at] = value

    return call(
        kernel,
        me,
        (1,),
        [resident(a) for a in sums] + [(a, *whole(shape)) for a in (weight, first, second)],
        [(shape, t, *whole(shape)) for t in (F32, F32, F32, F32, BF16)],
        [],
        name,
        moved=4 * 8 * shape[0] * shape[1],
    )


def update_up(me, sums, ffn_in, ffn_in_m, ffn_in_v, places):
    r = D // places.n

    def joined(me_ref, own_ref, other_ref):
        lower = me_ref[2] == 0
        mine, sib = own_ref[...], other_ref[...]
        for base, part in ((0, jnp.where(lower, mine, sib)), (FF // 2, jnp.where(lower, sib, mine))):
            for k in range(4):
                yield slice(base + k * HALF, base + (k + 1) * HALF), part[k * r : (k + 1) * r]

    return update_rows(me, sums, RATE_FFN_IN, ffn_in, ffn_in_m, ffn_in_v, "update_up", joined)


def update_down(me, sums, ffn_out, ffn_out_m, ffn_out_v, places):
    r = D // places.n

    def joined(me_ref, own_ref, other_ref):
        lower = me_ref[2] == 0
        mine, sib = [places.y_joined(me_ref, ref)[r:] for ref in (own_ref, other_ref)]
        yield slice(0, HALF), jnp.where(lower, mine, sib)
        yield slice(HALF, D), jnp.where(lower, sib, mine)

    return update_rows(me, sums, RATE_FFN_OUT, ffn_out, ffn_out_m, ffn_out_v, "update_down", joined)


def update_attention(me, rest, sums, attn_w, attn_m, attn_v, norm_params, norm_m, norm_v, places):
    r, r2 = D // places.n, FF // places.n
    h = r // 2
    sums = [*rest, *sums]

    def kernel(me_ref, *refs):
        sum_refs = refs[: len(sums)]
        w, m, v, nw, nm, nv = refs[len(sums) : len(sums) + 6]
        outs = refs[len(sums) + 6 : len(sums) + 11]
        norm_outs = refs[len(sums) + 11 :]
        lower = me_ref[2] == 0
        step = pl.program_id(0)

        def put(rate, at, columns, grad):
            first, second, new = adamw(w[0, at, columns], grad, m[0, at, columns], v[0, at, columns], rate)
            for ref, value in zip(outs, (grad, first, second, new, new.astype(BF16))):
                ref[0, at, columns] = value

        def halves(mine, sib):
            return jnp.where(lower, mine, sib).astype(F32), jnp.where(lower, sib, mine).astype(F32)

        for k in range(3):

            @pl.when(step == k)
            def _(k=k):
                for p in range(2):
                    columns = slice(p * HALF, (p + 1) * HALF)
                    at = p * 3 * h + k * h
                    low, high = halves(*[ref[at : at + h, :] for ref in sum_refs[2:]])
                    put(RATES_ATTENTION[k], slice(0, h), columns, low)
                    put(RATES_ATTENTION[k], slice(h, r), columns, high)

        @pl.when(step == 3)
        def _():
            low, high = halves(*[places.y_joined(me_ref, ref)[:r] for ref in sum_refs[:2]])
            put(RATES_ATTENTION[3], slice(0, r), slice(0, HALF), low)
            put(RATES_ATTENTION[3], slice(0, r), slice(HALF, D), high)

        @pl.when(step == 0)
        def _():
            grad = sum_refs[2][6 * h :, :].astype(F32)[0:4, 0:r]
            first, second, new = adamw(nw[...], grad, nm[...], nv[...], RATE_NORM)
            for ref, value in zip(norm_outs, (grad, first, second, new, new.astype(BF16))):
                ref[...] = value

    shape, small = (4, r, D), (4, r)
    block = (1, r, D), lambda i: (i, 0, 0)
    kinds = (F32, F32, F32, F32, BF16)
    return call(
        kernel,
        me,
        (4,),
        [resident(a) for a in sums]
        + [(a, *block) for a in (attn_w, attn_m, attn_v)]
        + [(a, *whole(small)) for a in (norm_params, norm_m, norm_v)],
        [(shape, t, *block) for t in kinds] + [(small, t, *whole(small)) for t in kinds],
        [],
        "update_attention",
        moved=4 * 8 * 4 * r * D,
    )


def shards(
    places,
    frames,
    memory,
    left_keys,
    left_values,
    lengths,
    cotangent,
    attn_w,
    ffn_in,
    ffn_out,
    norm_params,
    attn_m,
    attn_v,
    ffn_in_m,
    ffn_in_v,
    ffn_out_m,
    ffn_out_v,
    norm_m,
    norm_v,
):
    X, Z = places.X, places.Z
    tie = lax.optimization_barrier
    me = places.me()
    masks = jnp.asarray(span_masks())

    def direct(value):
        return [
            value if dx == dz == 0 else places.shift(value, dz, dx)
            for dx in range(X)
            for dz in range(Z)
        ]

    def along_z(value):
        return [value if dz == 0 else places.shift(value, dz, 0) for dz in range(Z)]

    def along_x(value):
        return [value if dx == 0 else places.shift(value, 0, dx) for dx in range(X)]

    def split(total):
        return total.reshape((X, Z) + total.shape[1:])

    def send_x(total):
        return [places.shift(total[dx].astype(BF16), 0, dx) for dx in range(1, X)]

    def send_z(column):
        return [places.shift(column[dz].astype(BF16), dz, 0) for dz in range(1, Z)]

    def collect(mine, got):
        for part in got:
            mine = add(mine, part)
        return mine

    first_wire = pack_first(attn_w, norm_params, places)
    mixed, up_wire = pack_rest(me, attn_w, ffn_in, ffn_out, places)
    first = direct(first_wire)
    mixed = along_z(mixed)
    up_wire, first = tie((up_wire, first))
    first = jnp.stack(first)
    up = along_z(up_wire)
    me, first = tie((me, first))

    def forward(token, half, x, weights, **part):
        return attention_forward(
            token, half, x, memory, left_keys, left_values, lengths, masks, weights, places, **part
        )

    low = forward(me, 0, frames, (first, places.other_core(first)), parts=2)
    me, low, mixed = tie((me, low, mixed))
    mixed = along_x(jnp.stack(mixed))
    low = forward(me, 0, frames, None, parts=2, part=1, before=low)
    me, low, mixed, up = tie((me, low, mixed, up))
    qkv0, kvm0, att0, p0, hidden, xhat, memory_t, w_low, norm = low
    h3 = 3 * (D // places.n) // 2
    second = jnp.concatenate([part[:, :h3] for part in mixed], axis=0)
    down = jnp.stack([part[:, h3:] for part in mixed])
    down = [down if dy == 0 else places.shift_y(down, dy) for dy in range(places.Y)]
    up = along_x(jnp.stack(up))
    early = places.other_core(up[0]), places.other_core(down[0])
    qkv1, kvm1, att1, p1, w_high = forward(me, 1, hidden, (second, places.other_core(second)))
    me, att1, up, down, early = tie((me, att1, up, down, early))
    up = up, [early[0]] + [places.other_core(part) for part in up[1:]]
    down = down, [early[1]] + [places.other_core(part) for part in down[1:]]
    output, grad_residual, grad_att, norm_two, keep_up, send_up, keep_down, send_down = feed_forward(
        me, (att0, att1), frames, cotangent, norm, up, down, places
    )

    def backward(token, half, saved, norm_parts=None):
        return attention_backward(
            token, half, xhat, memory_t, left_keys, left_values, saved, grad_att, norm, norm_parts, places
        )

    def send_y(total):
        return [places.shift_y(total[dy].astype(BF16), dy) for dy in range(1, places.Y)]

    up = split(add(keep_up, places.other_core(send_up)))
    down = add(keep_down, places.other_core(send_down))
    got_up, got_down = send_x(up), send_y(down)
    me, up, down = tie((me, up, down))
    d0, keep0, send0, n0 = backward(me, 0, (qkv0, kvm0, p0, w_low, att0))
    me, d0, got_up, got_down = tie((me, d0, got_up, got_down))
    up, down = collect(up[0], got_up), split(collect(down[0], got_down))
    got_up, got_down = send_z(up), send_x(down)
    got0 = places.other_core(send0)
    d1, keep1, send1, n1 = backward(me, 1, (qkv1, kvm1, p1, w_high, att1), [norm_two, n0])
    me, d1, keep1, send1, got0, got_up, got_down = tie((me, d1, keep1, send1, got0, got_up, got_down))
    got1 = places.other_core(send1)
    attn = jnp.concatenate([add(keep0, got0), add(keep1, got1)], axis=1)
    attn, up, down, got_up, got_down = tie((attn, up, down, got_up, got_down))
    attn = split(attn)
    got = send_x(attn)
    up, down = collect(up[0], got_up).astype(BF16), collect(down[0], got_down)
    got_down = send_z(down)
    up = places.sum_over_y(up)
    frames_part = functools.partial(
        frames_gradient, frames=frames, grad_residual=grad_residual, grads=(d0, d1),
        weights=(w_low, w_high), norm=norm,
    )
    me, attn = tie((me, attn))
    input_grad = frames_part(me, part=0, before=None)
    me, input_grad, up, got, got_down = tie((me, input_grad, up, got, got_down))
    attn = collect(attn[0], got)
    got = send_z(attn)
    up = up, places.other_core(up)
    down = collect(down[0], got_down).astype(BF16)
    down = jnp.stack([down if dy == 0 else places.shift_y(down, dy) for dy in range(places.Y)])
    input_grad = frames_part(me, part=1, before=input_grad)
    me, input_grad, up, down, got = tie((me, input_grad, up, down, got))
    down = down, places.other_core(down)
    attn = places.sum_over_y(collect(attn[0], got).astype(BF16))
    ffn_up = update_up(me, up, ffn_in, ffn_in_m, ffn_in_v, places)
    me, ffn_up, attn, down = tie((me, ffn_up, attn, down))
    attn = attn, places.other_core(attn)
    ffn_down = update_down(me, down, ffn_out, ffn_out_m, ffn_out_v, places)
    me, ffn_down = tie((me, ffn_down))
    attention = update_attention(
        me, down, attn, attn_w, attn_m, attn_v, norm_params, norm_m, norm_v, places
    )
    ffn = *ffn_up, *ffn_down
    return (output, input_grad, *attention[:5], *ffn, *attention[5:])


def solution(mesh):
    rows = P(("dp", "fsdp"), None)
    attn, ffn, norm = P(None, "fsdp", None), P("fsdp", None), P(None, "fsdp")
    return jax.shard_map(
        functools.partial(shards, Places(mesh)),
        mesh=mesh,
        in_specs=(rows,) * 4
        + (P(("dp", "fsdp")), rows, attn, ffn, ffn, norm)
        + (attn, attn, ffn, ffn, ffn, ffn, norm, norm),
        out_specs=(rows, rows) + (attn,) * 5 + (ffn,) * 10 + (norm,) * 5,
        check_vma=False,
    )
```

```python
import functools
import math

import jax
import jax.numpy as jnp
import numpy as np
from jax import lax
from jax.experimental import pallas as pl
from jax.experimental.pallas import tpu as pltpu
from jax.sharding import PartitionSpec as P

D = 512
FF = 2048
HEADS = 8
SEG = 16
LEFT = 30
MEM = 4
STEP = 5
ROWS_SPAN = 20
GROUP = 4
QROWS = GROUP * ROWS_SPAN
MROWS = GROUP * MEM
LROWS = GROUP * LEFT
LWIN = 128
KPAD = 256
HALF = 256
PAIR = 128
NORM_ROWS = 16

F32 = jnp.float32
BF16 = jnp.bfloat16
BLOCKED = -1e9
EPS_NORM = 1e-05
BETA_FIRST = 0.5
BETA_SECOND = 0.5
WEIGHT_DECAY = 0.01
EPS_ADAM = 1e-08
RATES_ATTENTION = (0.04, 0.04, 0.04, 0.25)
RATE_FFN_IN = 0.04
RATE_FFN_OUT = 0.02
RATE_NORM = 0.2


def dot(a, b):
    return lax.dot_general(a, b, (((1,), (0,)), ((), ())), preferred_element_type=F32)


def dot_last(a, b):
    return lax.dot_general(a, b, (((1,), (1,)), ((), ())), preferred_element_type=F32)


def dot_rows(a, b):
    return lax.dot_general(a, b, (((0,), (0,)), ((), ())), preferred_element_type=F32)


def normalize(x):
    mean = jnp.mean(x, axis=1, keepdims=True)
    centred = x - mean
    variance = jnp.mean(centred * centred, axis=1, keepdims=True)
    scale = lax.rsqrt(variance + EPS_NORM)
    return centred * scale, scale


def norm_back(grad, normed, scale, gain):
    grad = grad * gain
    first = jnp.mean(grad, axis=1, keepdims=True)
    second = jnp.mean(grad * normed, axis=1, keepdims=True)
    return scale * (grad - first - normed * second)


def gelu_parts(x):
    c = math.sqrt(2.0 / math.pi)
    square = x * x
    t = jnp.tanh(x * (c + (c * 0.044715) * square))
    half = 0.5 * x
    value = half + half * t
    slope = 0.5 + 0.5 * t + half * (1.0 - t * t) * (c + (3.0 * c * 0.044715) * square)
    return value, slope


def spread_pair(x):
    lane = lax.broadcasted_iota(jnp.int32, x.shape, 1)
    zero = jnp.zeros_like(x)
    return jnp.concatenate([jnp.where(lane < 64, x, zero), jnp.where(lane < 64, zero, x)], axis=0)


def join_pair(x):
    rows = x.shape[0] // 2
    lane = lax.broadcasted_iota(jnp.int32, (rows, PAIR), 1)
    return jnp.where(lane < 64, x[:rows], x[rows:])


def left_start(g):
    return LROWS * g - (8 if g % 2 else 0)


def span_masks():
    query_span = np.arange(2 * QROWS) % QROWS // ROWS_SPAN
    masks = np.full((2, 2 * QROWS, KPAD), BLOCKED, np.float32)
    for odd in range(2):
        span = np.full(KPAD, -1)
        span[:MROWS] = np.arange(MROWS) // MEM
        span[MROWS : MROWS + QROWS] = np.arange(QROWS) // ROWS_SPAN
        start = MROWS + QROWS + (8 if odd else 0)
        span[start : start + LROWS] = np.arange(LROWS) // LEFT
        masks[odd][query_span[:, None] == span[None, :]] = 0.0
    return masks


def dead_keys(lengths_ref, group):
    key = lax.broadcasted_iota(jnp.int32, (1, KPAD), 1) - MROWS
    length = jnp.full((1, KPAD), ROWS_SPAN, jnp.int32)
    place = jnp.zeros((1, KPAD), jnp.int32)
    for s in range(GROUP):
        inside = (key >= s * ROWS_SPAN) & (key < s * ROWS_SPAN + SEG)
        length = jnp.where(inside, lengths_ref[group * GROUP + s], length)
        place = jnp.where(inside, key - s * ROWS_SPAN, place)
    return jnp.where(place >= length, BLOCKED, 0.0)


def adamw(weight, grad, first_old, second_old, rate):
    first = BETA_FIRST * first_old + (1.0 - BETA_FIRST) * grad
    second = BETA_SECOND * second_old + (1.0 - BETA_SECOND) * grad * grad
    first_hat = first / (1.0 - BETA_FIRST**STEP)
    second_hat = second / (1.0 - BETA_SECOND**STEP)
    new = weight - rate * (first_hat / (jnp.sqrt(second_hat) + EPS_ADAM) + WEIGHT_DECAY * weight)
    return first, second, new


class Places:
    def __init__(self, mesh):
        self.n = mesh.shape["fsdp"]
        self.dp = mesh.shape["dp"]
        power = max(int(math.log2(self.n)) - 1, 0) // 2
        self.X = 2**power
        self.Z = self.n // self.X
        self.C = 2
        self.Y = self.dp // self.C

    def me(self):
        f = lax.axis_index("fsdp")
        d = lax.axis_index("dp")
        return jnp.stack([f // self.X, f % self.X, d % self.C, d // self.C]).astype(jnp.int32)

    def slot_to(self, me_ref, f):
        dz = lax.rem(f // self.X + self.Z - me_ref[0], self.Z)
        dx = lax.rem(f % self.X + self.X - me_ref[1], self.X)
        return dx * self.Z + dz

    def slot_halving(self, me_ref, f):
        dx = lax.rem(f % self.X + self.X - me_ref[1], self.X)
        return dx * self.Z + lax.bitwise_xor(me_ref[0], jnp.int32(f // self.X))

    def swap_z(self, value, step):
        X = self.X
        return lax.ppermute(value, "fsdp", [(f, (f // X ^ step) * X + f % X) for f in range(self.n)])

    def slot_from(self, me_ref, f):
        dz = lax.rem(me_ref[0] + self.Z - f // self.X, self.Z)
        dx = lax.rem(me_ref[1] + self.X - f % self.X, self.X)
        return dx * self.Z + dz

    def shift(self, value, dz, dx):
        X, Z = self.X, self.Z
        perm = [
            (z * X + x, (z + dz) % Z * X + (x + dx) % X) for z in range(Z) for x in range(X)
        ]
        return lax.ppermute(value, "fsdp", perm)

    def y_joined(self, me_ref, ref):
        slots = [lax.rem(me_ref[3] + self.Y - y, self.Y) for y in range(self.Y)]
        return jnp.concatenate([ref[slot] for slot in slots], axis=0)

    def y_slot_to(self, me_ref, y):
        return lax.rem(y + self.Y - me_ref[3], self.Y)

    def shift_y(self, value, dy):
        dp = self.dp
        return lax.ppermute(value, "dp", [(d, (d + 2 * dy) % dp) for d in range(dp)])

    def other_core(self, value):
        return lax.ppermute(value, "dp", [(d, d ^ 1) for d in range(self.dp)])

    def sum_over_y(self, value):
        step = 1
        while step < self.Y:
            got = lax.ppermute(value, "dp", [(d, d ^ (2 * step)) for d in range(self.dp)])
            value = (value.astype(F32) + got.astype(F32)).astype(BF16)
            step *= 2
        return value


def call(kernel, me, grid, ins, outs, scratch, name, flops=0, moved=0, aliases=None, limit=32):
    def spec(block, index):
        if block == "scalar":
            return pl.BlockSpec(memory_space=pltpu.SMEM)
        if block is None:
            return pl.BlockSpec(memory_space=pltpu.VMEM if index is None else pl.ANY)
        if getattr(index, "by_device", False):
            return pl.BlockSpec(block, lambda *a: index(a[-1]))
        return pl.BlockSpec(block, lambda *a: index(*a[:-1]))

    return pl.pallas_call(
        kernel,
        grid_spec=pltpu.PrefetchScalarGridSpec(
            num_scalar_prefetch=1,
            grid=grid,
            in_specs=[spec(b, f) for _, b, f in ins],
            out_specs=[spec(b, f) for _, _, b, f in outs],
            scratch_shapes=scratch,
        ),
        out_shape=[jax.ShapeDtypeStruct(s, d) for s, d, _, _ in outs],
        compiler_params=pltpu.CompilerParams(vmem_limit_bytes=limit * 2**20),
        cost_estimate=pl.CostEstimate(flops=flops // 1000, bytes_accessed=moved // 1000, transcendentals=0),
        input_output_aliases=aliases or {},
        name=name,
    )(me, *[a for a, _, _ in ins])


def placed(shape, index):
    place = functools.partial(index)
    place.by_device = True
    return shape, place


def resident(array):
    return array, None, None


def whole(shape):
    return shape, lambda i: (0,) * len(shape)


def rows_of(shape, column=0):
    return shape, lambda i: (i, column)


def pack_first(attn_w, norm_params, places):
    r = D // places.n
    h = r // 2
    start = lax.axis_index("dp") % 2 * h
    rows = lax.dynamic_slice(attn_w[:3, :, :HALF], (0, start, 0), (3, h, HALF)).reshape(3 * h, HALF)
    norms = jnp.pad(norm_params, ((0, NORM_ROWS - 4), (0, HALF - r)))
    return jnp.concatenate([rows, norms], axis=0).astype(BF16)


def pack_rest(me, attn_w, ffn_in, ffn_out, places):
    r, r2 = D // places.n, FF // places.n
    h, q = r // 2, r2 // places.dp

    def kernel(me_ref, w_ref, wo_ref, in_ref, out_w_ref, second_ref, up_ref):
        for k in range(3):
            second_ref[k * h : (k + 1) * h, :] = w_ref[k].astype(BF16)
        w = out_w_ref[...].astype(BF16)
        second_ref[3 * h : 3 * h + q, :] = w[:, :HALF]
        second_ref[3 * h + q :, :] = w[:, HALF:]
        for k in range(4):
            up_ref[k * r : (k + 1) * r, :] = in_ref[:, k * HALF : (k + 1) * HALF].astype(BF16)
        up_ref[4 * r :, :] = wo_ref[0].astype(BF16)

    shapes = (3 * h + 2 * q, HALF), (5 * r, HALF)
    return call(
        kernel,
        me,
        (1,),
        [
            (attn_w, *placed((3, h, HALF), lambda me_ref: (0, me_ref[2], 1))),
            (attn_w, *placed((1, r, HALF), lambda me_ref: (3, 0, me_ref[2]))),
            (ffn_in, *placed((r, FF // 2), lambda me_ref: (0, me_ref[2]))),
            (ffn_out, *placed((q, D), lambda me_ref: (me_ref[3] * 2 + me_ref[2], 0))),
        ],
        [(shape, BF16, *whole(shape)) for shape in shapes],
        [],
        "pack_rest",
        limit=58,
        moved=4 * (4 * r * D + r * FF + r2 * D),
    )


def attention_forward(me, half, x, memory, left_keys, left_values, lengths, masks, weights, places, part=0, parts=1, before=None):
    first = half == 0
    fresh = before is None
    spans = memory.shape[0] // MEM
    step_spans = 32 if spans % 32 == 0 else 16
    groups = step_spans // GROUP
    rows = step_spans * ROWS_SPAN
    n, r = places.n, D // places.n
    h = r // 2

    steps = spans // step_spans // parts
    start = part * steps

    def kernel(me_ref, x_ref, mem_ref, lk_ref, lv_ref, len_ref, mask_ref, *rest):
        if fresh:
            own_ref, other_ref, *rest = rest
        else:
            w_ref, *rest = rest
            if first:
                norm_ref, *rest = rest
            rest = rest[len(aliased) :]
        qkv_ref, kvm_ref, att_ref, p_ref, *rest = rest
        if first:
            hid_ref, xhat_ref, memt_ref, *rest = rest
        if fresh:
            w_ref, *rest = rest
            if first:
                norm_ref, *rest = rest
        ks, vs = rest

        @pl.when(pl.program_id(0) == 0)
        def _():
            ks[...] = jnp.zeros_like(ks)
            vs[...] = jnp.zeros_like(vs)
            lower = me_ref[2] == 0
            if first and fresh:
                norm_ref[...] = jnp.zeros_like(norm_ref)
            for f in range(n) if fresh else ():
                slot = places.slot_from(me_ref, f)
                mine, sib = own_ref[slot], other_ref[slot]
                for at, part in (
                    (slice(f * r, f * r + h), jnp.where(lower, mine, sib)),
                    (slice(f * r + h, (f + 1) * r), jnp.where(lower, sib, mine)),
                ):
                    for k in range(3):
                        w_ref[at, k * HALF : (k + 1) * HALF] = part[k * h : (k + 1) * h]
                if first:
                    tail = mine[3 * h :, :].astype(F32)
                    norm_ref[:, f * r : (f + 1) * r] = tail[0:8, 0:r]

        w = w_ref[...]
        if first:
            xhat, _ = normalize(x_ref[...].astype(F32))
            xhat_ref[...] = xhat.astype(BF16).T
            memt_ref[...] = mem_ref[...].T
            hidden = (xhat * norm_ref[0:1, :] + norm_ref[1:2, :]).astype(BF16)
            hid_ref[...] = hidden
        else:
            hidden = x_ref[...]
        qkv = dot(hidden, w).astype(BF16)
        query = qkv[:, :HALF] * jnp.asarray(0.125, BF16)
        qkv_ref[:, :HALF] = query
        qkv_ref[:, HALF:] = qkv[:, HALF:]
        kvm = dot(mem_ref[...], w[:, HALF:]).astype(BF16)
        kvm_ref[...] = kvm
        for g in range(groups):
            ls = left_start(g)
            for dest, low, src in ((ks, 0, lk_ref), (vs, HALF, lv_ref)):
                dest[g, 0:MROWS, :] = kvm[MROWS * g : MROWS * (g + 1), low : low + HALF]
                dest[g, MROWS : MROWS + QROWS, :] = qkv[
                    QROWS * g : QROWS * (g + 1), HALF + low : 2 * HALF + low
                ]
                dest[g, MROWS + QROWS : MROWS + QROWS + LWIN, :] = src[ls : ls + LWIN, :]
        for g0 in range(0, groups, 4):
            work = {}
            units = [(g, p) for g in range(g0, g0 + 4) for p in range(2)]
            dead = {
                g: mask_ref[g % 2] + dead_keys(len_ref, (start + pl.program_id(0)) * groups + g)
                for g in range(g0, g0 + 4)
            }
            for g, p in units:
                s = slice(p * PAIR, (p + 1) * PAIR)
                work[g, p] = dot_last(spread_pair(query[QROWS * g : QROWS * (g + 1), s]), ks[g, :, s])
            for g, p in units:
                scores = work[g, p] + dead[g]
                work[g, p] = jnp.exp(scores - jnp.max(scores, axis=1, keepdims=True))
            for g, p in units:
                s = slice(p * PAIR, (p + 1) * PAIR)
                e = work[g, p]
                right = jnp.concatenate([vs[g, :, s], jnp.ones((KPAD, PAIR), BF16)], axis=1)
                work[g, p] = e, dot(e.astype(BF16), right)
            for g, p in units:
                s = slice(p * PAIR, (p + 1) * PAIR)
                e, mixed = work[g, p]
                scale = 1.0 / mixed[:, PAIR:]
                at = slice(2 * QROWS * g, 2 * QROWS * (g + 1))
                p_ref[p, at, :PAIR] = (e[:, :PAIR] * scale).astype(BF16)
                p_ref[p, at, PAIR:] = (e[:, PAIR:] * scale).astype(BF16)
                att_ref[QROWS * g : QROWS * (g + 1), s] = join_pair(mixed[:, :PAIR] * scale).astype(BF16)

    count = x.shape[0]
    wide = 3 * HALF

    def some(shape, column=0):
        return shape, lambda i: (start + i, column)

    ins = [
        (x, *some((rows, D))),
        (memory, *some((step_spans * MEM, D))),
        (left_keys, *some((step_spans * LEFT, HALF), half)),
        (left_values, *some((step_spans * LEFT, HALF), half)),
        (lengths, "scalar", None),
        (masks, *whole((2, 2 * QROWS, KPAD))),
    ]
    outs = [
        ((count, wide), BF16, *some((rows, wide))),
        ((spans * MEM, 2 * HALF), BF16, *some((step_spans * MEM, 2 * HALF))),
        ((count, HALF), BF16, *some((rows, HALF))),
        ((2, 2 * count, KPAD), BF16, (2, 2 * rows, KPAD), lambda i: (0, start + i, 0)),
    ]
    if first:
        columns = lambda i: (0, start + i)
        outs += [
            ((count, D), BF16, *some((rows, D))),
            ((D, count), BF16, (D, rows), columns),
            ((D, spans * MEM), BF16, (D, step_spans * MEM), columns),
        ]
    shared = 2 if first else 1
    if fresh:
        aliased = []
        ins += [resident(a) for a in weights]
        outs += [((D, wide), BF16, *whole((D, wide))), ((8, D), F32, *whole((8, D)))][:shared]
    else:
        aliased, kept = before[:-shared], before[-shared:]
        ins += [(a, *whole(a.shape)) for a in kept] + [(a, None, 0) for a in aliased]
    result = call(
        kernel,
        me,
        (steps,),
        ins,
        outs,
        [pltpu.VMEM((groups, KPAD, HALF), BF16)] * 2,
        f"attention_forward_{half}_{part}",
        limit=48,
        flops=2 * count * D * wide * 4 // parts,
        moved=2 * (count * D * 3 + spans * LEFT * D + spans * 4 * ROWS_SPAN * KPAD) // parts,
        aliases={1 + len(ins) - len(aliased) + k: k for k in range(len(aliased))},
    )
    return list(result) if fresh else [*result, *kept]


def feed_forward(me, attended_halves, frames, cotangent, norm, up, down, places):
    count = frames.shape[0]
    rows = 512
    steps = count // rows
    chunk = 256
    n, r, r2 = places.n, D // places.n, FF // places.n
    X, Y, Z = places.X, places.Y, places.Z
    q, part_rows = r2 // places.dp, (r + r2) // Y

    def kernel(me_ref, a0, a1, fr_ref, cot_ref, norm_ref, *rest):
        up_refs, other_up_refs, rest = rest[:X], rest[X : 2 * X], rest[2 * X :]
        down_refs, other_down_refs, rest = rest[:Y], rest[Y : 2 * Y], rest[2 * Y :]
        out_ref, res_ref, gatt_ref, gn_ref, keep_up, send_up, keep_down, send_down, *rest = rest
        w1, w2, wo, acc1, acc2, acco = rest
        i = pl.program_id(0)
        lower = me_ref[2] == 0

        @pl.when(i == 0)
        def _():
            acc1[...] = jnp.zeros_like(acc1)
            acc2[...] = jnp.zeros_like(acc2)
            acco[...] = jnp.zeros_like(acco)
            gn_ref[...] = jnp.zeros_like(gn_ref)
            for dx in range(X):
                xx = lax.rem(me_ref[1] + X - dx, X)
                for dz in range(Z):
                    zz = lax.rem(me_ref[0] + Z - dz, Z)
                    f = zz * X + xx

                    def halves(mine, sib):
                        return jnp.where(lower, mine, sib), jnp.where(lower, sib, mine)

                    low, high = halves(up_refs[dx][dz], other_up_refs[dx][dz])
                    at = pl.ds(pl.multiple_of(f * r, r), r)
                    for k in range(4):
                        w1[at, k * HALF : (k + 1) * HALF] = low[k * r : (k + 1) * r]
                        w1[at, FF // 2 + k * HALF : FF // 2 + (k + 1) * HALF] = high[k * r : (k + 1) * r]
                    wo[at, :HALF] = low[4 * r :]
                    wo[at, HALF:] = high[4 * r :]
                    for dy in range(Y):
                        yy = lax.rem(me_ref[3] + Y - dy, Y)
                        for core, part in enumerate(
                            halves(down_refs[dy][dx, dz], other_down_refs[dy][dx, dz])
                        ):
                            at = pl.ds(pl.multiple_of(f * r2 + (yy * 2 + core) * q, q), q)
                            w2[at, :HALF] = part[:q]
                            w2[at, HALF:] = part[q:]

        attended = jnp.concatenate([a0[...], a1[...]], axis=1)
        residual = fr_ref[...].astype(F32) + dot(attended, wo[...])
        normed, scale = normalize(residual)
        gain = norm_ref[2:3, :]
        hidden = (normed * gain + norm_ref[3:4, :]).astype(BF16)
        cot = cot_ref[...]
        output = residual
        grad = None
        slices = [slice(j * chunk, (j + 1) * chunk) for j in range(FF // chunk)]
        late = None
        for j, s in enumerate(slices):
            inner, grad_act = dot(hidden, w1[:, s]), dot_last(cot, w2[s, :])
            if late is not None:
                u, active, grad_inner = late
                output = output + dot(active, w2[u, :])
                part = dot_last(grad_inner, w1[:, u])
                grad = part if grad is None else grad + part
                acc1[:, u] += dot_rows(hidden, grad_inner)
                acc2[:, u] += dot_rows(cot, active)
            value, slope = gelu_parts(inner)
            late = s, value.astype(BF16), (grad_act * slope).astype(BF16)
        u, active, grad_inner = late
        output = output + dot(active, w2[u, :])
        grad = grad + dot_last(grad_inner, w1[:, u])
        acc1[:, u] += dot_rows(hidden, grad_inner)
        acc2[:, u] += dot_rows(cot, active)
        out_ref[...] = output.astype(BF16)
        gn_ref[0:1, :] += jnp.sum(grad * normed, axis=0, keepdims=True)
        gn_ref[1:2, :] += jnp.sum(grad, axis=0, keepdims=True)
        grad_residual = cot.astype(F32) + norm_back(grad, normed, scale, gain)
        res_ref[...] = grad_residual
        grad_low = grad_residual.astype(BF16)
        gatt_ref[...] = dot_last(grad_low, wo[...]).astype(BF16)
        acco[...] += dot_rows(attended, grad_low)

        @pl.when(i == steps - 1)
        def _():
            for f in range(n):
                slot = places.slot_to(me_ref, f)
                halving = places.slot_halving(me_ref, f)

                def sides(low, high):
                    low, high = low.astype(BF16), high.astype(BF16)
                    return jnp.where(lower, low, high), jnp.where(lower, high, low)

                here = slice(f * r, (f + 1) * r)
                for k in range(4):
                    at = slice(k * r, (k + 1) * r)
                    keep_up[halving, at, :], send_up[halving, at, :] = sides(
                        acc1[here, k * HALF : (k + 1) * HALF],
                        acc1[here, FF // 2 + k * HALF : FF // 2 + (k + 1) * HALF],
                    )
                turned = acc2[:, f * r2 : (f + 1) * r2].T
                low = jnp.concatenate([acco[here, :HALF], turned[:, :HALF]], axis=0)
                high = jnp.concatenate([acco[here, HALF:], turned[:, HALF:]], axis=0)
                for y in range(Y):
                    at = slice(y * part_rows, (y + 1) * part_rows)
                    to = places.y_slot_to(me_ref, y)
                    keep_down[to, slot], send_down[to, slot] = sides(low[at], high[at])

    wires = [(n, 4 * r, HALF)] * 2 + [(Y, n, part_rows, HALF)] * 2
    return call(
        kernel,
        me,
        (steps,),
        [(a, *rows_of((rows, HALF))) for a in attended_halves]
        + [
            (frames, *rows_of((rows, D))),
            (cotangent, *rows_of((rows, D))),
            (norm, *whole((8, D))),
        ]
        + [resident(a) for a in (*up[0], *up[1], *down[0], *down[1])],
        [
            ((count, D), BF16, *rows_of((rows, D))),
            ((count, D), F32, *rows_of((rows, D))),
            ((count, D), BF16, *rows_of((rows, D))),
            ((8, D), F32, *whole((8, D))),
        ]
        + [(wire, BF16, *whole(wire)) for wire in wires],
        [
            pltpu.VMEM((D, FF), BF16),
            pltpu.VMEM((FF, D), BF16),
            pltpu.VMEM((D, D), BF16),
            pltpu.VMEM((D, FF), F32),
            pltpu.VMEM((D, FF), F32),
            pltpu.VMEM((D, D), F32),
        ],
        "feed_forward",
        limit=42,
        flops=2 * count * D * (6 * FF + 3 * D) * 2,
        moved=2 * count * D * 8,
    )


def attention_backward(me, half, xhat, memory_t, left_keys, left_values, saved, grad_att, norm, norm_parts, places):
    last = norm_parts is not None
    qkv, kvm, probs, weights, attended = saved
    spans = memory_t.shape[1] // MEM
    step_spans = 32 if spans % 32 == 0 else 16
    steps = spans // step_spans
    groups = step_spans // GROUP
    rows = step_spans * ROWS_SPAN
    n, r = places.n, D // places.n
    h = r // 2
    m = 3 * h + (NORM_ROWS if last else 0)
    wide = 3 * HALF
    parts = norm_parts if last else []

    def kernel(me_ref, xhat_ref, mem_ref, lk_ref, lv_ref, qkv_ref, kvm_ref, p_ref, da_ref, att_ref, w_ref, norm_ref, *rest):
        part_refs = rest[: len(parts)]
        d_ref, keep_ref, send_ref, gn_ref, ks, vs, dm, acc, accm, sums = rest[len(parts) :]
        i = pl.program_id(0)

        @pl.when(i == 0)
        def _():
            ks[...] = jnp.zeros_like(ks)
            vs[...] = jnp.zeros_like(vs)
            acc[...] = jnp.zeros_like(acc)
            accm[...] = jnp.zeros_like(accm)
            sums[...] = jnp.zeros_like(sums)

        for g in range(groups):
            ls = left_start(g)
            for dest, low, src in ((ks, 0, lk_ref), (vs, HALF, lv_ref)):
                dest[g, 0:MROWS, :] = kvm_ref[MROWS * g : MROWS * (g + 1), low : low + HALF]
                dest[g, MROWS : MROWS + QROWS, :] = qkv_ref[
                    QROWS * g : QROWS * (g + 1), HALF + low : 2 * HALF + low
                ]
                dest[g, MROWS + QROWS : MROWS + QROWS + LWIN, :] = src[ls : ls + LWIN, :]
        negative = jnp.full((KPAD, PAIR), -1.0, BF16)
        for g0 in range(0, groups, 4):
            work = {}
            units = [(g, k) for g in range(g0, g0 + 4) for k in range(2)]
            for g, k in units:
                here = slice(QROWS * g, QROWS * (g + 1))
                s = slice(k * PAIR, (k + 1) * PAIR)
                grad = da_ref[here, s]
                product = (grad.astype(F32) * att_ref[here, s].astype(F32)).astype(BF16)
                da = spread_pair(grad)
                left = jnp.concatenate([da, spread_pair(product)], axis=1)
                right = jnp.concatenate([vs[g, :, s], negative], axis=1)
                work[g, k] = da, dot_last(left, right)
            for g, k in units:
                da, centred = work[g, k]
                p = p_ref[k, 2 * QROWS * g : 2 * QROWS * (g + 1), :]
                work[g, k] = da, p, (p.astype(F32) * centred).astype(BF16)
            for g, k in units:
                here = slice(QROWS * g, QROWS * (g + 1))
                s = slice(k * PAIR, (k + 1) * PAIR)
                d_ref[here, s] = (join_pair(dot(work[g, k][2], ks[g, :, s])) * 0.125).astype(BF16)
            for g, k in units:
                here = slice(QROWS * g, QROWS * (g + 1))
                there = slice(MROWS * g, MROWS * (g + 1))
                s = slice(k * PAIR, (k + 1) * PAIR)
                at = k * PAIR
                da, p, ds = work[g, k]
                q = spread_pair(qkv_ref[here, s])
                dk = dot_rows(ds[:, :PAIR], q).astype(BF16)
                dv = dot_rows(p[:, :PAIR], da).astype(BF16)
                d_ref[here, HALF + at : HALF + at + PAIR] = dk[MROWS : MROWS + QROWS]
                d_ref[here, 2 * HALF + at : 2 * HALF + at + PAIR] = dv[MROWS : MROWS + QROWS]
                dm[there, at : at + PAIR] = dk[:MROWS]
                dm[there, HALF + at : HALF + at + PAIR] = dv[:MROWS]
        d = d_ref[...]
        acc[...] += dot(xhat_ref[...], d)
        accm[...] += dot(mem_ref[...], dm[...])
        sums[0:1, :] += jnp.sum(d.astype(F32), axis=0, keepdims=True)

        @pl.when(i == steps - 1)
        def _():
            lower = me_ref[2] == 0
            w = w_ref[...].astype(F32)
            total = acc[...]
            row_sum = sums[0:1, :]
            lane = lax.broadcasted_iota(jnp.int32, (D, PAIR), 1)
            gain_grad = jnp.sum(total * w, axis=1, keepdims=True)
            shift_grad = jnp.sum(row_sum * w, axis=1, keepdims=True)
            turned = jnp.where(lane == 0, gain_grad, jnp.where(lane == 1, shift_grad, 0.0)).T[0:8, :]
            gn_ref[...] = turned
            line = lax.broadcasted_iota(jnp.int32, (PAIR, D), 0)
            columns = jnp.where(line == 0, norm_ref[0:1, :], jnp.where(line == 1, norm_ref[1:2, :], 0.0)).T
            grads = total * columns[:, 0:1] + columns[:, 1:2] * row_sum
            gq = grads[:, :HALF]
            gk = grads[:, HALF : 2 * HALF] + accm[:, :HALF]
            gv = grads[:, 2 * HALF :] + accm[:, HALF:]
            if last:
                first_norm = turned
                for ref in part_refs[1:]:
                    first_norm = first_norm + ref[...]
                norm_grad = jnp.concatenate([first_norm[0:2], part_refs[0][0:2, :], jnp.zeros((12, D), F32)], axis=0)
                gn_ref[...] = norm_grad[0:8]
            for f in range(n):
                slot = places.slot_to(me_ref, f)
                for k, grad in enumerate((gq, gk, gv)):
                    low = grad[f * r : f * r + h].astype(BF16)
                    high = grad[f * r + h : (f + 1) * r].astype(BF16)
                    keep_ref[slot, k * h : (k + 1) * h, :] = jnp.where(lower, low, high)
                    send_ref[slot, k * h : (k + 1) * h, :] = jnp.where(lower, high, low)
                if last:
                    piece = norm_grad[:, f * r : (f + 1) * r].astype(BF16)
                    for ref in (keep_ref, send_ref):
                        ref[slot, 3 * h :, :] = jnp.zeros((NORM_ROWS, HALF), BF16)
                        ref[slot, 3 * h :, 0:r] = piece

    count = xhat.shape[1]
    wire = (n, m, HALF)
    return call(
        kernel,
        me,
        (steps,),
        [
            (xhat, (D, rows), lambda i: (0, i)),
            (memory_t, (D, step_spans * MEM), lambda i: (0, i)),
            (left_keys, *rows_of((step_spans * LEFT, HALF), half)),
            (left_values, *rows_of((step_spans * LEFT, HALF), half)),
            (qkv, *rows_of((rows, wide))),
            (kvm, *rows_of((step_spans * MEM, 2 * HALF))),
            (probs, (2, 2 * rows, KPAD), lambda i: (0, i, 0)),
            (grad_att, *rows_of((rows, HALF), half)),
            (attended, *rows_of((rows, HALF))),
            (weights, *whole((D, wide))),
            (norm, *whole((8, D))),
        ]
        + [(a, *whole((8, D))) for a in parts],
        [
            ((count, wide), BF16, *rows_of((rows, wide))),
            (wire, BF16, *whole(wire)),
            (wire, BF16, *whole(wire)),
            ((8, D), F32, *whole((8, D))),
        ],
        [pltpu.VMEM((groups, KPAD, HALF), BF16)] * 2
        + [
            pltpu.VMEM((step_spans * MEM, 2 * HALF), BF16),
            pltpu.VMEM((D, wide), F32),
            pltpu.VMEM((D, 2 * HALF), F32),
            pltpu.VMEM((8, wide), F32),
        ],
        f"attention_backward_{half}",
        limit=46,
        flops=2 * count * D * wide * 8,
        moved=2 * (count * D * 5 + spans * LEFT * D + spans * 4 * ROWS_SPAN * KPAD),
    )


def frames_gradient(me, frames, grad_residual, grads, weights, norm, part, before):
    count = frames.shape[0]
    rows = 256
    steps = count // rows // 2
    start = part * steps

    def kernel(me_ref, fr_ref, res_ref, d0, d1, w0_ref, w1_ref, norm_ref, *rest):
        out_ref = rest[-1]
        grad = dot_last(d0[...], w0_ref[...]) + dot_last(d1[...], w1_ref[...])
        xhat, scale = normalize(fr_ref[...].astype(F32))
        out_ref[...] = res_ref[...] + norm_back(grad, xhat, scale, norm_ref[0:1, :])

    def block(shape):
        return shape, lambda i: (start + i, 0)

    ins = [(frames, *block((rows, D))), (grad_residual, *block((rows, D)))]
    ins += [(d, *block((rows, 3 * HALF))) for d in grads]
    ins += [(w, *whole((D, 3 * HALF))) for w in weights]
    ins += [(norm, *whole((8, D)))]
    if part:
        ins += [(before, None, 0)]
    (out,) = call(
        kernel,
        me,
        (steps,),
        ins,
        [((count, D), F32, *block((rows, D)))],
        [],
        f"frames_gradient_{part}",
        limit=32,
        flops=count * D * 3 * D,
        moved=count * D * 8,
        aliases={len(ins): 0} if part else None,
    )
    return out


def after(value, *others):
    return lax.optimization_barrier((value, *others))[0]


def add(a, b):
    return a.astype(F32) + b.astype(F32)


def update_rows(me, sums, rate, weight, first, second, name, joined):
    shape = weight.shape

    def kernel(me_ref, own_ref, other_ref, w, m, v, *outs):
        for at, part in joined(me_ref, own_ref, other_ref):
            part = part.astype(F32)
            new = adamw(w[:, at], part, m[:, at], v[:, at], rate)
            for ref, value in zip(outs, (part, *new, new[2].astype(BF16))):
                ref[:, at] = value

    return call(
        kernel,
        me,
        (1,),
        [resident(a) for a in sums] + [(a, *whole(shape)) for a in (weight, first, second)],
        [(shape, t, *whole(shape)) for t in (F32, F32, F32, F32, BF16)],
        [],
        name,
        moved=4 * 8 * shape[0] * shape[1],
    )


def update_up(me, sums, ffn_in, ffn_in_m, ffn_in_v, places):
    r = D // places.n

    def joined(me_ref, own_ref, other_ref):
        lower = me_ref[2] == 0
        mine, sib = own_ref[...], other_ref[...]
        for base, part in ((0, jnp.where(lower, mine, sib)), (FF // 2, jnp.where(lower, sib, mine))):
            for k in range(4):
                yield slice(base + k * HALF, base + (k + 1) * HALF), part[k * r : (k + 1) * r]

    return update_rows(me, sums, RATE_FFN_IN, ffn_in, ffn_in_m, ffn_in_v, "update_up", joined)


def update_down(me, sums, ffn_out, ffn_out_m, ffn_out_v, places):
    r = D // places.n

    def joined(me_ref, own_ref, other_ref):
        lower = me_ref[2] == 0
        mine, sib = [places.y_joined(me_ref, ref)[r:] for ref in (own_ref, other_ref)]
        yield slice(0, HALF), jnp.where(lower, mine, sib)
        yield slice(HALF, D), jnp.where(lower, sib, mine)

    return update_rows(me, sums, RATE_FFN_OUT, ffn_out, ffn_out_m, ffn_out_v, "update_down", joined)


def update_attention(me, rest, sums, attn_w, attn_m, attn_v, norm_params, norm_m, norm_v, places):
    r, r2 = D // places.n, FF // places.n
    h = r // 2
    sums = [*rest, *sums]

    def kernel(me_ref, *refs):
        sum_refs = refs[: len(sums)]
        w, m, v, nw, nm, nv = refs[len(sums) : len(sums) + 6]
        outs = refs[len(sums) + 6 : len(sums) + 11]
        norm_outs = refs[len(sums) + 11 :]
        lower = me_ref[2] == 0
        step = pl.program_id(0)

        def put(rate, at, columns, grad):
            first, second, new = adamw(w[0, at, columns], grad, m[0, at, columns], v[0, at, columns], rate)
            for ref, value in zip(outs, (grad, first, second, new, new.astype(BF16))):
                ref[0, at, columns] = value

        def halves(mine, sib):
            return jnp.where(lower, mine, sib).astype(F32), jnp.where(lower, sib, mine).astype(F32)

        for k in range(3):

            @pl.when(step == k)
            def _(k=k):
                for p in range(2):
                    columns = slice(p * HALF, (p + 1) * HALF)
                    at = p * 3 * h + k * h
                    low, high = halves(*[ref[at : at + h, :] for ref in sum_refs[2:]])
                    put(RATES_ATTENTION[k], slice(0, h), columns, low)
                    put(RATES_ATTENTION[k], slice(h, r), columns, high)

        @pl.when(step == 3)
        def _():
            low, high = halves(*[places.y_joined(me_ref, ref)[:r] for ref in sum_refs[:2]])
            put(RATES_ATTENTION[3], slice(0, r), slice(0, HALF), low)
            put(RATES_ATTENTION[3], slice(0, r), slice(HALF, D), high)

        @pl.when(step == 0)
        def _():
            grad = sum_refs[2][6 * h :, :].astype(F32)[0:4, 0:r]
            first, second, new = adamw(nw[...], grad, nm[...], nv[...], RATE_NORM)
            for ref, value in zip(norm_outs, (grad, first, second, new, new.astype(BF16))):
                ref[...] = value

    shape, small = (4, r, D), (4, r)
    block = (1, r, D), lambda i: (i, 0, 0)
    kinds = (F32, F32, F32, F32, BF16)
    return call(
        kernel,
        me,
        (4,),
        [resident(a) for a in sums]
        + [(a, *block) for a in (attn_w, attn_m, attn_v)]
        + [(a, *whole(small)) for a in (norm_params, norm_m, norm_v)],
        [(shape, t, *block) for t in kinds] + [(small, t, *whole(small)) for t in kinds],
        [],
        "update_attention",
        moved=4 * 8 * 4 * r * D,
    )


def shards(
    places,
    frames,
    memory,
    left_keys,
    left_values,
    lengths,
    cotangent,
    attn_w,
    ffn_in,
    ffn_out,
    norm_params,
    attn_m,
    attn_v,
    ffn_in_m,
    ffn_in_v,
    ffn_out_m,
    ffn_out_v,
    norm_m,
    norm_v,
):
    X, Z = places.X, places.Z
    tie = lax.optimization_barrier
    me = places.me()
    masks = jnp.asarray(span_masks())

    def direct(value):
        return [
            value if dx == dz == 0 else places.shift(value, dz, dx)
            for dx in range(X)
            for dz in range(Z)
        ]

    def along_z(value):
        return [value if dz == 0 else places.shift(value, dz, 0) for dz in range(Z)]

    def along_x(value):
        return [value if dx == 0 else places.shift(value, 0, dx) for dx in range(X)]

    def split(total):
        return total.reshape((X, Z) + total.shape[1:])

    def send_x(total):
        return [places.shift(total[dx].astype(BF16), 0, dx) for dx in range(1, X)]

    def send_z(column):
        return [places.shift(column[dz].astype(BF16), dz, 0) for dz in range(1, Z)]

    def collect(mine, got):
        for part in got:
            mine = add(mine, part)
        return mine

    first_wire = pack_first(attn_w, norm_params, places)
    mixed, up_wire = pack_rest(me, attn_w, ffn_in, ffn_out, places)
    first = direct(first_wire)
    mixed = along_z(mixed)
    up_wire, first = tie((up_wire, first))
    first = jnp.stack(first)
    up = along_z(up_wire)
    me, first = tie((me, first))

    def forward(token, half, x, weights, **part):
        return attention_forward(
            token, half, x, memory, left_keys, left_values, lengths, masks, weights, places, **part
        )

    low = forward(me, 0, frames, (first, places.other_core(first)), parts=2)
    me, low, mixed = tie((me, low, mixed))
    mixed = along_x(jnp.stack(mixed))
    low = forward(me, 0, frames, None, parts=2, part=1, before=low)
    me, low, mixed, up = tie((me, low, mixed, up))
    qkv0, kvm0, att0, p0, hidden, xhat, memory_t, w_low, norm = low
    h3 = 3 * (D // places.n) // 2
    second = jnp.concatenate([part[:, :h3] for part in mixed], axis=0)
    down = jnp.stack([part[:, h3:] for part in mixed])
    down = [down if dy == 0 else places.shift_y(down, dy) for dy in range(places.Y)]
    up = along_x(jnp.stack(up))
    early = places.other_core(up[0]), places.other_core(down[0])
    qkv1, kvm1, att1, p1, w_high = forward(me, 1, hidden, (second, places.other_core(second)))
    me, att1, up, down, early = tie((me, att1, up, down, early))
    up = up, [early[0]] + [places.other_core(part) for part in up[1:]]
    down = down, [early[1]] + [places.other_core(part) for part in down[1:]]
    output, grad_residual, grad_att, norm_two, keep_up, send_up, keep_down, send_down = feed_forward(
        me, (att0, att1), frames, cotangent, norm, up, down, places
    )

    def backward(token, half, saved, norm_parts=None):
        return attention_backward(
            token, half, xhat, memory_t, left_keys, left_values, saved, grad_att, norm, norm_parts, places
        )

    def send_y(total):
        return [places.shift_y(total[dy].astype(BF16), dy) for dy in range(1, places.Y)]

    up = split(add(keep_up, places.other_core(send_up)))
    down = add(keep_down, places.other_core(send_down))
    got_up, got_down = send_x(up), send_y(down)
    me, up, down = tie((me, up, down))
    d0, keep0, send0, n0 = backward(me, 0, (qkv0, kvm0, p0, w_low, att0))
    me, d0, got_up, got_down = tie((me, d0, got_up, got_down))
    up, down = collect(up[0], got_up), split(collect(down[0], got_down))
    half = places.Z // 2
    got_up, got_down = [places.swap_z(up[half:].astype(BF16), half)], send_x(down)
    got0 = places.other_core(send0)
    d1, keep1, send1, n1 = backward(me, 1, (qkv1, kvm1, p1, w_high, att1), [norm_two, n0])
    me, d1, keep1, send1, got0, got_up, got_down = tie((me, d1, keep1, send1, got0, got_up, got_down))
    got1 = places.other_core(send1)
    attn = jnp.concatenate([add(keep0, got0), add(keep1, got1)], axis=1)
    attn, up, down, got_up, got_down = tie((attn, up, down, got_up, got_down))
    attn = split(attn)
    got = send_x(attn)
    up, down = collect(up[:half], got_up), collect(down[0], got_down)
    got_down = send_z(down)
    while half > 2:
        half //= 2
        up = add(up[:half], places.swap_z(up[half:].astype(BF16), half))
    up = up[0], places.swap_z(up[1].astype(BF16), 1)
    frames_part = functools.partial(
        frames_gradient, frames=frames, grad_residual=grad_residual, grads=(d0, d1),
        weights=(w_low, w_high), norm=norm,
    )
    me, attn = tie((me, attn))
    input_grad = frames_part(me, part=0, before=None)
    me, input_grad, up, got, got_down = tie((me, input_grad, up, got, got_down))
    attn = collect(attn[0], got)
    got = send_z(attn)
    up = add(*up).astype(BF16)
    down = collect(down[0], got_down).astype(BF16)
    if places.Y == 2:
        both = places.shift_y(jnp.concatenate([up, down], axis=0), 1)
        up, both = add(up, both[: up.shape[0]]).astype(BF16), both[up.shape[0] :]
        down = jnp.stack([down, both])
    else:
        up = places.sum_over_y(up)
        down = jnp.stack([down if dy == 0 else places.shift_y(down, dy) for dy in range(places.Y)])
    input_grad = frames_part(me, part=1, before=input_grad)
    me, input_grad, up, down, got = tie((me, input_grad, up, down, got))
    up, down = (up, places.other_core(up)), (down, places.other_core(down))
    attn = places.sum_over_y(collect(attn[0], got).astype(BF16))
    ffn_up = update_up(me, up, ffn_in, ffn_in_m, ffn_in_v, places)
    me, ffn_up, attn, down = tie((me, ffn_up, attn, down))
    attn = attn, places.other_core(attn)
    ffn_down = update_down(me, down, ffn_out, ffn_out_m, ffn_out_v, places)
    me, ffn_down = tie((me, ffn_down))
    attention = update_attention(
        me, down, attn, attn_w, attn_m, attn_v, norm_params, norm_m, norm_v, places
    )
    ffn = *ffn_up, *ffn_down
    return (output, input_grad, *attention[:5], *ffn, *attention[5:])


def solution(mesh):
    rows = P(("dp", "fsdp"), None)
    attn, ffn, norm = P(None, "fsdp", None), P("fsdp", None), P(None, "fsdp")
    return jax.shard_map(
        functools.partial(shards, Places(mesh)),
        mesh=mesh,
        in_specs=(rows,) * 4
        + (P(("dp", "fsdp")), rows, attn, ffn, ffn, norm)
        + (attn, attn, ffn, ffn, ffn, ffn, norm, norm),
        out_specs=(rows, rows) + (attn,) * 5 + (ffn,) * 10 + (norm,) * 5,
        check_vma=False,
    )
```

```python
import functools
import math

import jax
import jax.numpy as jnp
import numpy as np
from jax import lax
from jax.experimental import pallas as pl
from jax.experimental.pallas import tpu as pltpu
from jax.sharding import PartitionSpec as P

D = 512
FF = 2048
HEADS = 8
SEG = 16
LEFT = 30
MEM = 4
STEP = 5
ROWS_SPAN = 20
GROUP = 4
QROWS = GROUP * ROWS_SPAN
MROWS = GROUP * MEM
LROWS = GROUP * LEFT
LWIN = 128
KPAD = 256
HALF = 256
PAIR = 128
NORM_ROWS = 16

F32 = jnp.float32
BF16 = jnp.bfloat16
BLOCKED = -1e9
EPS_NORM = 1e-05
BETA_FIRST = 0.5
BETA_SECOND = 0.5
WEIGHT_DECAY = 0.01
EPS_ADAM = 1e-08
RATES_ATTENTION = (0.04, 0.04, 0.04, 0.25)
RATE_FFN_IN = 0.04
RATE_FFN_OUT = 0.02
RATE_NORM = 0.2


def dot(a, b):
    return lax.dot_general(a, b, (((1,), (0,)), ((), ())), preferred_element_type=F32)


def dot_last(a, b):
    return lax.dot_general(a, b, (((1,), (1,)), ((), ())), preferred_element_type=F32)


def dot_rows(a, b):
    return lax.dot_general(a, b, (((0,), (0,)), ((), ())), preferred_element_type=F32)


def normalize(x):
    mean = jnp.mean(x, axis=1, keepdims=True)
    centred = x - mean
    variance = jnp.mean(centred * centred, axis=1, keepdims=True)
    scale = lax.rsqrt(variance + EPS_NORM)
    return centred * scale, scale


def norm_back(grad, normed, scale, gain):
    grad = grad * gain
    first = jnp.mean(grad, axis=1, keepdims=True)
    second = jnp.mean(grad * normed, axis=1, keepdims=True)
    return scale * (grad - first - normed * second)


def gelu_parts(x):
    c = math.sqrt(2.0 / math.pi)
    square = x * x
    t = jnp.tanh(x * (c + (c * 0.044715) * square))
    half = 0.5 * x
    value = half + half * t
    slope = 0.5 + 0.5 * t + half * (1.0 - t * t) * (c + (3.0 * c * 0.044715) * square)
    return value, slope


def spread_pair(x):
    lane = lax.broadcasted_iota(jnp.int32, x.shape, 1)
    zero = jnp.zeros_like(x)
    return jnp.concatenate([jnp.where(lane < 64, x, zero), jnp.where(lane < 64, zero, x)], axis=0)


def join_pair(x):
    rows = x.shape[0] // 2
    lane = lax.broadcasted_iota(jnp.int32, (rows, PAIR), 1)
    return jnp.where(lane < 64, x[:rows], x[rows:])


def left_start(g):
    return LROWS * g - (8 if g % 2 else 0)


def span_masks():
    query_span = np.arange(2 * QROWS) % QROWS // ROWS_SPAN
    masks = np.full((2, 2 * QROWS, KPAD), BLOCKED, np.float32)
    for odd in range(2):
        span = np.full(KPAD, -1)
        span[:MROWS] = np.arange(MROWS) // MEM
        span[MROWS : MROWS + QROWS] = np.arange(QROWS) // ROWS_SPAN
        start = MROWS + QROWS + (8 if odd else 0)
        span[start : start + LROWS] = np.arange(LROWS) // LEFT
        masks[odd][query_span[:, None] == span[None, :]] = 0.0
    return masks


def dead_keys(lengths_ref, group):
    key = lax.broadcasted_iota(jnp.int32, (1, KPAD), 1) - MROWS
    length = jnp.full((1, KPAD), ROWS_SPAN, jnp.int32)
    place = jnp.zeros((1, KPAD), jnp.int32)
    for s in range(GROUP):
        inside = (key >= s * ROWS_SPAN) & (key < s * ROWS_SPAN + SEG)
        length = jnp.where(inside, lengths_ref[group * GROUP + s], length)
        place = jnp.where(inside, key - s * ROWS_SPAN, place)
    return jnp.where(place >= length, BLOCKED, 0.0)


def adamw(weight, grad, first_old, second_old, rate):
    first = BETA_FIRST * first_old + (1.0 - BETA_FIRST) * grad
    second = BETA_SECOND * second_old + (1.0 - BETA_SECOND) * grad * grad
    first_hat = first / (1.0 - BETA_FIRST**STEP)
    second_hat = second / (1.0 - BETA_SECOND**STEP)
    new = weight - rate * (first_hat / (jnp.sqrt(second_hat) + EPS_ADAM) + WEIGHT_DECAY * weight)
    return first, second, new


class Places:
    def __init__(self, mesh):
        self.n = mesh.shape["fsdp"]
        self.dp = mesh.shape["dp"]
        power = max(int(math.log2(self.n)) - 1, 0) // 2
        self.X = 2**power
        self.Z = self.n // self.X
        self.C = 2
        self.Y = self.dp // self.C

    def me(self):
        f = lax.axis_index("fsdp")
        d = lax.axis_index("dp")
        return jnp.stack([f // self.X, f % self.X, d % self.C, d // self.C]).astype(jnp.int32)

    def slot_to(self, me_ref, f):
        dz = lax.rem(f // self.X + self.Z - me_ref[0], self.Z)
        dx = lax.rem(f % self.X + self.X - me_ref[1], self.X)
        return dx * self.Z + dz

    def slot_halving(self, me_ref, f):
        dx = lax.rem(f % self.X + self.X - me_ref[1], self.X)
        return dx * self.Z + lax.bitwise_xor(me_ref[0], jnp.int32(f // self.X))

    def swap_z(self, value, step):
        X = self.X
        return lax.ppermute(value, "fsdp", [(f, (f // X ^ step) * X + f % X) for f in range(self.n)])

    def slot_from(self, me_ref, f):
        dz = lax.rem(me_ref[0] + self.Z - f // self.X, self.Z)
        dx = lax.rem(me_ref[1] + self.X - f % self.X, self.X)
        return dx * self.Z + dz

    def shift(self, value, dz, dx):
        X, Z = self.X, self.Z
        perm = [
            (z * X + x, (z + dz) % Z * X + (x + dx) % X) for z in range(Z) for x in range(X)
        ]
        return lax.ppermute(value, "fsdp", perm)

    def y_joined(self, me_ref, ref):
        slots = [lax.rem(me_ref[3] + self.Y - y, self.Y) for y in range(self.Y)]
        return jnp.concatenate([ref[slot] for slot in slots], axis=0)

    def y_slot_to(self, me_ref, y):
        return lax.rem(y + self.Y - me_ref[3], self.Y)

    def shift_y(self, value, dy):
        dp = self.dp
        return lax.ppermute(value, "dp", [(d, (d + 2 * dy) % dp) for d in range(dp)])

    def other_core(self, value):
        return lax.ppermute(value, "dp", [(d, d ^ 1) for d in range(self.dp)])

    def sum_over_y(self, value):
        step = 1
        while step < self.Y:
            got = lax.ppermute(value, "dp", [(d, d ^ (2 * step)) for d in range(self.dp)])
            value = (value.astype(F32) + got.astype(F32)).astype(BF16)
            step *= 2
        return value


def call(kernel, me, grid, ins, outs, scratch, name, flops=0, moved=0, aliases=None, limit=32):
    def spec(block, index):
        if block == "scalar":
            return pl.BlockSpec(memory_space=pltpu.SMEM)
        if block is None:
            return pl.BlockSpec(memory_space=pltpu.VMEM if index is None else pl.ANY)
        if getattr(index, "by_device", False):
            return pl.BlockSpec(block, lambda *a: index(a[-1]))
        return pl.BlockSpec(block, lambda *a: index(*a[:-1]))

    return pl.pallas_call(
        kernel,
        grid_spec=pltpu.PrefetchScalarGridSpec(
            num_scalar_prefetch=1,
            grid=grid,
            in_specs=[spec(b, f) for _, b, f in ins],
            out_specs=[spec(b, f) for _, _, b, f in outs],
            scratch_shapes=scratch,
        ),
        out_shape=[jax.ShapeDtypeStruct(s, d) for s, d, _, _ in outs],
        compiler_params=pltpu.CompilerParams(vmem_limit_bytes=limit * 2**20),
        cost_estimate=pl.CostEstimate(flops=flops // 1000, bytes_accessed=moved // 1000, transcendentals=0),
        input_output_aliases=aliases or {},
        name=name,
    )(me, *[a for a, _, _ in ins])


def placed(shape, index):
    place = functools.partial(index)
    place.by_device = True
    return shape, place


def resident(array):
    return array, None, None


def whole(shape):
    return shape, lambda i: (0,) * len(shape)


def rows_of(shape, column=0):
    return shape, lambda i: (i, column)


def pack_first(attn_w, norm_params, places):
    r = D // places.n
    h = r // 2
    start = lax.axis_index("dp") % 2 * h
    rows = lax.dynamic_slice(attn_w[:3, :, :HALF], (0, start, 0), (3, h, HALF)).reshape(3 * h, HALF)
    norms = jnp.pad(norm_params, ((0, NORM_ROWS - 4), (0, HALF - r)))
    return jnp.concatenate([rows, norms], axis=0).astype(BF16)


def pack_rest(me, attn_w, ffn_in, ffn_out, places):
    r, r2 = D // places.n, FF // places.n
    h, q = r // 2, r2 // places.dp

    def kernel(me_ref, w_ref, wo_ref, in_ref, out_w_ref, second_ref, up_ref):
        for k in range(3):
            second_ref[k * h : (k + 1) * h, :] = w_ref[k].astype(BF16)
        w = out_w_ref[...].astype(BF16)
        second_ref[3 * h : 3 * h + q, :] = w[:, :HALF]
        second_ref[3 * h + q :, :] = w[:, HALF:]
        for k in range(4):
            up_ref[k * r : (k + 1) * r, :] = in_ref[:, k * HALF : (k + 1) * HALF].astype(BF16)
        up_ref[4 * r :, :] = wo_ref[0].astype(BF16)

    shapes = (3 * h + 2 * q, HALF), (5 * r, HALF)
    return call(
        kernel,
        me,
        (1,),
        [
            (attn_w, *placed((3, h, HALF), lambda me_ref: (0, me_ref[2], 1))),
            (attn_w, *placed((1, r, HALF), lambda me_ref: (3, 0, me_ref[2]))),
            (ffn_in, *placed((r, FF // 2), lambda me_ref: (0, me_ref[2]))),
            (ffn_out, *placed((q, D), lambda me_ref: (me_ref[3] * 2 + me_ref[2], 0))),
        ],
        [(shape, BF16, *whole(shape)) for shape in shapes],
        [],
        "pack_rest",
        limit=58,
        moved=4 * (4 * r * D + r * FF + r2 * D),
    )


def attention_forward(me, half, x, memory, left_keys, left_values, lengths, masks, weights, places, part=0, parts=1, before=None):
    first = half == 0
    fresh = before is None
    spans = memory.shape[0] // MEM
    step_spans = 32 if spans % 32 == 0 else 16
    groups = step_spans // GROUP
    rows = step_spans * ROWS_SPAN
    n, r = places.n, D // places.n
    h = r // 2

    steps = spans // step_spans // parts
    start = part * steps

    def kernel(me_ref, x_ref, mem_ref, lk_ref, lv_ref, len_ref, mask_ref, *rest):
        if fresh:
            own_ref, other_ref, *rest = rest
        else:
            w_ref, *rest = rest
            if first:
                norm_ref, *rest = rest
            rest = rest[len(aliased) :]
        qkv_ref, kvm_ref, att_ref, p_ref, *rest = rest
        if first:
            hid_ref, xhat_ref, memt_ref, *rest = rest
        if fresh:
            w_ref, *rest = rest
            if first:
                norm_ref, *rest = rest
        ks, vs = rest

        @pl.when(pl.program_id(0) == 0)
        def _():
            rest_rows = MROWS + QROWS + LWIN
            for dest in (ks, vs):
                dest[:, rest_rows:, :] = jnp.zeros((groups, KPAD - rest_rows, HALF), BF16)
            lower = me_ref[2] == 0
            if first and fresh:
                norm_ref[...] = jnp.zeros_like(norm_ref)
            for f in range(n) if fresh else ():
                slot = places.slot_from(me_ref, f)
                mine, sib = own_ref[slot], other_ref[slot]
                for at, part in (
                    (slice(f * r, f * r + h), jnp.where(lower, mine, sib)),
                    (slice(f * r + h, (f + 1) * r), jnp.where(lower, sib, mine)),
                ):
                    for k in range(3):
                        w_ref[at, k * HALF : (k + 1) * HALF] = part[k * h : (k + 1) * h]
                if first:
                    tail = mine[3 * h :, :].astype(F32)
                    norm_ref[:, f * r : (f + 1) * r] = tail[0:8, 0:r]

        w = w_ref[...]
        if first:
            xhat, _ = normalize(x_ref[...].astype(F32))
            xhat_ref[...] = xhat.astype(BF16).T
            memt_ref[...] = mem_ref[...].T
            hidden = (xhat * norm_ref[0:1, :] + norm_ref[1:2, :]).astype(BF16)
            hid_ref[...] = hidden
        else:
            hidden = x_ref[...]
        qkv = dot(hidden, w).astype(BF16)
        query = qkv[:, :HALF] * jnp.asarray(0.125, BF16)
        qkv_ref[:, :HALF] = query
        qkv_ref[:, HALF:] = qkv[:, HALF:]
        kvm = dot(mem_ref[...], w[:, HALF:]).astype(BF16)
        kvm_ref[...] = kvm
        for g in range(groups):
            ls = left_start(g)
            for dest, low, src in ((ks, 0, lk_ref), (vs, HALF, lv_ref)):
                dest[g, 0:MROWS, :] = kvm[MROWS * g : MROWS * (g + 1), low : low + HALF]
                dest[g, MROWS : MROWS + QROWS, :] = qkv[
                    QROWS * g : QROWS * (g + 1), HALF + low : 2 * HALF + low
                ]
                dest[g, MROWS + QROWS : MROWS + QROWS + LWIN, :] = src[ls : ls + LWIN, :]
        for g0 in range(0, groups, 4):
            work = {}
            units = [(g, p) for g in range(g0, g0 + 4) for p in range(2)]
            dead = {
                g: mask_ref[g % 2] + dead_keys(len_ref, (start + pl.program_id(0)) * groups + g)
                for g in range(g0, g0 + 4)
            }
            for g, p in units:
                s = slice(p * PAIR, (p + 1) * PAIR)
                work[g, p] = dot_last(spread_pair(query[QROWS * g : QROWS * (g + 1), s]), ks[g, :, s])
            for g, p in units:
                scores = work[g, p] + dead[g]
                work[g, p] = jnp.exp(scores - jnp.max(scores, axis=1, keepdims=True))
            for g, p in units:
                s = slice(p * PAIR, (p + 1) * PAIR)
                e = work[g, p]
                right = jnp.concatenate([vs[g, :, s], jnp.ones((KPAD, PAIR), BF16)], axis=1)
                work[g, p] = e, dot(e.astype(BF16), right)
            for g, p in units:
                s = slice(p * PAIR, (p + 1) * PAIR)
                e, mixed = work[g, p]
                scale = 1.0 / mixed[:, PAIR:]
                at = slice(2 * QROWS * g, 2 * QROWS * (g + 1))
                p_ref[p, at, :PAIR] = (e[:, :PAIR] * scale).astype(BF16)
                p_ref[p, at, PAIR:] = (e[:, PAIR:] * scale).astype(BF16)
                att_ref[QROWS * g : QROWS * (g + 1), s] = join_pair(mixed[:, :PAIR] * scale).astype(BF16)

    count = x.shape[0]
    wide = 3 * HALF

    def some(shape, column=0):
        return shape, lambda i: (start + i, column)

    ins = [
        (x, *some((rows, D))),
        (memory, *some((step_spans * MEM, D))),
        (left_keys, *some((step_spans * LEFT, HALF), half)),
        (left_values, *some((step_spans * LEFT, HALF), half)),
        (lengths, "scalar", None),
        (masks, *whole((2, 2 * QROWS, KPAD))),
    ]
    outs = [
        ((count, wide), BF16, *some((rows, wide))),
        ((spans * MEM, 2 * HALF), BF16, *some((step_spans * MEM, 2 * HALF))),
        ((count, HALF), BF16, *some((rows, HALF))),
        ((2, 2 * count, KPAD), BF16, (2, 2 * rows, KPAD), lambda i: (0, start + i, 0)),
    ]
    if first:
        columns = lambda i: (0, start + i)
        outs += [
            ((count, D), BF16, *some((rows, D))),
            ((D, count), BF16, (D, rows), columns),
            ((D, spans * MEM), BF16, (D, step_spans * MEM), columns),
        ]
    shared = 2 if first else 1
    if fresh:
        aliased = []
        ins += [resident(a) for a in weights]
        outs += [((D, wide), BF16, *whole((D, wide))), ((8, D), F32, *whole((8, D)))][:shared]
    else:
        aliased, kept = before[:-shared], before[-shared:]
        ins += [(a, *whole(a.shape)) for a in kept] + [(a, None, 0) for a in aliased]
    result = call(
        kernel,
        me,
        (steps,),
        ins,
        outs,
        [pltpu.VMEM((groups, KPAD, HALF), BF16)] * 2,
        f"attention_forward_{half}_{part}",
        limit=48,
        flops=2 * count * D * wide * 4 // parts,
        moved=2 * (count * D * 3 + spans * LEFT * D + spans * 4 * ROWS_SPAN * KPAD) // parts,
        aliases={1 + len(ins) - len(aliased) + k: k for k in range(len(aliased))},
    )
    return list(result) if fresh else [*result, *kept]


def feed_forward(me, attended_halves, frames, cotangent, norm, up, down, places):
    count = frames.shape[0]
    rows = 512
    steps = count // rows
    chunk = 256
    n, r, r2 = places.n, D // places.n, FF // places.n
    X, Y, Z = places.X, places.Y, places.Z
    q, part_rows = r2 // places.dp, (r + r2) // Y

    def kernel(me_ref, a0, a1, fr_ref, cot_ref, norm_ref, *rest):
        up_refs, other_up_refs, rest = rest[:X], rest[X : 2 * X], rest[2 * X :]
        down_refs, other_down_refs, rest = rest[:Y], rest[Y : 2 * Y], rest[2 * Y :]
        out_ref, res_ref, gatt_ref, gn_ref, keep_up, send_up, keep_down, send_down, *rest = rest
        w1, w2, wo, acc1, acc2, acco = rest
        i = pl.program_id(0)
        lower = me_ref[2] == 0

        @pl.when(i == 0)
        def _():
            acc1[...] = jnp.zeros_like(acc1)
            acc2[...] = jnp.zeros_like(acc2)
            acco[...] = jnp.zeros_like(acco)
            gn_ref[...] = jnp.zeros_like(gn_ref)
            for dx in range(X):
                xx = lax.rem(me_ref[1] + X - dx, X)
                for dz in range(Z):
                    zz = lax.rem(me_ref[0] + Z - dz, Z)
                    f = zz * X + xx

                    def halves(mine, sib):
                        return jnp.where(lower, mine, sib), jnp.where(lower, sib, mine)

                    low, high = halves(up_refs[dx][dz], other_up_refs[dx][dz])
                    at = pl.ds(pl.multiple_of(f * r, r), r)
                    for k in range(4):
                        w1[at, k * HALF : (k + 1) * HALF] = low[k * r : (k + 1) * r]
                        w1[at, FF // 2 + k * HALF : FF // 2 + (k + 1) * HALF] = high[k * r : (k + 1) * r]
                    wo[at, :HALF] = low[4 * r :]
                    wo[at, HALF:] = high[4 * r :]
                    for dy in range(Y):
                        yy = lax.rem(me_ref[3] + Y - dy, Y)
                        for core, part in enumerate(
                            halves(down_refs[dy][dx, dz], other_down_refs[dy][dx, dz])
                        ):
                            at = pl.ds(pl.multiple_of(f * r2 + (yy * 2 + core) * q, q), q)
                            w2[at, :HALF] = part[:q]
                            w2[at, HALF:] = part[q:]

        attended = jnp.concatenate([a0[...], a1[...]], axis=1)
        residual = fr_ref[...].astype(F32) + dot(attended, wo[...])
        normed, scale = normalize(residual)
        gain = norm_ref[2:3, :]
        hidden = (normed * gain + norm_ref[3:4, :]).astype(BF16)
        cot = cot_ref[...]
        output = residual
        grad = None
        slices = [slice(j * chunk, (j + 1) * chunk) for j in range(FF // chunk)]
        late = None
        for j, s in enumerate(slices):
            inner, grad_act = dot(hidden, w1[:, s]), dot_last(cot, w2[s, :])
            if late is not None:
                u, active, grad_inner = late
                output = output + dot(active, w2[u, :])
                part = dot_last(grad_inner, w1[:, u])
                grad = part if grad is None else grad + part
                acc1[:, u] += dot_rows(hidden, grad_inner)
                acc2[:, u] += dot_rows(cot, active)
            value, slope = gelu_parts(inner)
            late = s, value.astype(BF16), (grad_act * slope).astype(BF16)
        u, active, grad_inner = late
        output = output + dot(active, w2[u, :])
        grad = grad + dot_last(grad_inner, w1[:, u])
        acc1[:, u] += dot_rows(hidden, grad_inner)
        acc2[:, u] += dot_rows(cot, active)
        out_ref[...] = output.astype(BF16)
        gn_ref[0:1, :] += jnp.sum(grad * normed, axis=0, keepdims=True)
        gn_ref[1:2, :] += jnp.sum(grad, axis=0, keepdims=True)
        grad_residual = cot.astype(F32) + norm_back(grad, normed, scale, gain)
        res_ref[...] = grad_residual
        grad_low = grad_residual.astype(BF16)
        gatt_ref[...] = dot_last(grad_low, wo[...]).astype(BF16)
        acco[...] += dot_rows(attended, grad_low)

        @pl.when(i == steps - 1)
        def _():
            for f in range(n):
                slot = places.slot_to(me_ref, f)
                halving = places.slot_halving(me_ref, f)

                def sides(low, high):
                    low, high = low.astype(BF16), high.astype(BF16)
                    return jnp.where(lower, low, high), jnp.where(lower, high, low)

                here = slice(f * r, (f + 1) * r)
                for k in range(4):
                    at = slice(k * r, (k + 1) * r)
                    keep_up[halving, at, :], send_up[halving, at, :] = sides(
                        acc1[here, k * HALF : (k + 1) * HALF],
                        acc1[here, FF // 2 + k * HALF : FF // 2 + (k + 1) * HALF],
                    )
                turned = acc2[:, f * r2 : (f + 1) * r2].T
                low = jnp.concatenate([acco[here, :HALF], turned[:, :HALF]], axis=0)
                high = jnp.concatenate([acco[here, HALF:], turned[:, HALF:]], axis=0)
                for y in range(Y):
                    at = slice(y * part_rows, (y + 1) * part_rows)
                    to = places.y_slot_to(me_ref, y)
                    keep_down[to, slot], send_down[to, slot] = sides(low[at], high[at])

    wires = [(n, 4 * r, HALF)] * 2 + [(Y, n, part_rows, HALF)] * 2
    return call(
        kernel,
        me,
        (steps,),
        [(a, *rows_of((rows, HALF))) for a in attended_halves]
        + [
            (frames, *rows_of((rows, D))),
            (cotangent, *rows_of((rows, D))),
            (norm, *whole((8, D))),
        ]
        + [resident(a) for a in (*up[0], *up[1], *down[0], *down[1])],
        [
            ((count, D), BF16, *rows_of((rows, D))),
            ((count, D), F32, *rows_of((rows, D))),
            ((count, D), BF16, *rows_of((rows, D))),
            ((8, D), F32, *whole((8, D))),
        ]
        + [(wire, BF16, *whole(wire)) for wire in wires],
        [
            pltpu.VMEM((D, FF), BF16),
            pltpu.VMEM((FF, D), BF16),
            pltpu.VMEM((D, D), BF16),
            pltpu.VMEM((D, FF), F32),
            pltpu.VMEM((D, FF), F32),
            pltpu.VMEM((D, D), F32),
        ],
        "feed_forward",
        limit=42,
        flops=2 * count * D * (6 * FF + 3 * D) * 2,
        moved=2 * count * D * 8,
    )


def attention_backward(me, half, xhat, memory_t, left_keys, left_values, saved, grad_att, norm, norm_parts, places):
    last = norm_parts is not None
    qkv, kvm, probs, weights, attended = saved
    spans = memory_t.shape[1] // MEM
    step_spans = 32 if spans % 32 == 0 else 16
    steps = spans // step_spans
    groups = step_spans // GROUP
    rows = step_spans * ROWS_SPAN
    n, r = places.n, D // places.n
    h = r // 2
    m = 3 * h + (NORM_ROWS if last else 0)
    wide = 3 * HALF
    parts = norm_parts if last else []

    def kernel(me_ref, xhat_ref, mem_ref, lk_ref, lv_ref, qkv_ref, kvm_ref, p_ref, da_ref, att_ref, w_ref, norm_ref, *rest):
        part_refs = rest[: len(parts)]
        d_ref, keep_ref, send_ref, gn_ref, ks, vs, dm, acc, accm, sums = rest[len(parts) :]
        i = pl.program_id(0)

        @pl.when(i == 0)
        def _():
            rest_rows = MROWS + QROWS + LWIN
            for dest in (ks, vs):
                dest[:, rest_rows:, :] = jnp.zeros((groups, KPAD - rest_rows, HALF), BF16)
            acc[...] = jnp.zeros_like(acc)
            accm[...] = jnp.zeros_like(accm)
            sums[...] = jnp.zeros_like(sums)

        for g in range(groups):
            ls = left_start(g)
            for dest, low, src in ((ks, 0, lk_ref), (vs, HALF, lv_ref)):
                dest[g, 0:MROWS, :] = kvm_ref[MROWS * g : MROWS * (g + 1), low : low + HALF]
                dest[g, MROWS : MROWS + QROWS, :] = qkv_ref[
                    QROWS * g : QROWS * (g + 1), HALF + low : 2 * HALF + low
                ]
                dest[g, MROWS + QROWS : MROWS + QROWS + LWIN, :] = src[ls : ls + LWIN, :]
        negative = jnp.full((KPAD, PAIR), -1.0, BF16)
        for g0 in range(0, groups, 4):
            work = {}
            units = [(g, k) for g in range(g0, g0 + 4) for k in range(2)]
            for g, k in units:
                here = slice(QROWS * g, QROWS * (g + 1))
                s = slice(k * PAIR, (k + 1) * PAIR)
                grad = da_ref[here, s]
                product = (grad.astype(F32) * att_ref[here, s].astype(F32)).astype(BF16)
                da = spread_pair(grad)
                left = jnp.concatenate([da, spread_pair(product)], axis=1)
                right = jnp.concatenate([vs[g, :, s], negative], axis=1)
                work[g, k] = da, dot_last(left, right)
            for g, k in units:
                da, centred = work[g, k]
                p = p_ref[k, 2 * QROWS * g : 2 * QROWS * (g + 1), :]
                work[g, k] = da, p, (p.astype(F32) * centred).astype(BF16)
            for g, k in units:
                here = slice(QROWS * g, QROWS * (g + 1))
                s = slice(k * PAIR, (k + 1) * PAIR)
                d_ref[here, s] = (join_pair(dot(work[g, k][2], ks[g, :, s])) * 0.125).astype(BF16)
            for g, k in units:
                here = slice(QROWS * g, QROWS * (g + 1))
                there = slice(MROWS * g, MROWS * (g + 1))
                s = slice(k * PAIR, (k + 1) * PAIR)
                at = k * PAIR
                da, p, ds = work[g, k]
                q = spread_pair(qkv_ref[here, s])
                dk = dot_rows(ds[:, :PAIR], q).astype(BF16)
                dv = dot_rows(p[:, :PAIR], da).astype(BF16)
                d_ref[here, HALF + at : HALF + at + PAIR] = dk[MROWS : MROWS + QROWS]
                d_ref[here, 2 * HALF + at : 2 * HALF + at + PAIR] = dv[MROWS : MROWS + QROWS]
                dm[there, at : at + PAIR] = dk[:MROWS]
                dm[there, HALF + at : HALF + at + PAIR] = dv[:MROWS]
        d = d_ref[...]
        acc[...] += dot(xhat_ref[...], d)
        accm[...] += dot(mem_ref[...], dm[...])
        sums[0:1, :] += jnp.sum(d.astype(F32), axis=0, keepdims=True)

        @pl.when(i == steps - 1)
        def _():
            lower = me_ref[2] == 0
            w = w_ref[...].astype(F32)
            total = acc[...]
            row_sum = sums[0:1, :]
            lane = lax.broadcasted_iota(jnp.int32, (D, PAIR), 1)
            gain_grad = jnp.sum(total * w, axis=1, keepdims=True)
            shift_grad = jnp.sum(row_sum * w, axis=1, keepdims=True)
            turned = jnp.where(lane == 0, gain_grad, jnp.where(lane == 1, shift_grad, 0.0)).T[0:8, :]
            gn_ref[...] = turned
            line = lax.broadcasted_iota(jnp.int32, (PAIR, D), 0)
            columns = jnp.where(line == 0, norm_ref[0:1, :], jnp.where(line == 1, norm_ref[1:2, :], 0.0)).T
            grads = total * columns[:, 0:1] + columns[:, 1:2] * row_sum
            gq = grads[:, :HALF]
            gk = grads[:, HALF : 2 * HALF] + accm[:, :HALF]
            gv = grads[:, 2 * HALF :] + accm[:, HALF:]
            if last:
                first_norm = turned
                for ref in part_refs[1:]:
                    first_norm = first_norm + ref[...]
                norm_grad = jnp.concatenate([first_norm[0:2], part_refs[0][0:2, :], jnp.zeros((12, D), F32)], axis=0)
                gn_ref[...] = norm_grad[0:8]
            for f in range(n):
                slot = places.slot_to(me_ref, f)
                for k, grad in enumerate((gq, gk, gv)):
                    low = grad[f * r : f * r + h].astype(BF16)
                    high = grad[f * r + h : (f + 1) * r].astype(BF16)
                    keep_ref[slot, k * h : (k + 1) * h, :] = jnp.where(lower, low, high)
                    send_ref[slot, k * h : (k + 1) * h, :] = jnp.where(lower, high, low)
                if last:
                    piece = norm_grad[:, f * r : (f + 1) * r].astype(BF16)
                    for ref in (keep_ref, send_ref):
                        ref[slot, 3 * h :, :] = jnp.zeros((NORM_ROWS, HALF), BF16)
                        ref[slot, 3 * h :, 0:r] = piece

    count = xhat.shape[1]
    wire = (n, m, HALF)
    return call(
        kernel,
        me,
        (steps,),
        [
            (xhat, (D, rows), lambda i: (0, i)),
            (memory_t, (D, step_spans * MEM), lambda i: (0, i)),
            (left_keys, *rows_of((step_spans * LEFT, HALF), half)),
            (left_values, *rows_of((step_spans * LEFT, HALF), half)),
            (qkv, *rows_of((rows, wide))),
            (kvm, *rows_of((step_spans * MEM, 2 * HALF))),
            (probs, (2, 2 * rows, KPAD), lambda i: (0, i, 0)),
            (grad_att, *rows_of((rows, HALF), half)),
            (attended, *rows_of((rows, HALF))),
            (weights, *whole((D, wide))),
            (norm, *whole((8, D))),
        ]
        + [(a, *whole((8, D))) for a in parts],
        [
            ((count, wide), BF16, *rows_of((rows, wide))),
            (wire, BF16, *whole(wire)),
            (wire, BF16, *whole(wire)),
            ((8, D), F32, *whole((8, D))),
        ],
        [pltpu.VMEM((groups, KPAD, HALF), BF16)] * 2
        + [
            pltpu.VMEM((step_spans * MEM, 2 * HALF), BF16),
            pltpu.VMEM((D, wide), F32),
            pltpu.VMEM((D, 2 * HALF), F32),
            pltpu.VMEM((8, wide), F32),
        ],
        f"attention_backward_{half}",
        limit=46,
        flops=2 * count * D * wide * 8,
        moved=2 * (count * D * 5 + spans * LEFT * D + spans * 4 * ROWS_SPAN * KPAD),
    )


def frames_gradient(me, frames, grad_residual, grads, weights, norm, part, before):
    count = frames.shape[0]
    rows = 256
    steps = count // rows // 2
    start = part * steps

    def kernel(me_ref, fr_ref, res_ref, d0, d1, w0_ref, w1_ref, norm_ref, *rest):
        out_ref = rest[-1]
        grad = dot_last(d0[...], w0_ref[...]) + dot_last(d1[...], w1_ref[...])
        xhat, scale = normalize(fr_ref[...].astype(F32))
        out_ref[...] = res_ref[...] + norm_back(grad, xhat, scale, norm_ref[0:1, :])

    def block(shape):
        return shape, lambda i: (start + i, 0)

    ins = [(frames, *block((rows, D))), (grad_residual, *block((rows, D)))]
    ins += [(d, *block((rows, 3 * HALF))) for d in grads]
    ins += [(w, *whole((D, 3 * HALF))) for w in weights]
    ins += [(norm, *whole((8, D)))]
    if part:
        ins += [(before, None, 0)]
    (out,) = call(
        kernel,
        me,
        (steps,),
        ins,
        [((count, D), F32, *block((rows, D)))],
        [],
        f"frames_gradient_{part}",
        limit=32,
        flops=count * D * 3 * D,
        moved=count * D * 8,
        aliases={len(ins): 0} if part else None,
    )
    return out


def after(value, *others):
    return lax.optimization_barrier((value, *others))[0]


def add(a, b):
    return a.astype(F32) + b.astype(F32)


def update_rows(me, sums, rate, weight, first, second, name, joined):
    shape = weight.shape

    def kernel(me_ref, own_ref, other_ref, w, m, v, *outs):
        for at, part in joined(me_ref, own_ref, other_ref):
            part = part.astype(F32)
            new = adamw(w[:, at], part, m[:, at], v[:, at], rate)
            for ref, value in zip(outs, (part, *new, new[2].astype(BF16))):
                ref[:, at] = value

    return call(
        kernel,
        me,
        (1,),
        [resident(a) for a in sums] + [(a, *whole(shape)) for a in (weight, first, second)],
        [(shape, t, *whole(shape)) for t in (F32, F32, F32, F32, BF16)],
        [],
        name,
        moved=4 * 8 * shape[0] * shape[1],
    )


def update_up(me, sums, ffn_in, ffn_in_m, ffn_in_v, places):
    r = D // places.n

    def joined(me_ref, own_ref, other_ref):
        lower = me_ref[2] == 0
        mine, sib = own_ref[...], other_ref[...]
        for base, part in ((0, jnp.where(lower, mine, sib)), (FF // 2, jnp.where(lower, sib, mine))):
            for k in range(4):
                yield slice(base + k * HALF, base + (k + 1) * HALF), part[k * r : (k + 1) * r]

    return update_rows(me, sums, RATE_FFN_IN, ffn_in, ffn_in_m, ffn_in_v, "update_up", joined)


def update_down(me, sums, ffn_out, ffn_out_m, ffn_out_v, places):
    r = D // places.n

    def joined(me_ref, own_ref, other_ref):
        lower = me_ref[2] == 0
        mine, sib = [places.y_joined(me_ref, ref)[r:] for ref in (own_ref, other_ref)]
        yield slice(0, HALF), jnp.where(lower, mine, sib)
        yield slice(HALF, D), jnp.where(lower, sib, mine)

    return update_rows(me, sums, RATE_FFN_OUT, ffn_out, ffn_out_m, ffn_out_v, "update_down", joined)


def update_attention(me, rest, sums, attn_w, attn_m, attn_v, norm_params, norm_m, norm_v, places):
    r, r2 = D // places.n, FF // places.n
    h = r // 2
    sums = [*rest, *sums]

    def kernel(me_ref, *refs):
        sum_refs = refs[: len(sums)]
        w, m, v, nw, nm, nv = refs[len(sums) : len(sums) + 6]
        outs = refs[len(sums) + 6 : len(sums) + 11]
        norm_outs = refs[len(sums) + 11 :]
        lower = me_ref[2] == 0
        step = pl.program_id(0)

        def put(rate, at, columns, grad):
            first, second, new = adamw(w[0, at, columns], grad, m[0, at, columns], v[0, at, columns], rate)
            for ref, value in zip(outs, (grad, first, second, new, new.astype(BF16))):
                ref[0, at, columns] = value

        def halves(mine, sib):
            return jnp.where(lower, mine, sib).astype(F32), jnp.where(lower, sib, mine).astype(F32)

        for k in range(3):

            @pl.when(step == k)
            def _(k=k):
                for p in range(2):
                    columns = slice(p * HALF, (p + 1) * HALF)
                    at = p * 3 * h + k * h
                    low, high = halves(*[ref[at : at + h, :] for ref in sum_refs[2:]])
                    put(RATES_ATTENTION[k], slice(0, h), columns, low)
                    put(RATES_ATTENTION[k], slice(h, r), columns, high)

        @pl.when(step == 3)
        def _():
            low, high = halves(*[places.y_joined(me_ref, ref)[:r] for ref in sum_refs[:2]])
            put(RATES_ATTENTION[3], slice(0, r), slice(0, HALF), low)
            put(RATES_ATTENTION[3], slice(0, r), slice(HALF, D), high)

        @pl.when(step == 0)
        def _():
            grad = sum_refs[2][6 * h :, :].astype(F32)[0:4, 0:r]
            first, second, new = adamw(nw[...], grad, nm[...], nv[...], RATE_NORM)
            for ref, value in zip(norm_outs, (grad, first, second, new, new.astype(BF16))):
                ref[...] = value

    shape, small = (4, r, D), (4, r)
    block = (1, r, D), lambda i: (i, 0, 0)
    kinds = (F32, F32, F32, F32, BF16)
    return call(
        kernel,
        me,
        (4,),
        [resident(a) for a in sums]
        + [(a, *block) for a in (attn_w, attn_m, attn_v)]
        + [(a, *whole(small)) for a in (norm_params, norm_m, norm_v)],
        [(shape, t, *block) for t in kinds] + [(small, t, *whole(small)) for t in kinds],
        [],
        "update_attention",
        moved=4 * 8 * 4 * r * D,
    )


def shards(
    places,
    frames,
    memory,
    left_keys,
    left_values,
    lengths,
    cotangent,
    attn_w,
    ffn_in,
    ffn_out,
    norm_params,
    attn_m,
    attn_v,
    ffn_in_m,
    ffn_in_v,
    ffn_out_m,
    ffn_out_v,
    norm_m,
    norm_v,
):
    X, Z = places.X, places.Z
    tie = lax.optimization_barrier
    me = places.me()
    masks = jnp.asarray(span_masks())

    def direct(value):
        return [
            value if dx == dz == 0 else places.shift(value, dz, dx)
            for dx in range(X)
            for dz in range(Z)
        ]

    def along_z(value):
        return [value if dz == 0 else places.shift(value, dz, 0) for dz in range(Z)]

    def along_x(value):
        return [value if dx == 0 else places.shift(value, 0, dx) for dx in range(X)]

    def split(total):
        return total.reshape((X, Z) + total.shape[1:])

    def send_x(total):
        return [places.shift(total[dx].astype(BF16), 0, dx) for dx in range(1, X)]

    def send_z(column):
        return [places.shift(column[dz].astype(BF16), dz, 0) for dz in range(1, Z)]

    def collect(mine, got):
        for part in got:
            mine = add(mine, part)
        return mine

    first_wire = pack_first(attn_w, norm_params, places)
    mixed, up_wire = pack_rest(me, attn_w, ffn_in, ffn_out, places)
    first = direct(first_wire)
    mixed = along_z(mixed)
    up_wire, first = tie((up_wire, first))
    first = jnp.stack(first)
    up = along_z(up_wire)
    me, first = tie((me, first))

    def forward(token, half, x, weights, **part):
        return attention_forward(
            token, half, x, memory, left_keys, left_values, lengths, masks, weights, places, **part
        )

    low = forward(me, 0, frames, (first, places.other_core(first)), parts=2)
    me, low, mixed = tie((me, low, mixed))
    mixed = along_x(jnp.stack(mixed))
    low = forward(me, 0, frames, None, parts=2, part=1, before=low)
    me, low, mixed, up = tie((me, low, mixed, up))
    qkv0, kvm0, att0, p0, hidden, xhat, memory_t, w_low, norm = low
    h3 = 3 * (D // places.n) // 2
    second = jnp.concatenate([part[:, :h3] for part in mixed], axis=0)
    down = jnp.stack([part[:, h3:] for part in mixed])
    down = [down if dy == 0 else places.shift_y(down, dy) for dy in range(places.Y)]
    up = along_x(jnp.stack(up))
    early = places.other_core(up[0]), places.other_core(down[0])
    qkv1, kvm1, att1, p1, w_high = forward(me, 1, hidden, (second, places.other_core(second)))
    me, att1, up, down, early = tie((me, att1, up, down, early))
    up = up, [early[0]] + [places.other_core(part) for part in up[1:]]
    down = down, [early[1]] + [places.other_core(part) for part in down[1:]]
    output, grad_residual, grad_att, norm_two, keep_up, send_up, keep_down, send_down = feed_forward(
        me, (att0, att1), frames, cotangent, norm, up, down, places
    )

    def backward(token, half, saved, norm_parts=None):
        return attention_backward(
            token, half, xhat, memory_t, left_keys, left_values, saved, grad_att, norm, norm_parts, places
        )

    def send_y(total):
        return [places.shift_y(total[dy].astype(BF16), dy) for dy in range(1, places.Y)]

    up = split(add(keep_up, places.other_core(send_up)))
    down = add(keep_down, places.other_core(send_down))
    got_up, got_down = send_x(up), send_y(down)
    me, up, down = tie((me, up, down))
    d0, keep0, send0, n0 = backward(me, 0, (qkv0, kvm0, p0, w_low, att0))
    me, d0, got_up, got_down = tie((me, d0, got_up, got_down))
    up, down = collect(up[0], got_up), split(collect(down[0], got_down))
    half = places.Z // 2
    got_up, got_down = [places.swap_z(up[half:].astype(BF16), half)], send_x(down)
    got0 = places.other_core(send0)
    d1, keep1, send1, n1 = backward(me, 1, (qkv1, kvm1, p1, w_high, att1), [norm_two, n0])
    me, d1, keep1, send1, got0, got_up, got_down = tie((me, d1, keep1, send1, got0, got_up, got_down))
    got1 = places.other_core(send1)
    attn = jnp.concatenate([add(keep0, got0), add(keep1, got1)], axis=1)
    attn, up, down, got_up, got_down = tie((attn, up, down, got_up, got_down))
    attn = split(attn)
    got = send_x(attn)
    up, down = collect(up[:half], got_up), collect(down[0], got_down)
    got_down = send_z(down)
    while half > 2:
        half //= 2
        up = add(up[:half], places.swap_z(up[half:].astype(BF16), half))
    up = up[0], places.swap_z(up[1].astype(BF16), 1)
    frames_part = functools.partial(
        frames_gradient, frames=frames, grad_residual=grad_residual, grads=(d0, d1),
        weights=(w_low, w_high), norm=norm,
    )
    me, attn = tie((me, attn))
    input_grad = frames_part(me, part=0, before=None)
    me, input_grad, up, got, got_down = tie((me, input_grad, up, got, got_down))
    attn = collect(attn[0], got)
    got = send_z(attn)
    up = add(*up).astype(BF16)
    down = collect(down[0], got_down).astype(BF16)
    if places.Y == 2:
        both = places.shift_y(jnp.concatenate([up, down], axis=0), 1)
        up, both = add(up, both[: up.shape[0]]).astype(BF16), both[up.shape[0] :]
        down = jnp.stack([down, both])
    else:
        up = places.sum_over_y(up)
        down = jnp.stack([down if dy == 0 else places.shift_y(down, dy) for dy in range(places.Y)])
    input_grad = frames_part(me, part=1, before=input_grad)
    me, input_grad, up, down, got = tie((me, input_grad, up, down, got))
    up, down = (up, places.other_core(up)), (down, places.other_core(down))
    attn = places.sum_over_y(collect(attn[0], got).astype(BF16))
    ffn_up = update_up(me, up, ffn_in, ffn_in_m, ffn_in_v, places)
    me, ffn_up, attn, down = tie((me, ffn_up, attn, down))
    attn = attn, places.other_core(attn)
    ffn_down = update_down(me, down, ffn_out, ffn_out_m, ffn_out_v, places)
    me, ffn_down = tie((me, ffn_down))
    attention = update_attention(
        me, down, attn, attn_w, attn_m, attn_v, norm_params, norm_m, norm_v, places
    )
    ffn = *ffn_up, *ffn_down
    return (output, input_grad, *attention[:5], *ffn, *attention[5:])


def solution(mesh):
    rows = P(("dp", "fsdp"), None)
    attn, ffn, norm = P(None, "fsdp", None), P("fsdp", None), P(None, "fsdp")
    return jax.shard_map(
        functools.partial(shards, Places(mesh)),
        mesh=mesh,
        in_specs=(rows,) * 4
        + (P(("dp", "fsdp")), rows, attn, ffn, ffn, norm)
        + (attn, attn, ffn, ffn, ffn, ffn, norm, norm),
        out_specs=(rows, rows) + (attn,) * 5 + (ffn,) * 10 + (norm,) * 5,
        check_vma=False,
    )
```
